32 devices in a mesh: parts: 2 (over x), expert: 16 (over z, y, core).
Axes of the slice: x: 2, y: 2, z: 4, core: 2. Of those that a mesh axis runs over, the one named last changes fastest.
Arguments:
- tokens: bfloat16 [4096, 1536], P(('parts', 'expert')), parts along dimension 0, may hold values from -6 to 6
- out_grad: bfloat16 [4096, 1536], P(('parts', 'expert')), parts along dimension 0, may hold values from -6 to 6
- gate: float32 [4096], P(('parts', 'expert')), parts along dimension 0, may hold values from 0.2 to 1
- expert_id: int32 [4096], P(('parts', 'expert')), parts along dimension 0, may hold values from 0 to 1, as said below
- dropped: int32 [4096], P(('parts', 'expert')), parts along dimension 0, may hold values from 0 to 1, as said below
- slot: int32 [4096], P(('parts', 'expert')), parts along dimension 0, may hold values from 0 to 79, as said below
- saved_hidden: bfloat16 [2560, 12288], P('parts', 'expert'), parts along dimension 0, may hold values from -6 to 6
- w_in: bfloat16 [1536, 12288], P(None, 'expert'), may hold values from -0.15625 to 0.15625
- w_out: bfloat16 [12288, 1536], P('expert'), may hold values from -0.078125 to 0.078125
Outputs:
- token_grad: bfloat16 [4096, 1536], P(('parts', 'expert')), parts along dimension 0
- gate_grad: float32 [4096], P(('parts', 'expert')), parts along dimension 0
- w_in_grad: bfloat16 [3072, 12288], P('parts', 'expert'), parts along dimension 0
- w_out_grad: bfloat16 [24576, 1536], P(('parts', 'expert')), parts along dimension 0
The draws below stay inside these ranges and needn't reach their ends.
There are 2 independent parts, one for each index of `parts`. The reference program is written for one: setup_inputs(seed, part) draws one part's arguments, and reference() takes and returns one part's arrays. A program takes and returns all parts, laid end to end along the dimension named above; an argument that names none is the same for every part. Nothing has to cross between parts.
Inputs may be any that keep to these rules, and one draw needn't show every extreme that they name: `expert_id`: each device's tokens name experts; one expert, the same for every device of a part, is chosen by more than 80 tokens of every device. Among one device's tokens that name one expert, in token order, the first 80 are kept and the others are dropped. A kept token's slot is its rank in token order among the device's tokens that name the same expert; a dropped token's slot is 0.
All inputs are finite; a program needn't handle non-finite values.
Results may differ from the reference program's by a relative error of at most 0.0085.
Values may be sent and summed in bfloat16 or wider, within the bound.
No kernel may reach another device: no remote copies, remote signals or barrier semaphores. Data moves between devices by JAX's collectives and lax.ppermute only.
A program may use at most 128 MiB of HBM per device.

```python
import math
import jax
import jax.numpy as jnp
from jax import lax

D = 1536
FF = 6144
SPLIT = 8
TOK_DEV = 128
SOURCES = 16
EXPERTS = 2
HID_DEV = 768
CAP = 80
TOKENS = 2048
SLOT_ROWS = 1280


def shuffled(row_key):
    return jax.random.permutation(row_key, TOK_DEV)


def routing(key):
    hottest_key, others_key, shuffle_key = jax.random.split(jax.random.fold_in(key, 7), 3)
    hottest = jax.random.randint(hottest_key, (), 0, EXPERTS)
    crowded = CAP + CAP // 2
    others = jax.random.randint(others_key, (SOURCES, TOK_DEV - crowded), 0, EXPERTS - 1)
    others = others + (others >= hottest).astype(jnp.int32)
    assigned = jnp.concatenate([jnp.full((SOURCES, crowded), hottest, jnp.int32), others], axis=1)
    row_keys = jax.random.split(shuffle_key, SOURCES)
    shuffle = jax.vmap(shuffled)(row_keys)
    chosen = jnp.take_along_axis(assigned, shuffle, axis=1)
    onehot = (chosen[:, :, None] == jnp.arange(EXPERTS, dtype=jnp.int32)[None, None, :]).astype(jnp.int32)
    ranked = jnp.sum((jnp.cumsum(onehot, axis=1) - 1) * onehot, axis=2)
    dropping = (ranked >= CAP).astype(jnp.int32)
    placed = jnp.where(dropping == 1, 0, ranked).astype(jnp.int32)
    return (chosen.reshape(-1), dropping.reshape(-1), placed.reshape(-1))


def draw_expert_id(key, part):
    chosen, dropping, placed = routing(key)
    return chosen


def draw_dropped(key, part):
    chosen, dropping, placed = routing(key)
    return dropping


def draw_slot(key, part):
    chosen, dropping, placed = routing(key)
    return placed


def level_of(rng, extent, cuts, least, largest):
    def one(dim, blocks):
        steps = jax.random.uniform(jax.random.fold_in(jax.random.fold_in(rng, 6), dim), (blocks,), jnp.float32, least / len(cuts), largest / len(cuts))
        return jnp.repeat(jnp.exp(steps), extent[dim] // blocks).reshape((-1,) + (1,) * (len(extent) - dim - 1))

    gain = one(*cuts[0])
    for cut in cuts[1:]:
        gain = gain * one(*cut)
    return gain


def noise(own_key, dims, scale, reach, shards=(), kind=jnp.bfloat16):
    values = scale * jax.random.normal(own_key, dims, jnp.float32)
    if shards:
        values = values * level_of(own_key, dims, shards, -0.22, 0.18)
    return jnp.clip(values, -reach, reach).astype(kind)


def setup_inputs(seed: int = 0, part: int = 0) -> dict:
    key_of = jax.random.split(jax.random.key(seed), 10)
    part_keys = jax.random.split(jax.random.fold_in(key_of[9], part), 10)
    tokens = noise(part_keys[0], (TOKENS, D), 1.0, 6.0, ((0, 16),))
    out_grad = noise(part_keys[1], (TOKENS, D), 1.0, 6.0, ((0, 16),))
    gate = jnp.clip(jnp.exp(math.log(1.0) - 1.609438 * jax.random.uniform(part_keys[2], (TOKENS,), jnp.float32) ** level_of(part_keys[2], (TOKENS,), ((0, 16),), -0.2, 0.2)), 0.2, 1.0)
    expert_id = draw_expert_id(jax.random.fold_in(jax.random.fold_in(key_of[9], part), 71), part)
    dropped = draw_dropped(jax.random.fold_in(jax.random.fold_in(key_of[9], part), 71), part)
    slot = draw_slot(jax.random.fold_in(jax.random.fold_in(key_of[9], part), 71), part)
    saved_hidden = noise(part_keys[6], (SLOT_ROWS, EXPERTS * FF), 1.0, 6.0, ((1, 16),))
    w_in = noise(key_of[7], (D, EXPERTS * FF), D ** -0.5, 0.15625, ((1, 16),))
    w_out = noise(key_of[8], (EXPERTS * FF, D), FF ** -0.5, 0.078125, ((0, 16),))
    return dict(tokens=tokens, out_grad=out_grad, gate=gate, expert_id=expert_id, dropped=dropped, slot=slot, saved_hidden=saved_hidden, w_in=w_in, w_out=w_out)


def normal_parts(hidden):
    normal_cdf = 0.5 * (1.0 + jax.scipy.special.erf(hidden * 0.7071067811865476))
    density = jnp.exp(-0.5 * hidden * hidden) * 0.3989422804014327
    return normal_cdf, density


def one_expert(packed):
    routed, routed_grad, hidden_b, w_in_block, w_out_block = packed
    hidden = hidden_b.astype(jnp.float32)
    normal_cdf, density = normal_parts(hidden)
    activated = hidden * normal_cdf
    grad_act = jnp.dot(routed_grad, w_out_block.T, preferred_element_type=jnp.float32)
    activated_b = activated.astype(jnp.bfloat16)
    hidden_grad = (grad_act * (normal_cdf + hidden * density)).astype(jnp.bfloat16)
    w_out_part = jnp.dot(activated_b.T, routed_grad, preferred_element_type=jnp.float32).astype(jnp.bfloat16)
    w_in_part = jnp.dot(routed.T, hidden_grad, preferred_element_type=jnp.float32).astype(jnp.bfloat16)
    grouped = hidden_grad.astype(jnp.float32).reshape(SLOT_ROWS, SPLIT, HID_DEV)
    weights = w_in_block.astype(jnp.float32).reshape(D, SPLIT, HID_DEV)
    parts = jnp.einsum("rsk,dsk->srd", grouped, weights).astype(jnp.bfloat16)
    slot_grad = jnp.sum(parts.astype(jnp.float32), axis=0)
    gate_parts = jnp.sum((grad_act * activated).reshape(SLOT_ROWS, SPLIT, HID_DEV), axis=2).astype(jnp.bfloat16)
    slot_gate = jnp.sum(gate_parts.astype(jnp.float32), axis=1)
    return slot_grad, slot_gate, w_in_part, w_out_part


def reference(tokens, out_grad, gate, expert_id, dropped, slot, saved_hidden, w_in, w_out):
    source = (jnp.arange(TOKENS) // TOK_DEV).astype(jnp.int32)
    place = (expert_id * SLOT_ROWS + source * CAP + slot).astype(jnp.int32)
    target = jnp.where(dropped == 1, EXPERTS * SLOT_ROWS, place).astype(jnp.int32)
    scaled = (gate[:, None] * out_grad.astype(jnp.float32)).astype(jnp.bfloat16)
    routed = jnp.zeros((EXPERTS * SLOT_ROWS, D), jnp.bfloat16).at[target].set(tokens, mode="drop")
    routed_grad = jnp.zeros((EXPERTS * SLOT_ROWS, D), jnp.bfloat16).at[target].set(scaled, mode="drop")
    routed = routed.reshape(EXPERTS, SLOT_ROWS, D)
    routed_grad = routed_grad.reshape(EXPERTS, SLOT_ROWS, D)
    hidden_all = saved_hidden.reshape(SLOT_ROWS, EXPERTS, FF).transpose(1, 0, 2)
    w_in_all = w_in.reshape(D, EXPERTS, FF).transpose(1, 0, 2)
    w_out_all = w_out.reshape(EXPERTS, FF, D)
    slot_grad, slot_gate, w_in_parts, w_out_parts = lax.map(one_expert, (routed, routed_grad, hidden_all, w_in_all, w_out_all))
    index_back = jnp.where(dropped == 1, 0, place).astype(jnp.int32)
    flat_grad = slot_grad.reshape(EXPERTS * SLOT_ROWS, D)
    flat_gate = slot_gate.reshape(EXPERTS * SLOT_ROWS)
    token_grad = jnp.where(dropped[:, None] == 1, jnp.float32(0.0), flat_grad[index_back]).astype(jnp.bfloat16)
    gate_grad = jnp.where(dropped == 1, jnp.float32(0.0), flat_gate[index_back] / gate)
    w_in_grad = w_in_parts.transpose(1, 0, 2).reshape(D, EXPERTS * FF)
    w_out_grad = w_out_parts.reshape(EXPERTS * FF, D)
    return token_grad, gate_grad, w_in_grad, w_out_grad
```

```python
import jax
import jax.numpy as jnp
from jax import lax
from jax.sharding import PartitionSpec as P

SPLIT = 8
CORE, LOW, HIGH = 1, 2, 4


def normal_parts(hidden):
    normal_cdf = 0.5 * (1.0 + jax.scipy.special.erf(hidden * 0.7071067811865476))
    density = jnp.exp(-0.5 * hidden * hidden) * 0.3989422804014327
    return (normal_cdf, density)


def bits(core):
    return (HIGH, LOW, CORE) if core == 0 else (LOW, HIGH, CORE)


def pairs(devices, step):
    return [(i, i ^ bits(i % 2)[step]) for i in range(devices)]


def gather_rows(rows, devices):
    for step in range(3):
        rows = jnp.concatenate([rows, lax.ppermute(rows, "expert", pairs(devices, step))])
    return rows


def scatter_sum(rows, devices):
    for step in (2, 1, 0):
        half = rows.shape[0] // 2
        got = lax.ppermute(rows[half:], "expert", pairs(devices, step))
        total = rows[:half].astype(jnp.float32) + got.astype(jnp.float32)
        rows = total.astype(rows.dtype) if step else total
    return rows


def shift(devices, by):
    return [(i, (i + by * SPLIT) % devices) for i in range(devices)]


def body(tokens, out_grad, gate, expert_id, dropped, slot, saved_hidden, w_in, w_out):
    devices = lax.axis_size("expert")
    experts = devices // SPLIT
    slots = saved_hidden.shape[0] // devices
    hidden_units = saved_hidden.shape[1]
    me = lax.axis_index("expert")
    my_expert, my_place = me // SPLIT, me % SPLIT

    scaled = (gate[:, None] * out_grad.astype(jnp.float32)).astype(jnp.bfloat16)
    ahead = lax.rem(expert_id - my_expert + experts, experts)
    place = jnp.where(dropped == 1, -1, ahead * slots + slot)
    chosen = lax.broadcasted_iota(jnp.int32, (experts * slots, place.shape[0]), 0) == place[None, :]
    onehot = chosen.astype(jnp.bfloat16)

    def to_slots(values):
        return jnp.dot(onehot, values, preferred_element_type=jnp.float32).astype(jnp.bfloat16)

    def dispatch(values):
        buffer = to_slots(values)
        far = jnp.concatenate(
            [
                lax.ppermute(buffer[s * slots : (s + 1) * slots], "expert", shift(devices, s))
                for s in range(1, experts)
            ]
        )
        return gather_rows(buffer[:slots], devices), gather_rows(far, devices)

    core = me % 2
    near_masks = []
    for i in range(SPLIT):
        swapped = core ^ (i >> 2)
        first, second = jnp.where(swapped, LOW, HIGH), jnp.where(swapped, HIGH, LOW)
        near_masks.append((i & 1) * first + ((i >> 1) & 1) * second + (i >> 2) * CORE)
    near_order = jnp.stack([my_expert * SPLIT + (my_place ^ m) for m in near_masks])
    far_order = jnp.stack(
        [
            lax.rem(my_expert - s + experts, experts) * SPLIT + (my_place ^ m)
            for m in near_masks
            for s in range(1, experts)
        ]
    )
    by_source = saved_hidden.reshape(devices, slots, hidden_units)
    grads = dispatch(scaled)
    routed = dispatch(tokens)

    returned, gate_parts = [], []
    w_out_grad = w_in_grad = jnp.float32(0.0)
    for order, rows, routed_grad in zip((near_order, far_order), routed, grads):
        hidden = by_source[order].reshape(rows.shape[0], hidden_units).astype(jnp.float32)
        normal_cdf, density = normal_parts(hidden)
        activated = hidden * normal_cdf
        activated_b = activated.astype(jnp.bfloat16)
        grad_act = lax.dot_general(
            routed_grad, w_out, (((1,), (1,)), ((), ())), preferred_element_type=jnp.float32
        )
        hidden_grad = (grad_act * (normal_cdf + hidden * density)).astype(jnp.bfloat16)
        partial_grad = lax.dot_general(
            hidden_grad, w_in, (((1,), (1,)), ((), ())), preferred_element_type=jnp.float32
        ).astype(jnp.bfloat16)
        gate_parts.append(jnp.sum(grad_act * activated, axis=1).reshape(SPLIT, -1))
        w_out_grad += lax.dot_general(
            activated_b, routed_grad, (((0,), (0,)), ((), ())), preferred_element_type=jnp.float32
        )
        w_in_grad += lax.dot_general(
            rows, hidden_grad, (((0,), (0,)), ((), ())), preferred_element_type=jnp.float32
        )
        returned.append(scatter_sum(partial_grad, devices))

    def home(own, far):
        back = [
            lax.ppermute(far[(s - 1) * slots : s * slots], "expert", shift(devices, -s))
            for s in range(1, experts)
        ]
        return jnp.concatenate([own] + back)

    summed = home(returned[0].astype(jnp.bfloat16), returned[1].astype(jnp.bfloat16))
    gate_sum = scatter_sum(jnp.concatenate(gate_parts, axis=1), devices).reshape(-1)
    gate_sum = home(gate_sum[:slots], gate_sum[slots:])
    token_grad = lax.dot_general(
        onehot, summed, (((0,), (0,)), ((), ())), preferred_element_type=jnp.float32
    ).astype(jnp.bfloat16)
    slot_gate = jnp.sum(jnp.where(chosen, gate_sum[:, None], 0.0), axis=0)
    gate_grad = jnp.where(dropped == 1, jnp.float32(0.0), slot_gate / gate)
    return (token_grad, gate_grad, w_in_grad.astype(jnp.bfloat16), w_out_grad.astype(jnp.bfloat16))


def solution(mesh):
    in_specs = (
        P(("parts", "expert"), None),
        P(("parts", "expert"), None),
        P(("parts", "expert")),
        P(("parts", "expert")),
        P(("parts", "expert")),
        P(("parts", "expert")),
        P("parts", "expert"),
        P(None, "expert"),
        P("expert", None),
    )
    out_specs = (
        P(("parts", "expert"), None),
        P(("parts", "expert")),
        P("parts", "expert"),
        P(("parts", "expert"), None),
    )
    return jax.shard_map(body, mesh=mesh, in_specs=in_specs, out_specs=out_specs, check_vma=False)
```

```python
import jax
import jax.numpy as jnp
from jax import lax
from jax.sharding import PartitionSpec as P

SPLIT = 8


def normal_parts(hidden):
    normal_cdf = 0.5 * (1.0 + jax.scipy.special.erf(hidden * 0.7071067811865476))
    density = jnp.exp(-0.5 * hidden * hidden) * 0.3989422804014327
    return (normal_cdf, density)


def groups(devices):
    return [list(range(e, e + SPLIT)) for e in range(0, devices, SPLIT)]


def gather_rows(rows, devices):
    return lax.all_gather(
        rows, "expert", axis_index_groups=groups(devices), axis=0, tiled=True
    )


def scatter_sum(rows, devices):
    return lax.psum_scatter(
        rows, "expert", axis_index_groups=groups(devices), scatter_dimension=0, tiled=True
    )


def shift(devices, by):
    return [(i, (i + by * SPLIT) % devices) for i in range(devices)]


def body(tokens, out_grad, gate, expert_id, dropped, slot, saved_hidden, w_in, w_out):
    devices = lax.axis_size("expert")
    experts = devices // SPLIT
    slots = saved_hidden.shape[0] // devices
    hidden_units = saved_hidden.shape[1]
    me = lax.axis_index("expert")
    my_expert = me // SPLIT

    scaled = (gate[:, None] * out_grad.astype(jnp.float32)).astype(jnp.bfloat16)
    ahead = lax.rem(expert_id - my_expert + experts, experts)
    place = jnp.where(dropped == 1, -1, ahead * slots + slot)
    chosen = lax.broadcasted_iota(jnp.int32, (experts * slots, place.shape[0]), 0) == place[None, :]
    onehot = chosen.astype(jnp.bfloat16)

    def to_slots(values):
        return jnp.dot(onehot, values, preferred_element_type=jnp.float32).astype(jnp.bfloat16)

    def dispatch(values):
        buffer = to_slots(values)
        far = jnp.concatenate(
            [
                lax.ppermute(buffer[s * slots : (s + 1) * slots], "expert", shift(devices, s))
                for s in range(1, experts)
            ]
        )
        return gather_rows(buffer[:slots], devices), gather_rows(far, devices)

    near_order = my_expert * SPLIT + jnp.arange(SPLIT)
    far_order = jnp.stack(
        [
            lax.rem(my_expert - s + experts, experts) * SPLIT + i
            for i in range(SPLIT)
            for s in range(1, experts)
        ]
    )
    by_source = saved_hidden.reshape(devices, slots, hidden_units)
    grads = dispatch(scaled)
    routed = dispatch(tokens)

    returned, gate_parts = [], []
    w_out_grad = w_in_grad = jnp.float32(0.0)
    for order, rows, routed_grad in zip((near_order, far_order), routed, grads):
        hidden = by_source[order].reshape(rows.shape[0], hidden_units).astype(jnp.float32)
        normal_cdf, density = normal_parts(hidden)
        activated = hidden * normal_cdf
        activated_b = activated.astype(jnp.bfloat16)
        grad_act = lax.dot_general(
            routed_grad, w_out, (((1,), (1,)), ((), ())), preferred_element_type=jnp.float32
        )
        hidden_grad = (grad_act * (normal_cdf + hidden * density)).astype(jnp.bfloat16)
        partial_grad = lax.dot_general(
            hidden_grad, w_in, (((1,), (1,)), ((), ())), preferred_element_type=jnp.float32
        ).astype(jnp.bfloat16)
        gate_parts.append(jnp.sum(grad_act * activated, axis=1).reshape(SPLIT, -1))
        w_out_grad += lax.dot_general(
            activated_b, routed_grad, (((0,), (0,)), ((), ())), preferred_element_type=jnp.float32
        )
        w_in_grad += lax.dot_general(
            rows, hidden_grad, (((0,), (0,)), ((), ())), preferred_element_type=jnp.float32
        )
        returned.append(scatter_sum(partial_grad, devices))

    def home(own, far):
        back = [
            lax.ppermute(far[(s - 1) * slots : s * slots], "expert", shift(devices, -s))
            for s in range(1, experts)
        ]
        return jnp.concatenate([own] + back)

    summed = home(returned[0].astype(jnp.bfloat16), returned[1].astype(jnp.bfloat16))
    gate_sum = scatter_sum(jnp.concatenate(gate_parts, axis=1), devices).reshape(-1)
    gate_sum = home(gate_sum[:slots], gate_sum[slots:])
    token_grad = lax.dot_general(
        onehot, summed, (((0,), (0,)), ((), ())), preferred_element_type=jnp.float32
    ).astype(jnp.bfloat16)
    slot_gate = jnp.sum(jnp.where(chosen, gate_sum[:, None], 0.0), axis=0)
    gate_grad = jnp.where(dropped == 1, jnp.float32(0.0), slot_gate / gate)
    return (token_grad, gate_grad, w_in_grad.astype(jnp.bfloat16), w_out_grad.astype(jnp.bfloat16))


def solution(mesh):
    in_specs = (
        P(("parts", "expert"), None),
        P(("parts", "expert"), None),
        P(("parts", "expert")),
        P(("parts", "expert")),
        P(("parts", "expert")),
        P(("parts", "expert")),
        P("parts", "expert"),
        P(None, "expert"),
        P("expert", None),
    )
    out_specs = (
        P(("parts", "expert"), None),
        P(("parts", "expert")),
        P("parts", "expert"),
        P(("parts", "expert"), None),
    )
    return jax.shard_map(body, mesh=mesh, in_specs=in_specs, out_specs=out_specs, check_vma=False)
```

```python
import functools

import jax
import jax.numpy as jnp
from jax import lax
from jax.experimental import pallas as pl
from jax.experimental.pallas import tpu as pltpu
from jax.sharding import PartitionSpec as P

SPLIT = 8
CORE, LOW, HIGH = 1, 2, 4
TILE = 256
LANES = 128
VMEM = pl.BlockSpec(memory_space=pltpu.VMEM)
ANY = pl.BlockSpec(memory_space=pl.ANY)
F32, BF16 = jnp.float32, jnp.bfloat16


def params():
    return pltpu.CompilerParams(vmem_limit_bytes=48 * 1024 * 1024)


def cost(flops, moved, exps=0):
    return pl.CostEstimate(flops=flops, bytes_accessed=moved, transcendentals=exps)


def bits(core):
    return (HIGH, LOW, CORE) if core == 0 else (LOW, HIGH, CORE)


def meet(rows, step):
    devices = lax.axis_size("expert")
    return lax.ppermute(rows, "expert", [(i, i ^ bits(i % 2)[step]) for i in range(devices)])


def shift(rows, by):
    devices = lax.axis_size("expert")
    pairs = [(i, (i + by * SPLIT) % devices) for i in range(devices)]
    return lax.ppermute(rows, "expert", pairs)


def cross(rows, sign):
    experts = lax.axis_size("expert") // SPLIT
    if experts == 2:
        return shift(rows, sign)
    slots = rows.shape[0] // (experts - 1)
    return jnp.concatenate(
        [shift(rows[(s - 1) * slots : s * slots], sign * s) for s in range(1, experts)]
    )


def gather_pieces(rows, *beside):
    got = meet(rows, 0)
    two = jnp.concatenate([rows, after(got, *beside) if beside else got])
    more = meet(two, 1)
    pieces = [two, more, meet(two, 2), meet(more, 2)]
    if two.shape[0] % 16:
        return [jnp.concatenate(pieces)]
    return pieces


def after(value, *earlier):
    return lax.optimization_barrier((value, *earlier))[0]


def sources_met(me, experts):
    block = jnp.arange(SPLIT * (experts - 1), dtype=jnp.int32)

    def place(i):
        first = jnp.where(((me ^ (i >> 2)) & 1) == 1, LOW, HIGH)
        second = (LOW + HIGH) - first
        mask = (i & 1) * first + ((i >> 1) & 1) * second + (i >> 2) * CORE
        return (me & (SPLIT - 1)) ^ mask

    my_expert = me >> 3
    from_expert = my_expert - 1 - block % (experts - 1)
    from_expert = jnp.where(from_expert < 0, from_expert + experts, from_expert)
    near = my_expert * SPLIT + place(block[:SPLIT])
    return near, from_expert * SPLIT + place(block // (experts - 1))


def slot_places(expert_id, dropped, slot, slots):
    devices = lax.axis_size("expert")
    ahead = expert_id - lax.axis_index("expert") // SPLIT
    ahead = jnp.where(ahead < 0, ahead + devices // SPLIT, ahead)
    return jnp.where(dropped == 1, -1, ahead * slots + slot)


def chosen(place, first, count):
    rows = lax.broadcasted_iota(jnp.int32, (count, place.shape[1]), 0) + first
    return rows == place


def place_kernel(slots, scale, expert_id, dropped, slot, gate, values, near, far):
    place = slot_places(expert_id[...], dropped[...], slot[...], slots)
    rows = values[...]
    if scale:
        count = rows.shape[0]
        across = lax.broadcasted_iota(jnp.int32, (count, count), 1)
        down = lax.broadcasted_iota(jnp.int32, (count, count), 0)
        column = jnp.sum(jnp.where(across == down, gate[...], 0.0), axis=1, keepdims=True)
        rows = (column * rows.astype(F32)).astype(BF16)
    for first, out in ((0, near), (slots, far)):
        onehot = chosen(place, first, out.shape[0]).astype(F32).astype(BF16)
        out[...] = jnp.dot(onehot, rows, preferred_element_type=F32).astype(BF16)


def to_slots(slots, scale, expert_id, dropped, slot, gate, values):
    experts = lax.axis_size("expert") // SPLIT
    width = values.shape[1]
    return pl.pallas_call(
        functools.partial(place_kernel, slots, scale),
        out_shape=(
            jax.ShapeDtypeStruct((slots, width), BF16),
            jax.ShapeDtypeStruct(((experts - 1) * slots, width), BF16),
        ),
        in_specs=[VMEM] * 5,
        out_specs=(VMEM, VMEM),
        compiler_params=params(),
        cost_estimate=cost(2 * experts * slots * values.size, 6 * values.size),
        name="rows_to_slots",
    )(expert_id, dropped, slot, gate, values)


def home_kernel(slots, expert_id, dropped, slot, gate, kept, got, back, token_grad, gate_grad):
    place = slot_places(expert_id[...], dropped[...], slot[...], slots)
    width = token_grad.shape[1]
    near = kept[...].astype(F32) + got[...].astype(F32)
    total = jnp.zeros(token_grad.shape, F32)
    gates = jnp.zeros(gate_grad.shape, F32)
    for first, rows in ((0, near), (slots, back[...].astype(F32))):
        picks = chosen(place, first, rows.shape[0])
        total += lax.dot_general(
            picks.astype(F32).astype(BF16),
            rows[:, :width].astype(BF16),
            (((0,), (0,)), ((), ())),
            preferred_element_type=F32,
        )
        column = rows[:, width : width + 1]
        gates += jnp.sum(jnp.where(picks, column, 0.0), axis=0, keepdims=True)
    token_grad[...] = total.astype(BF16)
    gate_grad[...] = jnp.where(dropped[...] == 1, 0.0, gates / gate[...])


def to_tokens(slots, expert_id, dropped, slot, gate, kept, got, back):
    count, width = expert_id.shape[1], kept.shape[1] - LANES
    return pl.pallas_call(
        functools.partial(home_kernel, slots),
        out_shape=(
            jax.ShapeDtypeStruct((count, width), BF16),
            jax.ShapeDtypeStruct((1, count), F32),
        ),
        in_specs=[VMEM] * 7,
        out_specs=(VMEM, VMEM),
        compiler_params=params(),
        name="slots_to_tokens",
    )(expert_id, dropped, slot, gate, kept, got, back)


def activation_kernel(order, hidden, activated, slope):
    rows = hidden.shape[1]
    step = 16 if rows % 16 == 0 else rows

    def chunk(i, carry):
        at = pl.ds(i * step, step) if rows > step else slice(None)
        h = hidden[0, at, :].astype(F32)
        cdf = 0.5 * (1.0 + lax.erf(h * 0.7071067811865476))
        density = jnp.exp(-0.5 * h * h) * 0.3989422804014327
        activated[0, at, :] = (h * cdf).astype(BF16)
        slope[0, at, :] = cdf + h * density
        return carry

    lax.fori_loop(0, rows // step, chunk, 0)


def activation(by_source, order):
    _, slots, units = by_source.shape
    block = (1, slots, units)
    shape = (order.shape[0], slots, units)
    size = order.shape[0] * slots * units
    act, slope = pl.pallas_call(
        activation_kernel,
        grid_spec=pltpu.PrefetchScalarGridSpec(
            num_scalar_prefetch=1,
            grid=(order.shape[0],),
            in_specs=[pl.BlockSpec(block, lambda i, order: (order[i], 0, 0))],
            out_specs=[pl.BlockSpec(block, lambda i, order: (i, 0, 0))] * 2,
        ),
        out_shape=(jax.ShapeDtypeStruct(shape, BF16), jax.ShapeDtypeStruct(shape, F32)),
        compiler_params=params(),
        cost_estimate=cost(60 * size, 8 * size, 2 * size),
        name="activation",
    )(order, by_source)
    return act.reshape(-1, units), slope.reshape(-1, units)


def copies(pairs, sem):
    made = [pltpu.make_async_copy(src, dst, sem.at[i]) for i, (src, dst) in enumerate(pairs)]
    for copy in made:
        copy.start()
    return made


def row_blocks(refs, buffer):
    pairs, first = [], 0
    for ref in refs:
        count = ref.shape[0]
        pairs.append((ref, buffer.at[pl.ds(first, count)]))
        first += count
    return pairs


def slot_grad_kernel(pieces, *refs):
    grads = refs[:pieces]
    w_out, w_in, act, slope, hidden_grad, kept, sent = refs[pieces : pieces + 7]
    g, wo, wi, a, s, hg, part, in_sem, out_sem = refs[pieces + 7 :]
    rows, units = hg.shape
    width = g.shape[1]
    half = rows // 2
    wo_tiles, wi_tiles = units // TILE, width // TILE
    pairs = row_blocks(grads, g)
    pairs += [(w_out.at[pl.ds(j * TILE, TILE)], wo.at[pl.ds(j * TILE, TILE)]) for j in range(wo_tiles)]
    pairs += [(act, a), (slope, s)]
    pairs += [(w_in.at[pl.ds(j * TILE, TILE)], wi.at[pl.ds(j * TILE, TILE)]) for j in range(wi_tiles)]
    loads = copies(pairs, in_sem)
    for copy in loads[:pieces]:
        copy.wait()
    loads = loads[pieces:]
    stores = []

    def store(src, dst):
        copy = pltpu.make_async_copy(src, dst, out_sem.at[len(stores)])
        copy.start()
        stores.append(copy)

    gates = jnp.zeros((rows, 1), F32)
    for j in range(wo_tiles):
        at = slice(j * TILE, (j + 1) * TILE)
        loads[j].wait()
        grad_act = lax.dot_general(
            g[...], wo[at, :], (((1,), (1,)), ((), ())), preferred_element_type=F32
        )
        if j == 0:
            loads[wo_tiles].wait()
            loads[wo_tiles + 1].wait()
        hg[:, at] = (grad_act * s[:, at]).astype(BF16)
        gates += jnp.sum(grad_act * a[:, at].astype(F32), axis=1, keepdims=True)
    store(hg, hidden_grad)
    part[:, width:] = jnp.broadcast_to(gates, (rows, LANES)).astype(BF16)
    loads = loads[wo_tiles + 2 :]

    def store_columns(at):
        store(part.at[pl.ds(half, half), at], sent.at[:, at])
        store(part.at[pl.ds(0, half), at], kept.at[:, at])

    store_columns(pl.ds(width, LANES))
    for j in range(wi_tiles):
        loads[j].wait()
        at = slice(j * TILE, (j + 1) * TILE)
        part[:, at] = lax.dot_general(
            hg[...], wi[at, :], (((1,), (1,)), ((), ())), preferred_element_type=F32
        ).astype(BF16)
        store_columns(pl.ds(j * TILE, TILE))
    for copy in stores:
        copy.wait()


def slot_grads(grads, w_out, w_in, act, slope):
    rows, units = act.shape
    width = w_in.shape[0]
    tiles = units // TILE, width // TILE
    wide = width + LANES
    return pl.pallas_call(
        functools.partial(slot_grad_kernel, len(grads)),
        out_shape=(
            jax.ShapeDtypeStruct((rows, units), BF16),
            jax.ShapeDtypeStruct((rows // 2, wide), BF16),
            jax.ShapeDtypeStruct((rows // 2, wide), BF16),
        ),
        in_specs=[ANY] * (len(grads) + 4),
        out_specs=(ANY, ANY, ANY),
        scratch_shapes=[
            pltpu.VMEM((rows, width), BF16),
            pltpu.VMEM((units, width), BF16),
            pltpu.VMEM((width, units), BF16),
            pltpu.VMEM((rows, units), BF16),
            pltpu.VMEM((rows, units), F32),
            pltpu.VMEM((rows, units), BF16),
            pltpu.VMEM((rows, wide), BF16),
            pltpu.SemaphoreType.DMA((len(grads) + 2 + sum(tiles),)),
            pltpu.SemaphoreType.DMA((3 + 2 * tiles[1],)),
        ],
        compiler_params=params(),
        cost_estimate=cost(4 * rows * units * width, 4 * units * width + 4 * rows * wide),
        name="slot_grads",
    )(*grads, w_out, w_in, act, slope)


def weight_kernel(left_count, right_count, *refs):
    lefts = refs[:left_count]
    rights = refs[left_count : left_count + right_count]
    out, left, right, result, in_sem, out_sem = refs[left_count + right_count :]
    loads = copies(row_blocks(lefts, left) + row_blocks(rights, right), in_sem)
    for copy in loads:
        copy.wait()
    stores = []
    for j in range(left.shape[1] // TILE):
        at = slice(j * TILE, (j + 1) * TILE)
        result[at, :] = lax.dot_general(
            left[:, at], right[...], (((0,), (0,)), ((), ())), preferred_element_type=F32
        ).astype(BF16)
        rows = pl.ds(j * TILE, TILE)
        copy = pltpu.make_async_copy(result.at[rows], out.at[rows], out_sem.at[j])
        copy.start()
        stores.append(copy)
    for copy in stores:
        copy.wait()


def weight_grad(lefts, rights, name):
    rows = sum(x.shape[0] for x in lefts)
    m, n = lefts[0].shape[1], rights[0].shape[1]
    return pl.pallas_call(
        functools.partial(weight_kernel, len(lefts), len(rights)),
        out_shape=jax.ShapeDtypeStruct((m, n), BF16),
        in_specs=[ANY] * (len(lefts) + len(rights)),
        out_specs=ANY,
        scratch_shapes=[
            pltpu.VMEM((rows, m), BF16),
            pltpu.VMEM((rows, n), BF16),
            pltpu.VMEM((m, n), BF16),
            pltpu.SemaphoreType.DMA((len(lefts) + len(rights),)),
            pltpu.SemaphoreType.DMA((m // TILE,)),
        ],
        compiler_params=params(),
        cost_estimate=cost(2 * rows * m * n, 2 * (rows * m + rows * n + m * n)),
        name=name,
    )(*lefts, *rights)


def add(a, b):
    return (a.astype(F32) + b.astype(F32)).astype(BF16)


def sum_pieces(kept, sent):
    for step in (2, 1):
        got = meet(sent, step)
        half = kept.shape[0] // 2
        sent = add(kept[half:], got[half:])
        kept = add(kept[:half], got[:half])
    return kept, meet(sent, 0)


def body(tokens, out_grad, gate, expert_id, dropped, slot, saved_hidden, w_in, w_out):
    devices = lax.axis_size("expert")
    experts = devices // SPLIT
    slots = saved_hidden.shape[0] // devices
    units = saved_hidden.shape[1]
    me = lax.axis_index("expert")
    row = lambda x: x.reshape(1, -1)
    gate, routing = row(gate), (row(expert_id), row(dropped), row(slot))

    near_order, far_order = sources_met(me, experts)
    by_source = saved_hidden.reshape(devices, slots, units)

    near_grad, far_grad = to_slots(slots, True, *routing, gate, out_grad)
    near_act, near_slope = activation(by_source, near_order)
    far_act, far_slope = activation(by_source, far_order)
    near_rows, far_rows = to_slots(slots, False, *routing, gate, tokens)

    near_grads = gather_pieces(near_grad, near_act)
    far_grad = after(cross(far_grad, 1), far_act, near_grads[0])
    far_rows = cross(after(far_rows, far_grad), 1)
    far_grads = gather_pieces(far_grad)
    near_grads[0] = after(near_grads[0], far_grads[0])

    near_hg, near_kept, near_sent = slot_grads(near_grads, w_out, w_in, near_act, near_slope)
    near_rows = gather_pieces(after(near_rows, far_grads[-3:][0]))
    near_kept, near_got = sum_pieces(near_kept, near_sent)
    far_hg, far_kept, far_sent = slot_grads(far_grads, w_out, w_in, far_act, far_slope)
    far_rows = gather_pieces(far_rows)
    far_kept, far_got = sum_pieces(far_kept, far_sent)
    far_sum = add(far_kept, far_got)
    near_act = after(near_act, far_sum)

    w_out_grad = weight_grad([near_act, far_act], near_grads + far_grads, "w_out_grad")
    w_in_grad = weight_grad(near_rows + far_rows, [near_hg, far_hg], "w_in_grad")
    back = after(cross(far_sum, -1), w_out_grad, w_in_grad)
    token_grad, gate_grad = to_tokens(slots, *routing, gate, near_kept, near_got, back)
    return (token_grad, gate_grad.reshape(-1), w_in_grad, w_out_grad)


def solution(mesh):
    in_specs = (
        P(("parts", "expert"), None),
        P(("parts", "expert"), None),
        P(("parts", "expert")),
        P(("parts", "expert")),
        P(("parts", "expert")),
        P(("parts", "expert")),
        P("parts", "expert"),
        P(None, "expert"),
        P("expert", None),
    )
    out_specs = (
        P(("parts", "expert"), None),
        P(("parts", "expert")),
        P("parts", "expert"),
        P(("parts", "expert"), None),
    )
    return jax.shard_map(body, mesh=mesh, in_specs=in_specs, out_specs=out_specs, check_vma=False)
```

```python
import functools

import jax
import jax.numpy as jnp
from jax import lax
from jax.experimental import pallas as pl
from jax.experimental.pallas import tpu as pltpu
from jax.sharding import PartitionSpec as P

SPLIT = 8
CORE, LOW, HIGH = 1, 2, 4
LANES = 128
VMEM = pl.BlockSpec(memory_space=pltpu.VMEM)
F32, BF16 = jnp.float32, jnp.bfloat16


def params():
    return pltpu.CompilerParams(vmem_limit_bytes=48 * 1024 * 1024)


def cost(flops, moved, exps=0):
    return pl.CostEstimate(flops=flops, bytes_accessed=moved, transcendentals=exps)


def bits(core):
    return (HIGH, LOW, CORE) if core == 0 else (LOW, HIGH, CORE)


def meet(rows, step):
    devices = lax.axis_size("expert")
    return lax.ppermute(rows, "expert", [(i, i ^ bits(i % 2)[step]) for i in range(devices)])


def shift(rows, by):
    devices = lax.axis_size("expert")
    pairs = [(i, (i + by * SPLIT) % devices) for i in range(devices)]
    return lax.ppermute(rows, "expert", pairs)


def cross(rows, sign):
    experts = lax.axis_size("expert") // SPLIT
    if experts == 2:
        return shift(rows, sign)
    slots = rows.shape[0] // (experts - 1)
    return jnp.concatenate(
        [shift(rows[(s - 1) * slots : s * slots], sign * s) for s in range(1, experts)]
    )


def after(value, *earlier):
    return lax.optimization_barrier((value, *earlier))[0]


def sources_met(me, experts):
    block = jnp.arange(SPLIT * (experts - 1), dtype=jnp.int32)

    def place(i):
        first = jnp.where(((me ^ (i >> 2)) & 1) == 1, LOW, HIGH)
        second = (LOW + HIGH) - first
        mask = (i & 1) * first + ((i >> 1) & 1) * second + (i >> 2) * CORE
        return (me & (SPLIT - 1)) ^ mask

    my_expert = me >> 3
    from_expert = my_expert - 1 - block % (experts - 1)
    from_expert = jnp.where(from_expert < 0, from_expert + experts, from_expert)
    near = my_expert * SPLIT + place(block[:SPLIT])
    return near, from_expert * SPLIT + place(block // (experts - 1))


def slot_places(expert_id, dropped, slot, slots):
    devices = lax.axis_size("expert")
    ahead = expert_id - lax.axis_index("expert") // SPLIT
    ahead = jnp.where(ahead < 0, ahead + devices // SPLIT, ahead)
    return jnp.where(dropped == 1, -1, ahead * slots + slot)


def chosen(place, first, count):
    rows = lax.broadcasted_iota(jnp.int32, (count, place.shape[1]), 0) + first
    return rows == place


def copies(sources, buffers, sem):
    made = [
        pltpu.make_async_copy(src, dst, sem.at[i]) for i, (src, dst) in enumerate(zip(sources, buffers))
    ]
    for copy in made:
        copy.start()
    for copy in made:
        copy.wait()


def place_kernel(slots, scale, *refs):
    near, far = refs[5:7]
    expert_id, dropped, slot, gate, values = refs[7:12]
    copies(refs[:5], refs[7:12], refs[12])
    place = slot_places(expert_id[...], dropped[...], slot[...], slots)
    rows = values[...]
    if scale:
        count = rows.shape[0]
        across = lax.broadcasted_iota(jnp.int32, (count, count), 1)
        down = lax.broadcasted_iota(jnp.int32, (count, count), 0)
        column = jnp.sum(jnp.where(across == down, gate[...], 0.0), axis=1, keepdims=True)
        rows = (column * rows.astype(F32)).astype(BF16)
    for first, out in ((0, near), (slots, far)):
        onehot = chosen(place, first, out.shape[0]).astype(F32).astype(BF16)
        out[...] = jnp.dot(onehot, rows, preferred_element_type=F32).astype(BF16)


def to_slots(slots, scale, *inputs):
    experts = lax.axis_size("expert") // SPLIT
    width = inputs[-1].shape[1]
    return pl.pallas_call(
        functools.partial(place_kernel, slots, scale),
        out_shape=(
            jax.ShapeDtypeStruct((slots, width), BF16),
            jax.ShapeDtypeStruct(((experts - 1) * slots, width), BF16),
        ),
        in_specs=[pl.BlockSpec(memory_space=pltpu.HBM)] * 5,
        out_specs=(VMEM, VMEM),
        scratch_shapes=[pltpu.VMEM(x.shape, x.dtype) for x in inputs]
        + [pltpu.SemaphoreType.DMA((5,))],
        compiler_params=params(),
        cost_estimate=cost(2 * experts * slots * inputs[-1].size, 6 * inputs[-1].size),
        name="rows_to_slots",
    )(*inputs)


def home_kernel(slots, expert_id, dropped, slot, gate, kept, got, back, token_grad, gate_grad):
    place = slot_places(expert_id[...], dropped[...], slot[...], slots)
    width = token_grad.shape[1]
    near = kept[...].astype(F32) + got[...].astype(F32)
    total = jnp.zeros(token_grad.shape, F32)
    gates = jnp.zeros(gate_grad.shape, F32)
    for first, rows in ((0, near), (slots, back[...].astype(F32))):
        picks = chosen(place, first, rows.shape[0])
        total += lax.dot_general(
            picks.astype(F32).astype(BF16),
            rows[:, :width].astype(BF16),
            (((0,), (0,)), ((), ())),
            preferred_element_type=F32,
        )
        column = rows[:, width : width + 1]
        gates += jnp.sum(jnp.where(picks, column, 0.0), axis=0, keepdims=True)
    token_grad[...] = total.astype(BF16)
    gate_grad[...] = jnp.where(dropped[...] == 1, 0.0, gates / gate[...])


def to_tokens(slots, expert_id, dropped, slot, gate, kept, got, back):
    count, width = expert_id.shape[1], kept.shape[1] - LANES
    return pl.pallas_call(
        functools.partial(home_kernel, slots),
        out_shape=(
            jax.ShapeDtypeStruct((count, width), BF16),
            jax.ShapeDtypeStruct((1, count), F32),
        ),
        in_specs=[VMEM] * 7,
        out_specs=(VMEM, VMEM),
        compiler_params=params(),
        name="slots_to_tokens",
    )(expert_id, dropped, slot, gate, kept, got, back)


def activation_kernel(order, hidden, activated, slope):
    rows = hidden.shape[1]
    step = 16 if rows % 16 == 0 else rows

    def chunk(i, carry):
        at = pl.ds(i * step, step) if rows > step else slice(None)
        h = hidden[0, at, :].astype(F32)
        cdf = 0.5 * (1.0 + lax.erf(h * 0.7071067811865476))
        density = jnp.exp(-0.5 * h * h) * 0.3989422804014327
        activated[0, at, :] = (h * cdf).astype(BF16)
        slope[0, at, :] = cdf + h * density
        return carry

    lax.fori_loop(0, rows // step, chunk, 0)


def activation(by_source, order):
    _, slots, units = by_source.shape
    block = (1, slots, units)
    shape = (order.shape[0], slots, units)
    size = order.shape[0] * slots * units
    act, slope = pl.pallas_call(
        activation_kernel,
        grid_spec=pltpu.PrefetchScalarGridSpec(
            num_scalar_prefetch=1,
            grid=(order.shape[0],),
            in_specs=[pl.BlockSpec(block, lambda i, order: (order[i], 0, 0))],
            out_specs=[pl.BlockSpec(block, lambda i, order: (i, 0, 0))] * 2,
        ),
        out_shape=(jax.ShapeDtypeStruct(shape, BF16), jax.ShapeDtypeStruct(shape, F32)),
        compiler_params=params(),
        cost_estimate=cost(60 * size, 8 * size, 2 * size),
        name="activation",
    )(order, by_source)
    return act.reshape(-1, units), slope.reshape(-1, units)


def add(a, b):
    return (a.astype(F32) + b.astype(F32)).astype(BF16)


def halves(x):
    half = x.shape[0] // 2
    return x[:half], x[half:]


def add_halves(kept, got):
    kept, got = halves(kept), halves(got)
    return add(kept[0], got[0]), add(kept[1], got[1])


def product(a, b, dims):
    return lax.dot_general(a, b, (dims, ((), ())), preferred_element_type=F32)


def hidden_part(grads, w_out, act, slope):
    grad_act = product(grads, w_out, ((1,), (1,)))
    gates = jnp.sum(grad_act * act.astype(F32), axis=1, keepdims=True)
    return (grad_act * slope).astype(BF16), gates


def slot_part(hidden_grad, gates, w_in):
    part = product(hidden_grad, w_in, ((1,), (1,))).astype(BF16)
    gates = jnp.broadcast_to(gates, (gates.shape[0], LANES)).astype(BF16)
    return halves(jnp.concatenate([part, gates], axis=1))


def body(tokens, out_grad, gate, expert_id, dropped, slot, saved_hidden, w_in, w_out):
    devices = lax.axis_size("expert")
    experts = devices // SPLIT
    slots = saved_hidden.shape[0] // devices
    units = saved_hidden.shape[1]
    me = lax.axis_index("expert")
    row = lambda x: x.reshape(1, -1)
    routing = (row(expert_id), row(dropped), row(slot), row(gate))
    near_order, far_order = sources_met(me, experts)
    by_source = saved_hidden.reshape(devices, slots, units)
    join = jnp.concatenate

    near_grad, far_grad = to_slots(slots, True, *routing, out_grad)
    near_row, far_row = to_slots(slots, False, *routing, tokens)

    far_grad = cross(far_grad, 1)
    got = meet(near_grad, 0)
    near_act, near_slope = activation(by_source, near_order)
    got = after(got, near_act, near_row)
    near_two = join([near_grad, got])
    near_more = meet(near_two, 1)
    far_act, far_slope = activation(by_source, after(far_order, near_two))
    near_more = after(near_more, far_act)
    near_last = meet(near_two, 2), meet(near_more, 2)

    far_grad = after(far_grad, near_more)
    got = meet(far_grad, 0)
    near_grads = join([near_two, near_more, *near_last])
    near_hg, near_gates = hidden_part(near_grads, w_out, near_act, near_slope)
    got = after(got, near_hg)
    far_two = join([far_grad, got])
    far_more = meet(far_two, 1)
    near_kept, near_sent = slot_part(after(near_hg, far_two), near_gates, w_in)
    far_more = after(far_more, near_sent)
    far_last = meet(far_two, 2), meet(far_more, 2)
    near_got = meet(near_sent, 2)

    near_row, far_row = after(near_row, far_more), after(far_row, far_more)
    far_row = cross(far_row, 1)
    got = meet(near_row, 0)
    far_grads = join([far_two, far_more, *far_last])
    far_hg, far_gates = hidden_part(far_grads, w_out, far_act, far_slope)
    got = after(got, far_hg)
    near_row2 = join([near_row, got])
    near_row4 = meet(near_row2, 1)
    far_kept, far_sent = slot_part(after(far_hg, near_row2), far_gates, w_in)

    far_got = meet(far_sent, 2)
    far_kept, far_sent = add_halves(far_kept, far_got)
    far_got = meet(far_sent, 1)
    near_kept, near_sent = add_halves(near_kept, after(near_got, far_sent))
    near_got = meet(near_sent, 1)
    act = join([near_act, far_act])
    w_out_grad = product(after(act, far_sent), join([near_grads, far_grads]), ((0,), (0,))).astype(BF16)
    far_row_got = meet(far_row, 0)
    far_got = after(far_got, w_out_grad, far_row)
    far_kept, far_sent = add_halves(far_kept, far_got)
    far_got = meet(far_sent, 0)
    near_row4 = after(near_row4, far_sent)
    near_rows = join([near_row2, near_row4, meet(near_row2, 2), meet(near_row4, 2)])
    far_row2 = join([far_row, far_row_got])
    far_row4 = meet(far_row2, 1)
    far_got = after(far_got, far_row2, near_row4)
    far_sum = add(far_kept, far_got)
    back = cross(far_sum, -1)
    near_kept, near_sent = add_halves(near_kept, after(near_got, far_sum))
    near_got = meet(near_sent, 0)
    far_rows = join([far_row2, far_row4, meet(far_row2, 2), meet(far_row4, 2)])
    w_in_grad = product(
        join([near_rows, far_rows]), join([near_hg, far_hg]), ((0,), (0,))
    ).astype(BF16)
    back = after(back, w_in_grad)
    token_grad, gate_grad = to_tokens(slots, *routing, near_kept, near_got, back)
    return (token_grad, gate_grad.reshape(-1), w_in_grad, w_out_grad)


def solution(mesh):
    in_specs = (
        P(("parts", "expert"), None),
        P(("parts", "expert"), None),
        P(("parts", "expert")),
        P(("parts", "expert")),
        P(("parts", "expert")),
        P(("parts", "expert")),
        P("parts", "expert"),
        P(None, "expert"),
        P("expert", None),
    )
    out_specs = (
        P(("parts", "expert"), None),
        P(("parts", "expert")),
        P("parts", "expert"),
        P(("parts", "expert"), None),
    )
    return jax.shard_map(body, mesh=mesh, in_specs=in_specs, out_specs=out_specs, check_vma=False)
```

```python
import functools

import jax
import jax.numpy as jnp
from jax import lax
from jax.experimental import pallas as pl
from jax.experimental.pallas import tpu as pltpu
from jax.sharding import PartitionSpec as P

SPLIT = 8
CORE, LOW, HIGH = 1, 2, 4
LANES = 128
VMEM = pl.BlockSpec(memory_space=pltpu.VMEM)
F32, BF16 = jnp.float32, jnp.bfloat16


def params():
    return pltpu.CompilerParams(vmem_limit_bytes=48 * 1024 * 1024)


def cost(flops, moved, exps=0):
    return pl.CostEstimate(flops=flops, bytes_accessed=moved, transcendentals=exps)


def bits(core):
    return (HIGH, LOW, CORE) if core == 0 else (LOW, HIGH, CORE)


def meet(rows, step):
    devices = lax.axis_size("expert")
    return lax.ppermute(rows, "expert", [(i, i ^ bits(i % 2)[step]) for i in range(devices)])


def shift(rows, by):
    devices = lax.axis_size("expert")
    pairs = [(i, (i + by * SPLIT) % devices) for i in range(devices)]
    return lax.ppermute(rows, "expert", pairs)


def cross(rows, sign):
    experts = lax.axis_size("expert") // SPLIT
    if experts == 2:
        return shift(rows, sign)
    slots = rows.shape[0] // (experts - 1)
    return jnp.concatenate(
        [shift(rows[(s - 1) * slots : s * slots], sign * s) for s in range(1, experts)]
    )


def after(value, *earlier):
    return lax.optimization_barrier((value, *earlier))[0]


def sources_met(me, experts):
    block = jnp.arange(SPLIT * (experts - 1), dtype=jnp.int32)

    def place(i):
        first = jnp.where(((me ^ (i >> 2)) & 1) == 1, LOW, HIGH)
        second = (LOW + HIGH) - first
        mask = (i & 1) * first + ((i >> 1) & 1) * second + (i >> 2) * CORE
        return (me & (SPLIT - 1)) ^ mask

    my_expert = me >> 3
    from_expert = my_expert - 1 - block % (experts - 1)
    from_expert = jnp.where(from_expert < 0, from_expert + experts, from_expert)
    near = my_expert * SPLIT + place(block[:SPLIT])
    return near, from_expert * SPLIT + place(block // (experts - 1))


def pack_routing(expert_id, dropped, slot, gate, slots):
    devices = lax.axis_size("expert")
    ahead = expert_id - (lax.axis_index("expert") >> 3)
    ahead = jnp.where(ahead < 0, ahead + devices // SPLIT, ahead)
    place = jnp.where(dropped == 1, -1, ahead * slots + slot)
    return jnp.stack([place.astype(F32), gate])


def chosen(place, first, count):
    rows = lax.broadcasted_iota(jnp.int32, (count, place.shape[1]), 0) + first
    return rows == place


def place_kernel(slots, scale, routing, values, near, far):
    place = routing[0:1, :].astype(jnp.int32)
    rows = values[...]
    if scale:
        count = rows.shape[0]
        across = lax.broadcasted_iota(jnp.int32, (count, count), 1)
        down = lax.broadcasted_iota(jnp.int32, (count, count), 0)
        gates = jnp.where(across == down, routing[1:2, :], 0.0)
        column = jnp.sum(gates, axis=1, keepdims=True)
        rows = (column * rows.astype(F32)).astype(BF16)
    for first, out in ((0, near), (slots, far)):
        onehot = chosen(place, first, out.shape[0]).astype(F32).astype(BF16)
        out[...] = jnp.dot(onehot, rows, preferred_element_type=F32).astype(BF16)


def to_slots(slots, scale, routing, values):
    experts = lax.axis_size("expert") // SPLIT
    width = values.shape[1]
    return pl.pallas_call(
        functools.partial(place_kernel, slots, scale),
        out_shape=(
            jax.ShapeDtypeStruct((slots, width), BF16),
            jax.ShapeDtypeStruct(((experts - 1) * slots, width), BF16),
        ),
        in_specs=[VMEM] * 2,
        out_specs=(VMEM, VMEM),
        compiler_params=params(),
        cost_estimate=cost(values.size, values.size),
        name="rows_to_slots",
    )(routing, values)


def home_kernel(slots, routing, kept, got, back, token_grad, gate_grad):
    place = routing[0:1, :].astype(jnp.int32)
    width = token_grad.shape[1]
    near = kept[...].astype(F32) + got[...].astype(F32)
    total = jnp.zeros(token_grad.shape, F32)
    gates = jnp.zeros(gate_grad.shape, F32)
    for first, rows in ((0, near), (slots, back[...].astype(F32))):
        picks = chosen(place, first, rows.shape[0])
        total += lax.dot_general(
            picks.astype(F32).astype(BF16),
            rows[:, :width].astype(BF16),
            (((0,), (0,)), ((), ())),
            preferred_element_type=F32,
        )
        column = rows[:, width : width + 1]
        gates += jnp.sum(jnp.where(picks, column, 0.0), axis=0, keepdims=True)
    token_grad[...] = total.astype(BF16)
    gate_grad[...] = jnp.where(place < 0, 0.0, gates / routing[1:2, :])


def to_tokens(slots, routing, kept, got, back):
    count, width = routing.shape[1], kept.shape[1] - LANES
    return pl.pallas_call(
        functools.partial(home_kernel, slots),
        out_shape=(
            jax.ShapeDtypeStruct((count, width), BF16),
            jax.ShapeDtypeStruct((1, count), F32),
        ),
        in_specs=[VMEM] * 4,
        out_specs=(VMEM, VMEM),
        compiler_params=params(),
        name="slots_to_tokens",
    )(routing, kept, got, back)


def activation_kernel(order, hidden, activated, slope):
    rows = hidden.shape[1]
    step = 16 if rows % 16 == 0 else rows

    def chunk(i, carry):
        at = pl.ds(i * step, step) if rows > step else slice(None)
        h = hidden[0, at, :].astype(F32)
        cdf = 0.5 * (1.0 + lax.erf(h * 0.7071067811865476))
        density = jnp.exp(-0.5 * h * h) * 0.3989422804014327
        activated[0, at, :] = (h * cdf).astype(BF16)
        slope[0, at, :] = cdf + h * density
        return carry

    lax.fori_loop(0, rows // step, chunk, 0)


def activation(by_source, order):
    _, slots, units = by_source.shape
    block = (1, slots, units)
    shape = (order.shape[0], slots, units)
    size = order.shape[0] * slots * units
    act, slope = pl.pallas_call(
        activation_kernel,
        grid_spec=pltpu.PrefetchScalarGridSpec(
            num_scalar_prefetch=1,
            grid=(order.shape[0],),
            in_specs=[pl.BlockSpec(block, lambda i, order: (order[i], 0, 0))],
            out_specs=[pl.BlockSpec(block, lambda i, order: (i, 0, 0))] * 2,
        ),
        out_shape=(jax.ShapeDtypeStruct(shape, BF16), jax.ShapeDtypeStruct(shape, F32)),
        compiler_params=params(),
        cost_estimate=cost(size, size),
        name="activation",
    )(order, by_source)
    return act.reshape(-1, units), slope.reshape(-1, units)


def add(a, b):
    return (a.astype(F32) + b.astype(F32)).astype(BF16)


def halves(x):
    half = x.shape[0] // 2
    return x[:half], x[half:]


def add_halves(kept, got):
    kept, got = halves(kept), halves(got)
    return add(kept[0], got[0]), add(kept[1], got[1])


def split_slots(rows, experts):
    rows = rows.reshape(experts - 1, 2, -1, rows.shape[1])
    return [rows[:, i].reshape(-1, rows.shape[3]) for i in range(2)]


def join_slots(a, b, experts):
    a, b = [x.reshape(experts - 1, -1, x.shape[1]) for x in (a, b)]
    return jnp.concatenate([a, b], axis=1).reshape(-1, a.shape[2])


def product(a, b, dims):
    return lax.dot_general(a, b, (dims, ((), ())), preferred_element_type=F32)


def hidden_part(grads, w_out, act, slope):
    grad_act = product(grads, w_out, ((1,), (1,)))
    gates = jnp.sum(grad_act * act.astype(F32), axis=1, keepdims=True)
    return (grad_act * slope).astype(BF16), gates


def slot_part(hidden_grad, gates, w_in):
    part = product(hidden_grad, w_in, ((1,), (1,))).astype(BF16)
    gates = jnp.broadcast_to(gates, (gates.shape[0], LANES)).astype(BF16)
    return halves(jnp.concatenate([part, gates], axis=1))


def body(tokens, out_grad, gate, expert_id, dropped, slot, saved_hidden, w_in, w_out):
    devices = lax.axis_size("expert")
    experts = devices // SPLIT
    slots = saved_hidden.shape[0] // devices
    units = saved_hidden.shape[1]
    me = lax.axis_index("expert")
    routing = pack_routing(expert_id, dropped, slot, gate, slots)
    near_order, far_order = sources_met(me, experts)
    by_source = saved_hidden.reshape(devices, slots, units)
    join = jnp.concatenate

    near_grad, far_grad = to_slots(slots, True, routing, out_grad)
    near_row, far_row = to_slots(slots, False, routing, tokens)

    far_grad_a, far_grad_b = split_slots(far_grad, experts)
    far_grad_a = cross(far_grad_a, 1)
    got = meet(near_grad, 0)
    near_act, near_slope = activation(by_source, near_order)
    far_grad_a = after(far_grad_a, near_act, near_row)
    far_grad_b = cross(after(far_grad_b, far_grad_a), 1)
    got = after(got, far_grad_a)
    near_two = join([near_grad, got])
    near_more = meet(near_two, 1)
    near_last = meet(near_two, 2)
    near_row_got = meet(after(near_row, near_two), 0)
    far_act, far_slope = activation(by_source, after(far_order, near_two))
    far_grad = join_slots(far_grad_a, after(far_grad_b, far_act), experts)
    far_got = meet(far_grad, 0)
    far_row_a, far_row_b = split_slots(far_row, experts)
    far_row_a = cross(after(far_row_a, far_grad), 1)
    near_more = after(near_more, far_grad)
    near_last = near_last, meet(near_more, 2)
    near_row2 = join([near_row, after(near_row_got, near_more)])
    near_row4 = meet(near_row2, 1)

    near_grads = join([near_two, near_more, *near_last])
    near_grads = after(near_grads, near_row2)
    near_hg, near_gates = hidden_part(near_grads, w_out, near_act, near_slope)
    far_two = join([far_grad, after(far_got, near_hg)])
    far_more = meet(far_two, 1)
    far_last = meet(far_two, 2)
    near_kept, near_sent = slot_part(after(near_hg, far_two), near_gates, w_in)
    near_got = meet(near_sent, 2)
    far_row_a = after(far_row_a, near_sent)
    far_more = after(far_more, far_row_a)
    far_last = far_last, meet(far_more, 2)
    far_row_b = cross(after(far_row_b, far_row_a), 1)
    near_row4 = after(near_row4, far_more)
    near_rows = join([near_row2, near_row4, meet(near_row2, 2), meet(near_row4, 2)])
    near_kept, near_sent = add_halves(near_kept, after(near_got, far_row_a))
    near_got = meet(near_sent, 1)

    far_grads = join([far_two, far_more, *far_last])
    far_grads = after(far_grads, near_sent)
    far_hg, far_gates = hidden_part(far_grads, w_out, far_act, far_slope)
    far_kept, far_sent = slot_part(far_hg, far_gates, w_in)
    far_kept, far_sent = add_halves(far_kept, meet(far_sent, 2))
    far_got = meet(far_sent, 1)
    far_row = join_slots(far_row_a, after(far_row_b, far_sent), experts)
    far_row_got = meet(far_row, 0)
    near_act, near_grads = after(near_act, far_row), after(near_grads, far_row)
    w_out_grad = product(
        join([near_act, far_act]), join([near_grads, far_grads]), ((0,), (0,))
    ).astype(BF16)
    far_row2 = join([far_row, after(far_row_got, w_out_grad)])
    far_row4 = meet(far_row2, 1)
    far_kept, far_sent = add_halves(far_kept, after(far_got, far_row2))
    far_got = meet(far_sent, 0)
    near_kept, near_sent = add_halves(near_kept, after(near_got, far_sent))
    near_got = meet(near_sent, 0)
    far_sum = add(far_kept, after(far_got, near_sent))
    back = cross(far_sum, -1)
    far_row4 = after(far_row4, far_sum)
    far_rows = join([far_row2, far_row4, meet(far_row2, 2), meet(far_row4, 2)])
    w_in_grad = product(
        join([near_rows, far_rows]), join([near_hg, far_hg]), ((0,), (0,))
    ).astype(BF16)
    near_got, back = after(near_got, w_in_grad), after(back, w_in_grad)
    token_grad, gate_grad = to_tokens(slots, routing, near_kept, near_got, back)
    return (token_grad, gate_grad.reshape(-1), w_in_grad, w_out_grad)


def solution(mesh):
    in_specs = (
        P(("parts", "expert"), None),
        P(("parts", "expert"), None),
        P(("parts", "expert")),
        P(("parts", "expert")),
        P(("parts", "expert")),
        P(("parts", "expert")),
        P("parts", "expert"),
        P(None, "expert"),
        P("expert", None),
    )
    out_specs = (
        P(("parts", "expert"), None),
        P(("parts", "expert")),
        P("parts", "expert"),
        P(("parts", "expert"), None),
    )
    return jax.shard_map(body, mesh=mesh, in_specs=in_specs, out_specs=out_specs, check_vma=False)
```

```python
import functools

import jax
import jax.numpy as jnp
from jax import lax
from jax.experimental import pallas as pl
from jax.experimental.pallas import tpu as pltpu
from jax.sharding import PartitionSpec as P

SPLIT = 8
CORE, LOW, HIGH = 1, 2, 4
LANES = 128
VMEM = pl.BlockSpec(memory_space=pltpu.VMEM)
F32, BF16 = jnp.float32, jnp.bfloat16


def params(mib):
    return pltpu.CompilerParams(vmem_limit_bytes=mib * 1024 * 1024)


def cost(flops, moved, exps=0):
    return pl.CostEstimate(flops=flops, bytes_accessed=moved, transcendentals=exps)


def bits(core):
    return (HIGH, LOW, CORE) if core == 0 else (LOW, HIGH, CORE)


def meet(rows, step):
    devices = lax.axis_size("expert")
    return lax.ppermute(rows, "expert", [(i, i ^ bits(i % 2)[step]) for i in range(devices)])


def shift(rows, by):
    devices = lax.axis_size("expert")
    pairs = [(i, (i + by * SPLIT) % devices) for i in range(devices)]
    return lax.ppermute(rows, "expert", pairs)


def cross(rows, sign):
    experts = lax.axis_size("expert") // SPLIT
    if experts == 2:
        return shift(rows, sign)
    slots = rows.shape[0] // (experts - 1)
    return jnp.concatenate(
        [shift(rows[(s - 1) * slots : s * slots], sign * s) for s in range(1, experts)]
    )


def after(value, *earlier):
    return lax.optimization_barrier((value, *earlier))[0]


def sources_met(me, experts):
    block = jnp.arange(SPLIT * (experts - 1), dtype=jnp.int32)

    def place(i):
        first = jnp.where(((me ^ (i >> 2)) & 1) == 1, LOW, HIGH)
        second = (LOW + HIGH) - first
        mask = (i & 1) * first + ((i >> 1) & 1) * second + (i >> 2) * CORE
        return (me & (SPLIT - 1)) ^ mask

    my_expert = me >> 3
    from_expert = my_expert - 1 - block % (experts - 1)
    from_expert = jnp.where(from_expert < 0, from_expert + experts, from_expert)
    near = my_expert * SPLIT + place(block[:SPLIT])
    return near, from_expert * SPLIT + place(block // (experts - 1))


def pack_routing(expert_id, dropped, slot, gate, slots):
    devices = lax.axis_size("expert")
    ahead = expert_id - (lax.axis_index("expert") >> 3)
    ahead = jnp.where(ahead < 0, ahead + devices // SPLIT, ahead)
    place = jnp.where(dropped == 1, -1, ahead * slots + slot)
    return place.reshape(1, -1), gate.reshape(1, -1)


def chosen(place, first, count):
    rows = lax.broadcasted_iota(jnp.int32, (count, place.shape[1]), 0) + first
    return rows == place


def place_kernel(slots, scale, place, gate, values, near, far):
    rows = values[...]
    if scale:
        count = rows.shape[0]
        across = lax.broadcasted_iota(jnp.int32, (count, count), 1)
        down = lax.broadcasted_iota(jnp.int32, (count, count), 0)
        gates = jnp.where(across == down, gate[...], 0.0)
        column = jnp.sum(gates, axis=1, keepdims=True)
        rows = (column * rows.astype(F32)).astype(BF16)
    for first, out in ((0, near), (slots, far)):
        onehot = chosen(place[...], first, out.shape[0]).astype(F32).astype(BF16)
        out[...] = jnp.dot(onehot, rows, preferred_element_type=F32).astype(BF16)


def to_slots(slots, scale, place, gate, values):
    experts = lax.axis_size("expert") // SPLIT
    width = values.shape[1]
    return pl.pallas_call(
        functools.partial(place_kernel, slots, scale),
        out_shape=(
            jax.ShapeDtypeStruct((slots, width), BF16),
            jax.ShapeDtypeStruct(((experts - 1) * slots, width), BF16),
        ),
        in_specs=[VMEM] * 3,
        out_specs=(VMEM, VMEM),
        compiler_params=params(6),
        cost_estimate=cost(values.size, values.size),
        name="rows_to_slots",
    )(place, gate, values)


def home_kernel(slots, place, gate, kept, got, back, token_grad, gate_grad):
    width = token_grad.shape[1]
    near = kept[...].astype(F32) + got[...].astype(F32)
    total = jnp.zeros(token_grad.shape, F32)
    gates = jnp.zeros(gate_grad.shape, F32)
    for first, rows in ((0, near), (slots, back[...].astype(F32))):
        picks = chosen(place[...], first, rows.shape[0])
        total += lax.dot_general(
            picks.astype(F32).astype(BF16),
            rows[:, :width].astype(BF16),
            (((0,), (0,)), ((), ())),
            preferred_element_type=F32,
        )
        column = rows[:, width : width + 1]
        gates += jnp.sum(jnp.where(picks, column, 0.0), axis=0, keepdims=True)
    token_grad[...] = total.astype(BF16)
    gate_grad[...] = jnp.where(place[...] < 0, 0.0, gates / gate[...])


def to_tokens(slots, place, gate, kept, got, back):
    count, width = place.shape[1], kept.shape[1] - LANES
    return pl.pallas_call(
        functools.partial(home_kernel, slots),
        out_shape=(
            jax.ShapeDtypeStruct((count, width), BF16),
            jax.ShapeDtypeStruct((1, count), F32),
        ),
        in_specs=[VMEM] * 5,
        out_specs=(VMEM, VMEM),
        compiler_params=params(12),
        name="slots_to_tokens",
    )(place, gate, kept, got, back)


def activation_kernel(order, hidden, activated, slope):
    rows = hidden.shape[1]
    step = 16 if rows % 16 == 0 else rows

    def chunk(i, carry):
        at = pl.ds(i * step, step) if rows > step else slice(None)
        h = hidden[0, at, :].astype(F32)
        cdf = 0.5 * (1.0 + lax.erf(h * 0.7071067811865476))
        density = jnp.exp(-0.5 * h * h) * 0.3989422804014327
        activated[0, at, :] = (h * cdf).astype(BF16)
        slope[0, at, :] = cdf + h * density
        return carry

    lax.fori_loop(0, rows // step, chunk, 0)


def activation(by_source, order):
    _, slots, units = by_source.shape
    block = (1, slots, units)
    shape = (order.shape[0], slots, units)
    size = order.shape[0] * slots * units
    act, slope = pl.pallas_call(
        activation_kernel,
        grid_spec=pltpu.PrefetchScalarGridSpec(
            num_scalar_prefetch=1,
            grid=(order.shape[0],),
            in_specs=[pl.BlockSpec(block, lambda i, order: (order[i], 0, 0))],
            out_specs=[pl.BlockSpec(block, lambda i, order: (i, 0, 0))] * 2,
        ),
        out_shape=(jax.ShapeDtypeStruct(shape, BF16), jax.ShapeDtypeStruct(shape, F32)),
        compiler_params=params(6),
        cost_estimate=cost(size, size),
        name="activation",
    )(order, by_source)
    return act.reshape(-1, units), slope.reshape(-1, units)


def stack_kernel(*refs):
    out, first = refs[-1], 0
    for ref in refs[:-1]:
        count = ref.shape[0]
        out[first : first + count, :] = ref[...]
        first += count


def join(*pieces):
    if any(x.shape[0] % 16 for x in pieces):
        return jnp.concatenate(pieces)
    rows, width = sum(x.shape[0] for x in pieces), pieces[0].shape[1]
    return pl.pallas_call(
        stack_kernel,
        out_shape=jax.ShapeDtypeStruct((rows, width), BF16),
        in_specs=[VMEM] * len(pieces),
        out_specs=VMEM,
        compiler_params=params(2 + rows * width * 4 // 1000000),
        cost_estimate=cost(0, rows * width),
        name="stack_rows",
    )(*pieces)


def add(a, b):
    return (a.astype(F32) + b.astype(F32)).astype(BF16)


def halves(x):
    half = x.shape[0] // 2
    return x[:half], x[half:]


def add_halves(kept, got):
    kept, got = halves(kept), halves(got)
    return add(kept[0], got[0]), add(kept[1], got[1])


def split_slots(rows, experts):
    rows = rows.reshape(experts - 1, 2, -1, rows.shape[1])
    return [rows[:, i].reshape(-1, rows.shape[3]) for i in range(2)]


def join_slots(a, b, experts):
    a, b = [x.reshape(experts - 1, -1, x.shape[1]) for x in (a, b)]
    return jnp.concatenate([a, b], axis=1).reshape(-1, a.shape[2])


def product(a, b, dims):
    return lax.dot_general(a, b, (dims, ((), ())), preferred_element_type=F32)


def hidden_part(grads, w_out, act, slope):
    grad_act = product(grads, w_out, ((1,), (1,)))
    gates = jnp.sum(grad_act * act.astype(F32), axis=1, keepdims=True)
    return (grad_act * slope).astype(BF16), gates


def slot_part(hidden_grad, gates, w_in):
    part = product(hidden_grad, w_in, ((1,), (1,))).astype(BF16)
    gates = jnp.broadcast_to(gates, (gates.shape[0], LANES)).astype(BF16)
    return halves(jnp.concatenate([part, gates], axis=1))


def body(tokens, out_grad, gate, expert_id, dropped, slot, saved_hidden, w_in, w_out):
    devices = lax.axis_size("expert")
    experts = devices // SPLIT
    slots = saved_hidden.shape[0] // devices
    units = saved_hidden.shape[1]
    me = lax.axis_index("expert")
    place, gate = pack_routing(expert_id, dropped, slot, gate, slots)
    near_order, far_order = sources_met(me, experts)
    by_source = saved_hidden.reshape(devices, slots, units)

    near_grad, far_grad = to_slots(slots, True, place, gate, out_grad)
    near_row, far_row = to_slots(slots, False, place, gate, tokens)

    far_grad = cross(far_grad, 1)
    got = meet(near_grad, 0)
    near_act, near_slope = activation(by_source, near_order)
    far_act, far_slope = activation(by_source, far_order)
    near_two = join(near_grad, after(got, near_act, far_act, near_row))
    got = meet(near_two, 1)
    row_got = meet(after(near_row, near_two), 0)
    far_grad = after(far_grad, near_two)
    far_got = meet(far_grad, 0)
    near_row2 = join(near_row, after(row_got, far_grad))
    far_two = join(far_grad, after(far_got, near_row2))
    far_got = meet(far_two, 1)
    near_four = join(near_two, after(got, far_two))
    got = meet(near_four, 2)

    near_grads = join(near_four, got)
    near_hg, near_gates = hidden_part(near_grads, w_out, near_act, near_slope)
    near_kept, near_sent = slot_part(near_hg, near_gates, w_in)
    near_got = meet(near_sent, 2)
    far_four = join(far_two, after(far_got, near_sent))
    far_got = meet(far_four, 2)
    far_row_a, far_row_b = split_slots(after(far_row, far_four), experts)
    far_row_a = cross(far_row_a, 1)
    row_got = meet(after(near_row2, far_four), 1)
    far_grads = join(far_four, far_got)
    near_kept, near_sent = add_halves(near_kept, after(near_got, far_grads))
    near_got = meet(near_sent, 1)
    far_grads = after(far_grads, near_sent)

    far_hg, far_gates = hidden_part(far_grads, w_out, far_act, far_slope)
    far_kept, far_sent = slot_part(far_hg, far_gates, w_in)
    far_got = meet(far_sent, 2)
    near_row4 = join(near_row2, after(row_got, far_sent))
    row_got = meet(near_row4, 2)
    far_row_a = after(far_row_a, near_row4)
    far_row_b = cross(after(far_row_b, far_row_a), 1)
    far_kept, far_sent = add_halves(far_kept, after(far_got, far_row_a))
    far_got = meet(far_sent, 1)
    near_kept, near_sent = add_halves(near_kept, after(near_got, far_sent))
    near_got = meet(near_sent, 0)
    acts = join(after(near_act, near_sent), far_act)
    w_out_grad = product(acts, join(near_grads, far_grads), ((0,), (0,))).astype(BF16)
    far_row = join_slots(far_row_a, after(far_row_b, w_out_grad), experts)
    far_row_got = meet(far_row, 0)
    far_kept, far_sent = add_halves(far_kept, after(far_got, far_row))
    far_got = meet(far_sent, 0)
    far_row2 = join(far_row, after(far_row_got, far_sent))
    far_row_got = meet(far_row2, 1)
    far_sum = add(far_kept, after(far_got, far_row2))
    back = cross(far_sum, -1)
    far_row4 = join(far_row2, after(far_row_got, far_sum))
    rows = join(near_row4, row_got, far_row4, meet(far_row4, 2))
    w_in_grad = product(rows, join(near_hg, far_hg), ((0,), (0,))).astype(BF16)
    near_got, back = after(near_got, w_in_grad), after(back, w_in_grad)
    token_grad, gate_grad = to_tokens(slots, place, gate, near_kept, near_got, back)
    return (token_grad, gate_grad.reshape(-1), w_in_grad, w_out_grad)


def solution(mesh):
    in_specs = (
        P(("parts", "expert"), None),
        P(("parts", "expert"), None),
        P(("parts", "expert")),
        P(("parts", "expert")),
        P(("parts", "expert")),
        P(("parts", "expert")),
        P("parts", "expert"),
        P(None, "expert"),
        P("expert", None),
    )
    out_specs = (
        P(("parts", "expert"), None),
        P(("parts", "expert")),
        P("parts", "expert"),
        P(("parts", "expert"), None),
    )
    return jax.shard_map(body, mesh=mesh, in_specs=in_specs, out_specs=out_specs, check_vma=False)
```

```python
import functools

import jax
import jax.numpy as jnp
from jax import lax
from jax.experimental import pallas as pl
from jax.experimental.pallas import tpu as pltpu
from jax.sharding import PartitionSpec as P

SPLIT = 8
CORE, LOW, HIGH = 1, 2, 4
LANES, TILE = 128, 256
VMEM = pl.BlockSpec(memory_space=pltpu.VMEM)
F32, BF16 = jnp.float32, jnp.bfloat16


def params(mib):
    return pltpu.CompilerParams(vmem_limit_bytes=mib * 1024 * 1024)


def cost(flops, moved, exps=0):
    return pl.CostEstimate(flops=flops, bytes_accessed=moved, transcendentals=exps)


def bits(core):
    return (HIGH, LOW, CORE) if core == 0 else (LOW, HIGH, CORE)


def meet(rows, step):
    devices = lax.axis_size("expert")
    return lax.ppermute(rows, "expert", [(i, i ^ bits(i % 2)[step]) for i in range(devices)])


def shift(rows, by):
    devices = lax.axis_size("expert")
    pairs = [(i, (i + by * SPLIT) % devices) for i in range(devices)]
    return lax.ppermute(rows, "expert", pairs)


def cross(rows, sign):
    experts = lax.axis_size("expert") // SPLIT
    if experts == 2:
        return shift(rows, sign)
    slots = rows.shape[0] // (experts - 1)
    return jnp.concatenate(
        [shift(rows[(s - 1) * slots : s * slots], sign * s) for s in range(1, experts)]
    )


def after(value, *earlier):
    return lax.optimization_barrier((value, *earlier))[0]


def sources_met(me, experts):
    block = jnp.arange(SPLIT * (experts - 1), dtype=jnp.int32)

    def place(i):
        first = jnp.where(((me ^ (i >> 2)) & 1) == 1, LOW, HIGH)
        second = (LOW + HIGH) - first
        mask = (i & 1) * first + ((i >> 1) & 1) * second + (i >> 2) * CORE
        return (me & (SPLIT - 1)) ^ mask

    my_expert = me >> 3
    from_expert = my_expert - 1 - block % (experts - 1)
    from_expert = jnp.where(from_expert < 0, from_expert + experts, from_expert)
    near = my_expert * SPLIT + place(block[:SPLIT])
    return jnp.concatenate([near, from_expert * SPLIT + place(block // (experts - 1))])


def pack_routing(expert_id, dropped, slot, gate, slots):
    devices = lax.axis_size("expert")
    ahead = expert_id - (lax.axis_index("expert") >> 3)
    ahead = jnp.where(ahead < 0, ahead + devices // SPLIT, ahead)
    place = jnp.where(dropped == 1, -1, ahead * slots + slot)
    return place.reshape(1, -1), gate.reshape(1, -1)


def chosen(place, first, count):
    rows = lax.broadcasted_iota(jnp.int32, (count, place.shape[1]), 0) + first
    return rows == place


def place_kernel(slots, scale, place, gate, values, near, far):
    rows = values[...]
    if scale:
        count = rows.shape[0]
        across = lax.broadcasted_iota(jnp.int32, (count, count), 1)
        down = lax.broadcasted_iota(jnp.int32, (count, count), 0)
        gates = jnp.where(across == down, gate[...], 0.0)
        column = jnp.sum(gates, axis=1, keepdims=True)
        rows = (column * rows.astype(F32)).astype(BF16)
    for first, out in ((0, near), (slots, far)):
        onehot = chosen(place[...], first, out.shape[0]).astype(F32).astype(BF16)
        out[...] = jnp.dot(onehot, rows, preferred_element_type=F32).astype(BF16)


def to_slots(slots, scale, place, gate, values):
    experts = lax.axis_size("expert") // SPLIT
    width = values.shape[1]
    return pl.pallas_call(
        functools.partial(place_kernel, slots, scale),
        out_shape=(
            jax.ShapeDtypeStruct((slots, width), BF16),
            jax.ShapeDtypeStruct(((experts - 1) * slots, width), BF16),
        ),
        in_specs=[VMEM] * 3,
        out_specs=(VMEM, VMEM),
        compiler_params=params(6),
        cost_estimate=cost(values.size, values.size),
        name="rows_to_slots",
    )(place, gate, values)


def home_kernel(slots, place, gate, kept, got, back, token_grad, gate_grad):
    width = token_grad.shape[1]
    near = kept[...].astype(F32) + got[...].astype(F32)
    total = jnp.zeros(token_grad.shape, F32)
    gates = jnp.zeros(gate_grad.shape, F32)
    for first, rows in ((0, near), (slots, back[...].astype(F32))):
        picks = chosen(place[...], first, rows.shape[0])
        total += lax.dot_general(
            picks.astype(F32).astype(BF16),
            rows[:, :width].astype(BF16),
            (((0,), (0,)), ((), ())),
            preferred_element_type=F32,
        )
        column = rows[:, width : width + 1]
        gates += jnp.sum(jnp.where(picks, column, 0.0), axis=0, keepdims=True)
    token_grad[...] = total.astype(BF16)
    gate_grad[...] = jnp.where(place[...] < 0, 0.0, gates / gate[...])


def to_tokens(slots, place, gate, kept, got, back):
    count, width = place.shape[1], kept.shape[1] - LANES
    return pl.pallas_call(
        functools.partial(home_kernel, slots),
        out_shape=(
            jax.ShapeDtypeStruct((count, width), BF16),
            jax.ShapeDtypeStruct((1, count), F32),
        ),
        in_specs=[VMEM] * 5,
        out_specs=(VMEM, VMEM),
        compiler_params=params(12),
        name="slots_to_tokens",
    )(place, gate, kept, got, back)


def activation_kernel(order, hidden, activated, slope):
    rows = hidden.shape[1]
    step = 16 if rows % 16 == 0 else rows

    def chunk(i, carry):
        at = pl.ds(i * step, step) if rows > step else slice(None)
        h = hidden[0, at, :].astype(F32)
        cdf = 0.5 * (1.0 + lax.erf(h * 0.7071067811865476))
        density = jnp.exp(-0.5 * h * h) * 0.3989422804014327
        activated[0, at, :] = (h * cdf).astype(BF16)
        slope[0, at, :] = (cdf + h * density).astype(BF16)
        return carry

    lax.fori_loop(0, rows // step, chunk, 0)


def activation(by_source, order):
    _, slots, units = by_source.shape
    block = (1, slots, units)
    shape = (order.shape[0], slots, units)
    act, slope = pl.pallas_call(
        activation_kernel,
        grid_spec=pltpu.PrefetchScalarGridSpec(
            num_scalar_prefetch=1,
            grid=(order.shape[0],),
            in_specs=[pl.BlockSpec(block, lambda i, order: (order[i], 0, 0))],
            out_specs=[pl.BlockSpec(block, lambda i, order: (i, 0, 0))] * 2,
        ),
        out_shape=(jax.ShapeDtypeStruct(shape, BF16),) * 2,
        compiler_params=params(6),
        cost_estimate=cost(0, 0),
        name="activation",
    )(order, by_source)
    return act.reshape(-1, units), slope.reshape(-1, units)


def stack_kernel(*refs):
    out, first = refs[-1], 0
    for ref in refs[:-1]:
        count = ref.shape[0]
        out[first : first + count, :] = ref[...]
        first += count


def join(*pieces):
    if any(x.shape[0] % 16 for x in pieces):
        return jnp.concatenate(pieces)
    rows, width = sum(x.shape[0] for x in pieces), pieces[0].shape[1]
    return pl.pallas_call(
        stack_kernel,
        out_shape=jax.ShapeDtypeStruct((rows, width), BF16),
        in_specs=[VMEM] * len(pieces),
        out_specs=VMEM,
        compiler_params=params(2 + rows * width * 4 // 1000000),
        cost_estimate=cost(0, rows * width),
        name="stack_rows",
    )(*pieces)


def add(a, b):
    return (a.astype(F32) + b.astype(F32)).astype(BF16)


def halves(x):
    half = x.shape[0] // 2
    return x[:half], x[half:]


def add_halves(kept, got):
    kept, got = halves(kept), halves(got)
    return add(kept[0], got[0]), add(kept[1], got[1])


def split_slots(rows, experts):
    rows = rows.reshape(experts - 1, 2, -1, rows.shape[1])
    return [rows[:, i].reshape(-1, rows.shape[3]) for i in range(2)]


def join_slots(a, b, experts):
    a, b = [x.reshape(experts - 1, -1, x.shape[1]) for x in (a, b)]
    return jnp.concatenate([a, b], axis=1).reshape(-1, a.shape[2])


def product(a, b, dims):
    return lax.dot_general(a, b, (dims, ((), ())), preferred_element_type=F32)


def slot_grad_kernel(grads, w_out, w_in, act, slope, hidden_grad, kept, sent):
    rows, units = act.shape
    width, half = grads.shape[1], rows // 2
    gates = jnp.zeros((rows, 1), F32)
    for j in range(units // TILE):
        at = slice(j * TILE, (j + 1) * TILE)
        grad_act = product(grads[...], w_out[at, :], ((1,), (1,)))
        hidden_grad[:, at] = (grad_act * slope[:, at].astype(F32)).astype(BF16)
        gates += jnp.sum(grad_act * act[:, at].astype(F32), axis=1, keepdims=True)
    gates = jnp.broadcast_to(gates, (rows, LANES)).astype(BF16)
    kept[:, width:] = gates[:half]
    sent[:, width:] = gates[half:]
    for j in range(width // TILE):
        at = slice(j * TILE, (j + 1) * TILE)
        part = product(hidden_grad[...], w_in[at, :], ((1,), (1,))).astype(BF16)
        kept[:, at] = part[:half]
        sent[:, at] = part[half:]


def slot_grads(grads, w_out, w_in, act, slope):
    rows, units = act.shape
    wide = w_in.shape[0] + LANES
    return pl.pallas_call(
        slot_grad_kernel,
        out_shape=(
            jax.ShapeDtypeStruct((rows, units), BF16),
            jax.ShapeDtypeStruct((rows // 2, wide), BF16),
            jax.ShapeDtypeStruct((rows // 2, wide), BF16),
        ),
        in_specs=[VMEM] * 5,
        out_specs=(VMEM, VMEM, VMEM),
        compiler_params=params(16 + rows // 64),
        cost_estimate=cost(0, 0),
        name="slot_grads",
    )(grads, w_out, w_in, act, slope)


def body(tokens, out_grad, gate, expert_id, dropped, slot, saved_hidden, w_in, w_out):
    devices = lax.axis_size("expert")
    experts = devices // SPLIT
    slots = saved_hidden.shape[0] // devices
    units = saved_hidden.shape[1]
    me = lax.axis_index("expert")
    place, gate = pack_routing(expert_id, dropped, slot, gate, slots)
    order = sources_met(me, experts)
    by_source = saved_hidden.reshape(devices, slots, units)
    near_count = SPLIT * slots

    near_grad, far_grad = to_slots(slots, True, place, gate, out_grad)
    near_row, far_row = to_slots(slots, False, place, gate, tokens)

    far_grad = cross(far_grad, 1)
    got = meet(near_grad, 0)
    near_two = join(near_grad, after(got, near_row))
    got = meet(near_two, 1)
    row_got = meet(after(near_row, near_two), 0)
    act, slope = activation(by_source, after(order, near_two))
    far_grad = after(far_grad, act)
    far_got = meet(far_grad, 0)
    near_row2 = join(near_row, after(row_got, far_grad))
    far_two = join(far_grad, after(far_got, near_row2))
    far_got = meet(far_two, 1)
    near_four = join(near_two, after(got, far_two))
    got = meet(near_four, 2)

    far_row_a, far_row_b = split_slots(after(far_row, far_two), experts)
    far_row_a = cross(far_row_a, 1)
    near_grads = join(near_four, got)
    near_hg, near_kept, near_sent = slot_grads(
        near_grads, w_out, w_in, act[:near_count], slope[:near_count]
    )
    near_got = meet(near_sent, 2)
    far_row_a = after(far_row_a, near_sent)
    far_four = join(far_two, after(far_got, far_row_a))
    far_got = meet(far_four, 2)
    far_row_b = cross(after(far_row_b, far_four), 1)
    row_got = meet(after(near_row2, far_four), 1)
    far_grads = join(far_four, far_got)

    far_hg, far_kept, far_sent = slot_grads(
        far_grads, w_out, w_in, act[near_count:], slope[near_count:]
    )
    far_row = join_slots(far_row_a, after(far_row_b, far_sent), experts)
    near_row4 = join(near_row2, after(row_got, far_row))
    near_kept, near_sent = add_halves(near_kept, after(near_got, near_row4))
    far_got = meet(after(far_sent, near_sent), 2)
    far_row_got = meet(far_row, 0)
    row_got = meet(near_row4, 2)
    near_got = meet(near_sent, 1)
    far_kept, far_sent = add_halves(far_kept, far_got)
    far_got = meet(far_sent, 1)
    w_out_grad = product(
        after(act, far_sent), join(near_grads, far_grads), ((0,), (0,))
    ).astype(BF16)
    far_row2 = join(far_row, after(far_row_got, w_out_grad))
    far_row_got = meet(far_row2, 1)
    far_kept, far_sent = add_halves(far_kept, after(far_got, far_row2))
    far_got = meet(far_sent, 0)
    near_kept, near_sent = add_halves(near_kept, after(near_got, far_sent))
    near_got = meet(near_sent, 0)
    far_sum = add(far_kept, after(far_got, near_sent))
    back = cross(far_sum, -1)
    far_row4 = join(far_row2, after(far_row_got, far_sum))
    rows = join(near_row4, row_got, far_row4, meet(far_row4, 2))
    w_in_grad = product(rows, join(near_hg, far_hg), ((0,), (0,))).astype(BF16)
    near_got, back = after(near_got, w_in_grad), after(back, w_in_grad)
    token_grad, gate_grad = to_tokens(slots, place, gate, near_kept, near_got, back)
    return (token_grad, gate_grad.reshape(-1), w_in_grad, w_out_grad)


def solution(mesh):
    in_specs = (
        P(("parts", "expert"), None),
        P(("parts", "expert"), None),
        P(("parts", "expert")),
        P(("parts", "expert")),
        P(("parts", "expert")),
        P(("parts", "expert")),
        P("parts", "expert"),
        P(None, "expert"),
        P("expert", None),
    )
    out_specs = (
        P(("parts", "expert"), None),
        P(("parts", "expert")),
        P("parts", "expert"),
        P(("parts", "expert"), None),
    )
    return jax.shard_map(body, mesh=mesh, in_specs=in_specs, out_specs=out_specs, check_vma=False)
```

```python
import functools

import jax
import jax.numpy as jnp
from jax import lax
from jax.experimental import pallas as pl
from jax.experimental.pallas import tpu as pltpu
from jax.sharding import PartitionSpec as P

SPLIT = 8
CORE, LOW, HIGH = 1, 2, 4
LANES, TILE = 128, 256
LONG = 20_000_000_000
VMEM = pl.BlockSpec(memory_space=pltpu.VMEM)
F32, BF16 = jnp.float32, jnp.bfloat16


def params(mib):
    return pltpu.CompilerParams(vmem_limit_bytes=mib * 1024 * 1024)


def cost(flops, moved, exps=0):
    return pl.CostEstimate(flops=flops, bytes_accessed=moved, transcendentals=exps)


def bits(core):
    return (HIGH, LOW, CORE) if core == 0 else (LOW, HIGH, CORE)


def meet(rows, step):
    devices = lax.axis_size("expert")
    return lax.ppermute(rows, "expert", [(i, i ^ bits(i % 2)[step]) for i in range(devices)])


def shift(rows, by):
    devices = lax.axis_size("expert")
    pairs = [(i, (i + by * SPLIT) % devices) for i in range(devices)]
    return lax.ppermute(rows, "expert", pairs)


def cross(rows, sign):
    experts = lax.axis_size("expert") // SPLIT
    if experts == 2:
        return shift(rows, sign)
    slots = rows.shape[0] // (experts - 1)
    return jnp.concatenate(
        [shift(rows[(s - 1) * slots : s * slots], sign * s) for s in range(1, experts)]
    )


def after(value, *earlier):
    return lax.optimization_barrier((value, *earlier))[0]


def sources_met(me, experts):
    block = jnp.arange(SPLIT * (experts - 1), dtype=jnp.int32)

    def place(i):
        first = jnp.where(((me ^ (i >> 2)) & 1) == 1, LOW, HIGH)
        second = (LOW + HIGH) - first
        mask = (i & 1) * first + ((i >> 1) & 1) * second + (i >> 2) * CORE
        return (me & (SPLIT - 1)) ^ mask

    my_expert = me >> 3
    from_expert = my_expert - 1 - block % (experts - 1)
    from_expert = jnp.where(from_expert < 0, from_expert + experts, from_expert)
    near = my_expert * SPLIT + place(block[:SPLIT])
    return jnp.concatenate([near, from_expert * SPLIT + place(block // (experts - 1))])


def pack_routing(expert_id, dropped, slot, gate, slots):
    devices = lax.axis_size("expert")
    ahead = expert_id - (lax.axis_index("expert") >> 3)
    ahead = jnp.where(ahead < 0, ahead + devices // SPLIT, ahead)
    place = jnp.where(dropped == 1, -1, ahead * slots + slot)
    return place.reshape(1, -1), gate.reshape(1, -1)


def chosen(place, first, count):
    rows = lax.broadcasted_iota(jnp.int32, (count, place.shape[1]), 0) + first
    return rows == place


def place_kernel(slots, scale, place, gate, values, near, far):
    rows = values[...]
    if scale:
        count = rows.shape[0]
        across = lax.broadcasted_iota(jnp.int32, (count, count), 1)
        down = lax.broadcasted_iota(jnp.int32, (count, count), 0)
        gates = jnp.where(across == down, gate[...], 0.0)
        column = jnp.sum(gates, axis=1, keepdims=True)
        rows = (column * rows.astype(F32)).astype(BF16)
    for first, out in ((0, near), (slots, far)):
        onehot = chosen(place[...], first, out.shape[0]).astype(F32).astype(BF16)
        out[...] = jnp.dot(onehot, rows, preferred_element_type=F32).astype(BF16)


def to_slots(slots, scale, place, gate, values):
    experts = lax.axis_size("expert") // SPLIT
    width = values.shape[1]
    return pl.pallas_call(
        functools.partial(place_kernel, slots, scale),
        out_shape=(
            jax.ShapeDtypeStruct((slots, width), BF16),
            jax.ShapeDtypeStruct(((experts - 1) * slots, width), BF16),
        ),
        in_specs=[VMEM] * 3,
        out_specs=(VMEM, VMEM),
        compiler_params=params(6),
        cost_estimate=cost(values.size, values.size),
        name="rows_to_slots",
    )(place, gate, values)


def home_kernel(slots, place, gate, kept, got, back, token_grad, gate_grad):
    width = token_grad.shape[1]
    near = kept[...].astype(F32) + got[...].astype(F32)
    total = jnp.zeros(token_grad.shape, F32)
    gates = jnp.zeros(gate_grad.shape, F32)
    for first, rows in ((0, near), (slots, back[...].astype(F32))):
        picks = chosen(place[...], first, rows.shape[0])
        total += lax.dot_general(
            picks.astype(F32).astype(BF16),
            rows[:, :width].astype(BF16),
            (((0,), (0,)), ((), ())),
            preferred_element_type=F32,
        )
        column = rows[:, width : width + 1]
        gates += jnp.sum(jnp.where(picks, column, 0.0), axis=0, keepdims=True)
    token_grad[...] = total.astype(BF16)
    gate_grad[...] = jnp.where(place[...] < 0, 0.0, gates / gate[...])


def to_tokens(slots, place, gate, kept, got, back):
    count, width = place.shape[1], kept.shape[1] - LANES
    return pl.pallas_call(
        functools.partial(home_kernel, slots),
        out_shape=(
            jax.ShapeDtypeStruct((count, width), BF16),
            jax.ShapeDtypeStruct((1, count), F32),
        ),
        in_specs=[VMEM] * 5,
        out_specs=(VMEM, VMEM),
        compiler_params=params(12),
        name="slots_to_tokens",
    )(place, gate, kept, got, back)


def activation_kernel(order, hidden, activated, slope):
    rows = hidden.shape[1]
    step = 16 if rows % 16 == 0 else rows

    def chunk(i, carry):
        at = pl.ds(i * step, step) if rows > step else slice(None)
        h = hidden[0, at, :].astype(F32)
        cdf = 0.5 * (1.0 + lax.erf(h * 0.7071067811865476))
        density = jnp.exp(-0.5 * h * h) * 0.3989422804014327
        activated[0, at, :] = (h * cdf).astype(BF16)
        slope[0, at, :] = (cdf + h * density).astype(BF16)
        return carry

    lax.fori_loop(0, rows // step, chunk, 0)


def activation(by_source, order):
    _, slots, units = by_source.shape
    block = (1, slots, units)
    shape = (order.shape[0], slots, units)
    act, slope = pl.pallas_call(
        activation_kernel,
        grid_spec=pltpu.PrefetchScalarGridSpec(
            num_scalar_prefetch=1,
            grid=(order.shape[0],),
            in_specs=[pl.BlockSpec(block, lambda i, order: (order[i], 0, 0))],
            out_specs=[pl.BlockSpec(block, lambda i, order: (i, 0, 0))] * 2,
        ),
        out_shape=(jax.ShapeDtypeStruct(shape, BF16),) * 2,
        compiler_params=params(6),
        cost_estimate=cost(0, 0),
        name="activation",
    )(order, by_source)
    return act.reshape(-1, units), slope.reshape(-1, units)


def stack_kernel(*refs):
    out, first = refs[-1], 0
    for ref in refs[:-1]:
        count = ref.shape[0]
        out[first : first + count, :] = ref[...]
        first += count


def join(*pieces, long=False):
    if any(x.shape[0] % 16 for x in pieces):
        return jnp.concatenate(pieces)
    rows, width = sum(x.shape[0] for x in pieces), pieces[0].shape[1]
    return pl.pallas_call(
        stack_kernel,
        out_shape=jax.ShapeDtypeStruct((rows, width), BF16),
        in_specs=[VMEM] * len(pieces),
        out_specs=VMEM,
        compiler_params=params(2 + rows * width * 4 // 1000000),
        cost_estimate=cost(LONG if long else 0, rows * width),
        name="stack_rows",
    )(*pieces)


def add(a, b):
    return (a.astype(F32) + b.astype(F32)).astype(BF16)


def halves(x):
    half = x.shape[0] // 2
    return x[:half], x[half:]


def add_halves(kept, got):
    kept, got = halves(kept), halves(got)
    return add(kept[0], got[0]), add(kept[1], got[1])


def split_slots(rows, experts):
    rows = rows.reshape(experts - 1, -1, rows.shape[1])
    cut = rows.shape[1] - rows.shape[1] // 5
    return [x.reshape(-1, rows.shape[2]) for x in (rows[:, :cut], rows[:, cut:])]


def pause_kernel(rows, out):
    out[...] = rows[...]


def pause(rows):
    return pl.pallas_call(
        pause_kernel,
        out_shape=jax.ShapeDtypeStruct(rows.shape, rows.dtype),
        in_specs=[VMEM],
        out_specs=VMEM,
        compiler_params=params(4),
        cost_estimate=cost(LONG, 0),
        name="pause",
    )(rows)


def join_slots(a, b, experts):
    a, b = [x.reshape(experts - 1, -1, x.shape[1]) for x in (a, b)]
    return jnp.concatenate([a, b], axis=1).reshape(-1, a.shape[2])


def product(a, b, dims):
    return lax.dot_general(a, b, (dims, ((), ())), preferred_element_type=F32)


def slot_grad_kernel(grads, w_out, w_in, act, slope, hidden_grad, kept, sent):
    rows, units = act.shape
    width, half = grads.shape[1], rows // 2
    gates = jnp.zeros((rows, 1), F32)
    for j in range(units // TILE):
        at = slice(j * TILE, (j + 1) * TILE)
        grad_act = product(grads[...], w_out[at, :], ((1,), (1,)))
        hidden_grad[:, at] = (grad_act * slope[:, at].astype(F32)).astype(BF16)
        gates += jnp.sum(grad_act * act[:, at].astype(F32), axis=1, keepdims=True)
    gates = jnp.broadcast_to(gates, (rows, LANES)).astype(BF16)
    kept[:, width:] = gates[:half]
    sent[:, width:] = gates[half:]
    for j in range(width // TILE):
        at = slice(j * TILE, (j + 1) * TILE)
        part = product(hidden_grad[...], w_in[at, :], ((1,), (1,))).astype(BF16)
        kept[:, at] = part[:half]
        sent[:, at] = part[half:]


def slot_grads(grads, w_out, w_in, act, slope):
    rows, units = act.shape
    wide = w_in.shape[0] + LANES
    return pl.pallas_call(
        slot_grad_kernel,
        out_shape=(
            jax.ShapeDtypeStruct((rows, units), BF16),
            jax.ShapeDtypeStruct((rows // 2, wide), BF16),
            jax.ShapeDtypeStruct((rows // 2, wide), BF16),
        ),
        in_specs=[VMEM] * 5,
        out_specs=(VMEM, VMEM, VMEM),
        compiler_params=params(16 + rows // 64),
        cost_estimate=cost(0, 0),
        name="slot_grads",
    )(grads, w_out, w_in, act, slope)


def body(tokens, out_grad, gate, expert_id, dropped, slot, saved_hidden, w_in, w_out):
    devices = lax.axis_size("expert")
    experts = devices // SPLIT
    slots = saved_hidden.shape[0] // devices
    units = saved_hidden.shape[1]
    me = lax.axis_index("expert")
    place, gate = pack_routing(expert_id, dropped, slot, gate, slots)
    order = sources_met(me, experts)
    by_source = saved_hidden.reshape(devices, slots, units)
    near_count = SPLIT * slots

    near_grad, far_grad = to_slots(slots, True, place, gate, out_grad)
    near_row, far_row = to_slots(slots, False, place, gate, tokens)

    far_grad = cross(far_grad, 1)
    got = meet(near_grad, 0)
    near_two = join(near_grad, after(got, near_row))
    got = meet(near_two, 1)
    act, slope = activation(by_source, after(order, near_two))
    far_grad = pause(after(far_grad, act))
    far_got = meet(far_grad, 0)
    near_four = join(near_two, after(got, far_grad))
    got = meet(near_four, 2)
    far_two = join(far_grad, after(far_got, near_four), long=True)
    far_got = meet(far_two, 1)

    far_row_a, far_row_b = split_slots(after(far_row, far_two), experts)
    far_row_a = cross(far_row_a, 1)
    near_grads = join(near_four, after(got, far_two))
    near_hg, near_kept, near_sent = slot_grads(
        near_grads, w_out, w_in, act[:near_count], slope[:near_count]
    )
    near_got = meet(near_sent, 2)
    far_row_a = after(far_row_a, near_sent)
    far_four = join(far_two, after(far_got, far_row_a), long=True)
    far_got = meet(far_four, 2)
    far_row_b = cross(after(far_row_b, far_four), 1)
    row_got = meet(after(near_row, far_four), 0)
    near_kept, near_sent = add_halves(near_kept, after(near_got, far_four))
    near_got = meet(near_sent, 1)
    far_grads = join(far_four, after(far_got, near_sent))

    far_hg, far_kept, far_sent = slot_grads(
        far_grads, w_out, w_in, act[near_count:], slope[near_count:]
    )
    far_row = join_slots(far_row_a, after(far_row_b, far_sent), experts)
    near_row2 = join(near_row, after(row_got, far_sent))
    far_kept, far_on = halves(far_kept)
    far_sent = halves(after(far_sent, far_row, near_row2))
    far_got, on_got = [meet(x, 2) for x in far_sent]
    row_got = meet(near_row2, 1)
    far_row_got = meet(far_row, 0)
    near_kept, near_sent = add_halves(near_kept, after(near_got, far_sent[1]))
    near_got = meet(near_sent, 0)
    far_sent = add(far_on, after(on_got, near_sent))
    on_got = meet(far_sent, 1)
    far_kept = add(far_kept, after(far_got, far_sent))
    w_out_grad = product(
        after(act, far_kept), join(near_grads, far_grads), ((0,), (0,))
    ).astype(BF16)
    far_row2 = join(far_row, after(far_row_got, w_out_grad))
    far_row_got = meet(far_row2, 1)
    near_row4 = join(near_row2, after(row_got, far_row2))
    row_got = meet(near_row4, 2)
    far_kept, far_sent = add_halves(far_kept, after(on_got, near_row4))
    far_got = meet(far_sent, 0)
    far_row4 = join(far_row2, after(far_row_got, far_sent))
    near_sent = far_row4
    far_sum = pause(add(far_kept, after(far_got, near_sent)))
    back = cross(far_sum, -1)
    rows = join(near_row4, row_got, far_row4, meet(far_row4, 2))
    w_in_grad = product(rows, join(near_hg, far_hg), ((0,), (0,))).astype(BF16)
    back = after(back, w_in_grad)
    near_got = after(near_got, back)
    token_grad, gate_grad = to_tokens(slots, place, gate, near_kept, near_got, back)
    return (token_grad, gate_grad.reshape(-1), w_in_grad, w_out_grad)


def solution(mesh):
    in_specs = (
        P(("parts", "expert"), None),
        P(("parts", "expert"), None),
        P(("parts", "expert")),
        P(("parts", "expert")),
        P(("parts", "expert")),
        P(("parts", "expert")),
        P("parts", "expert"),
        P(None, "expert"),
        P("expert", None),
    )
    out_specs = (
        P(("parts", "expert"), None),
        P(("parts", "expert")),
        P("parts", "expert"),
        P(("parts", "expert"), None),
    )
    return jax.shard_map(body, mesh=mesh, in_specs=in_specs, out_specs=out_specs, check_vma=False)
```

```python
import functools

import jax
import jax.numpy as jnp
from jax import lax
from jax.experimental import pallas as pl
from jax.experimental.pallas import tpu as pltpu
from jax.sharding import PartitionSpec as P

SPLIT = 8
CORE, LOW, HIGH = 1, 2, 4
LANES, TILE = 128, 256
LONG = 20_000_000_000
VMEM = pl.BlockSpec(memory_space=pltpu.VMEM)
F32, BF16 = jnp.float32, jnp.bfloat16


def params(mib):
    return pltpu.CompilerParams(vmem_limit_bytes=mib * 1024 * 1024)


def cost(flops, moved, exps=0):
    return pl.CostEstimate(flops=flops, bytes_accessed=moved, transcendentals=exps)


def bits(core):
    return (HIGH, LOW, CORE) if core == 0 else (LOW, HIGH, CORE)


def meet(rows, step):
    devices = lax.axis_size("expert")
    return lax.ppermute(rows, "expert", [(i, i ^ bits(i % 2)[step]) for i in range(devices)])


def shift(rows, by):
    devices = lax.axis_size("expert")
    pairs = [(i, (i + by * SPLIT) % devices) for i in range(devices)]
    return lax.ppermute(rows, "expert", pairs)


def cross(rows, sign):
    experts = lax.axis_size("expert") // SPLIT
    if experts == 2:
        return shift(rows, sign)
    slots = rows.shape[0] // (experts - 1)
    return jnp.concatenate(
        [shift(rows[(s - 1) * slots : s * slots], sign * s) for s in range(1, experts)]
    )


def after(value, *earlier):
    return lax.optimization_barrier((value, *earlier))[0]


def sources_met(me, experts):
    block = jnp.arange(SPLIT * (experts - 1), dtype=jnp.int32)

    def place(i):
        first = jnp.where(((me ^ (i >> 2)) & 1) == 1, LOW, HIGH)
        second = (LOW + HIGH) - first
        mask = (i & 1) * first + ((i >> 1) & 1) * second + (i >> 2) * CORE
        return (me & (SPLIT - 1)) ^ mask

    my_expert = me >> 3
    from_expert = my_expert - 1 - block % (experts - 1)
    from_expert = jnp.where(from_expert < 0, from_expert + experts, from_expert)
    near = my_expert * SPLIT + place(block[:SPLIT])
    return jnp.concatenate([near, from_expert * SPLIT + place(block // (experts - 1))])


def pack_routing(expert_id, dropped, slot, gate, slots):
    devices = lax.axis_size("expert")
    ahead = expert_id - (lax.axis_index("expert") >> 3)
    ahead = jnp.where(ahead < 0, ahead + devices // SPLIT, ahead)
    place = jnp.where(dropped == 1, -1, ahead * slots + slot)
    return place.reshape(1, -1), gate.reshape(1, -1)


def chosen(place, first, count):
    rows = lax.broadcasted_iota(jnp.int32, (count, place.shape[1]), 0) + first
    return rows == place


def place_kernel(slots, scale, place, gate, values, near, far):
    rows = values[...]
    if scale:
        count = rows.shape[0]
        across = lax.broadcasted_iota(jnp.int32, (count, count), 1)
        down = lax.broadcasted_iota(jnp.int32, (count, count), 0)
        gates = jnp.where(across == down, gate[...], 0.0)
        column = jnp.sum(gates, axis=1, keepdims=True)
        rows = (column * rows.astype(F32)).astype(BF16)
    for first, out in ((0, near), (slots, far)):
        onehot = chosen(place[...], first, out.shape[0]).astype(F32).astype(BF16)
        out[...] = jnp.dot(onehot, rows, preferred_element_type=F32).astype(BF16)


def to_slots(slots, scale, place, gate, values):
    experts = lax.axis_size("expert") // SPLIT
    width = values.shape[1]
    return pl.pallas_call(
        functools.partial(place_kernel, slots, scale),
        out_shape=(
            jax.ShapeDtypeStruct((slots, width), BF16),
            jax.ShapeDtypeStruct(((experts - 1) * slots, width), BF16),
        ),
        in_specs=[VMEM] * 3,
        out_specs=(VMEM, VMEM),
        compiler_params=params(6),
        cost_estimate=cost(values.size, values.size),
        name="rows_to_slots",
    )(place, gate, values)


def home_kernel(slots, place, gate, kept, got, back, token_grad, gate_grad):
    width = token_grad.shape[1]
    near = kept[...].astype(F32) + got[...].astype(F32)
    total = jnp.zeros(token_grad.shape, F32)
    gates = jnp.zeros(gate_grad.shape, F32)
    for first, rows in ((0, near), (slots, back[...].astype(F32))):
        picks = chosen(place[...], first, rows.shape[0])
        total += lax.dot_general(
            picks.astype(F32).astype(BF16),
            rows[:, :width].astype(BF16),
            (((0,), (0,)), ((), ())),
            preferred_element_type=F32,
        )
        column = rows[:, width : width + 1]
        gates += jnp.sum(jnp.where(picks, column, 0.0), axis=0, keepdims=True)
    token_grad[...] = total.astype(BF16)
    gate_grad[...] = jnp.where(place[...] < 0, 0.0, gates / gate[...])


def to_tokens(slots, place, gate, kept, got, back):
    count, width = place.shape[1], kept.shape[1] - LANES
    return pl.pallas_call(
        functools.partial(home_kernel, slots),
        out_shape=(
            jax.ShapeDtypeStruct((count, width), BF16),
            jax.ShapeDtypeStruct((1, count), F32),
        ),
        in_specs=[VMEM] * 5,
        out_specs=(VMEM, VMEM),
        compiler_params=params(12),
        name="slots_to_tokens",
    )(place, gate, kept, got, back)


def activation_kernel(order, hidden, activated, slope):
    rows = hidden.shape[1]
    step = 16 if rows % 16 == 0 else rows

    def chunk(i, carry):
        at = pl.ds(i * step, step) if rows > step else slice(None)
        h = hidden[0, at, :].astype(F32)
        cdf = 0.5 * (1.0 + lax.erf(h * 0.7071067811865476))
        density = jnp.exp(-0.5 * h * h) * 0.3989422804014327
        activated[0, at, :] = (h * cdf).astype(BF16)
        slope[0, at, :] = (cdf + h * density).astype(BF16)
        return carry

    lax.fori_loop(0, rows // step, chunk, 0)


def activation(by_source, order):
    _, slots, units = by_source.shape
    block = (1, slots, units)
    shape = (order.shape[0], slots, units)
    act, slope = pl.pallas_call(
        activation_kernel,
        grid_spec=pltpu.PrefetchScalarGridSpec(
            num_scalar_prefetch=1,
            grid=(order.shape[0],),
            in_specs=[pl.BlockSpec(block, lambda i, order: (order[i], 0, 0))],
            out_specs=[pl.BlockSpec(block, lambda i, order: (i, 0, 0))] * 2,
        ),
        out_shape=(jax.ShapeDtypeStruct(shape, BF16),) * 2,
        compiler_params=params(6),
        cost_estimate=cost(0, 0),
        name="activation",
    )(order, by_source)
    return act.reshape(-1, units), slope.reshape(-1, units)


def stack_kernel(*refs):
    out, first = refs[-1], 0
    for ref in refs[:-1]:
        count = ref.shape[0]
        out[first : first + count, :] = ref[...]
        first += count


def join(*pieces, long=False):
    if any(x.shape[0] % 16 for x in pieces):
        return jnp.concatenate(pieces)
    rows, width = sum(x.shape[0] for x in pieces), pieces[0].shape[1]
    return pl.pallas_call(
        stack_kernel,
        out_shape=jax.ShapeDtypeStruct((rows, width), BF16),
        in_specs=[VMEM] * len(pieces),
        out_specs=VMEM,
        compiler_params=params(2 + rows * width * 4 // 1000000),
        cost_estimate=cost(LONG if long else 0, rows * width),
        name="stack_rows",
    )(*pieces)


def add(a, b):
    return (a.astype(F32) + b.astype(F32)).astype(BF16)


def halves(x):
    half = x.shape[0] // 2
    return x[:half], x[half:]


def add_halves(kept, got):
    kept, got = halves(kept), halves(got)
    return add(kept[0], got[0]), add(kept[1], got[1])


def split_slots(rows, experts):
    rows = rows.reshape(experts - 1, -1, rows.shape[1])
    cut = rows.shape[1] - rows.shape[1] // 5
    return [x.reshape(-1, rows.shape[2]) for x in (rows[:, :cut], rows[:, cut:])]


def pause_kernel(rows, out):
    out[...] = rows[...]


def pause(rows):
    return pl.pallas_call(
        pause_kernel,
        out_shape=jax.ShapeDtypeStruct(rows.shape, rows.dtype),
        in_specs=[VMEM],
        out_specs=VMEM,
        compiler_params=params(4),
        cost_estimate=cost(LONG, 0),
        name="pause",
    )(rows)


def join_slots(a, b, experts):
    a, b = [x.reshape(experts - 1, -1, x.shape[1]) for x in (a, b)]
    return jnp.concatenate([a, b], axis=1).reshape(-1, a.shape[2])


def product(a, b, dims):
    return lax.dot_general(a, b, (dims, ((), ())), preferred_element_type=F32)


def slot_grad_kernel(grads, w_out, w_in, act, slope, hidden_grad, kept, sent):
    rows, units = act.shape
    width, half = grads.shape[1], rows // 2
    gates = jnp.zeros((rows, 1), F32)
    for j in range(units // TILE):
        at = slice(j * TILE, (j + 1) * TILE)
        grad_act = product(grads[...], w_out[at, :], ((1,), (1,)))
        hidden_grad[:, at] = (grad_act * slope[:, at].astype(F32)).astype(BF16)
        gates += jnp.sum(grad_act * act[:, at].astype(F32), axis=1, keepdims=True)
    gates = jnp.broadcast_to(gates, (rows, LANES)).astype(BF16)
    kept[:, width:] = gates[:half]
    sent[:, width:] = gates[half:]
    for j in range(width // TILE):
        at = slice(j * TILE, (j + 1) * TILE)
        part = product(hidden_grad[...], w_in[at, :], ((1,), (1,))).astype(BF16)
        kept[:, at] = part[:half]
        sent[:, at] = part[half:]


def slot_grads(grads, w_out, w_in, act, slope):
    rows, units = act.shape
    wide = w_in.shape[0] + LANES
    return pl.pallas_call(
        slot_grad_kernel,
        out_shape=(
            jax.ShapeDtypeStruct((rows, units), BF16),
            jax.ShapeDtypeStruct((rows // 2, wide), BF16),
            jax.ShapeDtypeStruct((rows // 2, wide), BF16),
        ),
        in_specs=[VMEM] * 5,
        out_specs=(VMEM, VMEM, VMEM),
        compiler_params=params(16 + rows // 64),
        cost_estimate=cost(0, 0),
        name="slot_grads",
    )(grads, w_out, w_in, act, slope)


def body(tokens, out_grad, gate, expert_id, dropped, slot, saved_hidden, w_in, w_out):
    devices = lax.axis_size("expert")
    experts = devices // SPLIT
    slots = saved_hidden.shape[0] // devices
    units = saved_hidden.shape[1]
    me = lax.axis_index("expert")
    place, gate = pack_routing(expert_id, dropped, slot, gate, slots)
    order = sources_met(me, experts)
    by_source = saved_hidden.reshape(devices, slots, units)
    near_count = SPLIT * slots

    near_grad, far_grad = to_slots(slots, True, place, gate, out_grad)
    near_row, far_row = to_slots(slots, False, place, gate, tokens)

    far_grad = cross(far_grad, 1)
    got = meet(near_grad, 0)
    row_got = meet(near_row, 0)
    act, slope = activation(by_source, order)
    near_two = join(near_grad, after(got, act))
    got = meet(near_two, 1)
    near_row2 = join(near_row, after(row_got, near_two))
    far_grad = pause(after(far_grad, near_row2))
    far_got = meet(far_grad, 0)
    near_four = join(near_two, after(got, far_grad))
    got = meet(near_four, 2)
    far_two = join(far_grad, after(far_got, near_four), long=True)
    far_got = meet(far_two, 1)

    far_row_a, far_row_b = split_slots(after(far_row, far_two), experts)
    far_row_a = cross(far_row_a, 1)
    near_grads = join(near_four, after(got, far_two))
    near_hg, near_kept, near_sent = slot_grads(
        near_grads, w_out, w_in, act[:near_count], slope[:near_count]
    )
    near_got = meet(near_sent, 2)
    far_row_a = after(far_row_a, near_sent)
    far_four = join(far_two, after(far_got, far_row_a), long=True)
    far_got = meet(far_four, 2)
    far_row_b = cross(after(far_row_b, far_four), 1)
    row_got = meet(after(near_row2, far_four), 1)
    near_kept, near_sent = add_halves(near_kept, after(near_got, far_four))
    near_got = meet(near_sent, 1)
    far_grads = join(far_four, after(far_got, near_sent))

    far_hg, far_kept, far_sent = slot_grads(
        far_grads, w_out, w_in, act[near_count:], slope[near_count:]
    )
    far_row = join_slots(far_row_a, after(far_row_b, far_sent), experts)
    far_kept, far_on = halves(far_kept)
    far_sent = halves(after(far_sent, far_row))
    on_got = meet(far_sent[1], 2)
    near_kept, near_sent = add_halves(near_kept, after(near_got, far_sent[1]))
    near_row4 = join(near_row2, after(row_got, near_sent), long=True)
    far_on = add(far_on, after(on_got, near_row4))
    on_got = meet(far_on, 1)
    far_row_got = meet(after(far_row, far_on), 0)
    far_got = meet(after(far_sent[0], far_on), 2)
    w_out_grad = product(
        after(act, far_on), join(near_grads, far_grads), ((0,), (0,))
    ).astype(BF16)
    far_kept = add(far_kept, after(far_got, w_out_grad))
    far_row2 = join(far_row, after(far_row_got, w_out_grad))
    far_row_got = meet(far_row2, 1)
    row_got = meet(near_row4, 2)
    near_got = meet(near_sent, 0)
    far_kept, far_sent = add_halves(far_kept, after(on_got, far_row2))
    far_got = meet(far_sent, 0)
    far_row4 = join(far_row2, after(far_row_got, far_sent))
    near_sent = far_row4
    far_sum = pause(add(far_kept, after(far_got, near_sent)))
    back = cross(far_sum, -1)
    rows = join(near_row4, row_got, far_row4, meet(far_row4, 2))
    w_in_grad = product(rows, join(near_hg, far_hg), ((0,), (0,))).astype(BF16)
    back = after(back, w_in_grad)
    near_got = after(near_got, back)
    token_grad, gate_grad = to_tokens(slots, place, gate, near_kept, near_got, back)
    return (token_grad, gate_grad.reshape(-1), w_in_grad, w_out_grad)


def solution(mesh):
    in_specs = (
        P(("parts", "expert"), None),
        P(("parts", "expert"), None),
        P(("parts", "expert")),
        P(("parts", "expert")),
        P(("parts", "expert")),
        P(("parts", "expert")),
        P("parts", "expert"),
        P(None, "expert"),
        P("expert", None),
    )
    out_specs = (
        P(("parts", "expert"), None),
        P(("parts", "expert")),
        P("parts", "expert"),
        P(("parts", "expert"), None),
    )
    return jax.shard_map(body, mesh=mesh, in_specs=in_specs, out_specs=out_specs, check_vma=False)
```

```python
import functools

import jax
import jax.numpy as jnp
from jax import lax
from jax.experimental import pallas as pl
from jax.experimental.pallas import tpu as pltpu
from jax.sharding import PartitionSpec as P

SPLIT = 8
CORE, LOW, HIGH = 1, 2, 4
LANES, TILE = 128, 256
LONG = 20_000_000_000
VMEM = pl.BlockSpec(memory_space=pltpu.VMEM)
F32, BF16 = jnp.float32, jnp.bfloat16


def params(mib):
    return pltpu.CompilerParams(vmem_limit_bytes=mib * 1024 * 1024)


def cost(flops, moved, exps=0):
    return pl.CostEstimate(flops=flops, bytes_accessed=moved, transcendentals=exps)


def bits(core):
    return (HIGH, LOW, CORE) if core == 0 else (LOW, HIGH, CORE)


def meet(rows, step):
    devices = lax.axis_size("expert")
    return lax.ppermute(rows, "expert", [(i, i ^ bits(i % 2)[step]) for i in range(devices)])


def shift(rows, by):
    devices = lax.axis_size("expert")
    pairs = [(i, (i + by * SPLIT) % devices) for i in range(devices)]
    return lax.ppermute(rows, "expert", pairs)


def cross(rows, sign):
    experts = lax.axis_size("expert") // SPLIT
    if experts == 2:
        return shift(rows, sign)
    slots = rows.shape[0] // (experts - 1)
    return jnp.concatenate(
        [shift(rows[(s - 1) * slots : s * slots], sign * s) for s in range(1, experts)]
    )


def after(value, *earlier):
    return lax.optimization_barrier((value, *earlier))[0]


def sources_met(me, experts):
    block = jnp.arange(SPLIT * (experts - 1), dtype=jnp.int32)

    def place(i):
        first = jnp.where(((me ^ (i >> 2)) & 1) == 1, LOW, HIGH)
        second = (LOW + HIGH) - first
        mask = (i & 1) * first + ((i >> 1) & 1) * second + (i >> 2) * CORE
        return (me & (SPLIT - 1)) ^ mask

    my_expert = me >> 3
    from_expert = my_expert - 1 - block % (experts - 1)
    from_expert = jnp.where(from_expert < 0, from_expert + experts, from_expert)
    near = my_expert * SPLIT + place(block[:SPLIT])
    return jnp.concatenate([near, from_expert * SPLIT + place(block // (experts - 1))])


def pack_routing(expert_id, dropped, slot, gate, slots):
    devices = lax.axis_size("expert")
    ahead = expert_id - (lax.axis_index("expert") >> 3)
    ahead = jnp.where(ahead < 0, ahead + devices // SPLIT, ahead)
    place = jnp.where(dropped == 1, -1, ahead * slots + slot)
    return place.reshape(1, -1), gate.reshape(1, -1)


def chosen(place, first, count):
    rows = lax.broadcasted_iota(jnp.int32, (count, place.shape[1]), 0) + first
    return rows == place


def place_kernel(slots, scale, place, gate, values, near, far):
    rows = values[...]
    if scale:
        count = rows.shape[0]
        across = lax.broadcasted_iota(jnp.int32, (count, count), 1)
        down = lax.broadcasted_iota(jnp.int32, (count, count), 0)
        gates = jnp.where(across == down, gate[...], 0.0)
        column = jnp.sum(gates, axis=1, keepdims=True)
        rows = (column * rows.astype(F32)).astype(BF16)
    for first, out in ((0, near), (slots, far)):
        onehot = chosen(place[...], first, out.shape[0]).astype(F32).astype(BF16)
        out[...] = jnp.dot(onehot, rows, preferred_element_type=F32).astype(BF16)


def to_slots(slots, scale, place, gate, values):
    experts = lax.axis_size("expert") // SPLIT
    width = values.shape[1]
    return pl.pallas_call(
        functools.partial(place_kernel, slots, scale),
        out_shape=(
            jax.ShapeDtypeStruct((slots, width), BF16),
            jax.ShapeDtypeStruct(((experts - 1) * slots, width), BF16),
        ),
        in_specs=[VMEM] * 3,
        out_specs=(VMEM, VMEM),
        compiler_params=params(6),
        cost_estimate=cost(values.size, values.size),
        name="rows_to_slots",
    )(place, gate, values)


def home_kernel(slots, place, gate, kept, got, back, token_grad, gate_grad):
    width = token_grad.shape[1]
    near = kept[...].astype(F32) + got[...].astype(F32)
    total = jnp.zeros(token_grad.shape, F32)
    gates = jnp.zeros(gate_grad.shape, F32)
    for first, rows in ((0, near), (slots, back[...].astype(F32))):
        picks = chosen(place[...], first, rows.shape[0])
        total += lax.dot_general(
            picks.astype(F32).astype(BF16),
            rows[:, :width].astype(BF16),
            (((0,), (0,)), ((), ())),
            preferred_element_type=F32,
        )
        column = rows[:, width : width + 1]
        gates += jnp.sum(jnp.where(picks, column, 0.0), axis=0, keepdims=True)
    token_grad[...] = total.astype(BF16)
    gate_grad[...] = jnp.where(place[...] < 0, 0.0, gates / gate[...])


def to_tokens(slots, place, gate, kept, got, back):
    count, width = place.shape[1], kept.shape[1] - LANES
    return pl.pallas_call(
        functools.partial(home_kernel, slots),
        out_shape=(
            jax.ShapeDtypeStruct((count, width), BF16),
            jax.ShapeDtypeStruct((1, count), F32),
        ),
        in_specs=[VMEM] * 5,
        out_specs=(VMEM, VMEM),
        compiler_params=params(12),
        cost_estimate=cost(LONG, 0),
        name="slots_to_tokens",
    )(place, gate, kept, got, back)


def activation_kernel(order, hidden, activated, slope):
    rows = hidden.shape[1]
    step = 16 if rows % 16 == 0 else rows

    def chunk(i, carry):
        at = pl.ds(i * step, step) if rows > step else slice(None)
        h = hidden[0, at, :].astype(F32)
        cdf = 0.5 * (1.0 + lax.erf(h * 0.7071067811865476))
        density = jnp.exp(-0.5 * h * h) * 0.3989422804014327
        activated[0, at, :] = (h * cdf).astype(BF16)
        slope[0, at, :] = (cdf + h * density).astype(BF16)
        return carry

    lax.fori_loop(0, rows // step, chunk, 0)


def activation(by_source, order):
    _, slots, units = by_source.shape
    block = (1, slots, units)
    shape = (order.shape[0], slots, units)
    act, slope = pl.pallas_call(
        activation_kernel,
        grid_spec=pltpu.PrefetchScalarGridSpec(
            num_scalar_prefetch=1,
            grid=(order.shape[0],),
            in_specs=[pl.BlockSpec(block, lambda i, order: (order[i], 0, 0))],
            out_specs=[pl.BlockSpec(block, lambda i, order: (i, 0, 0))] * 2,
        ),
        out_shape=(jax.ShapeDtypeStruct(shape, BF16),) * 2,
        compiler_params=params(6),
        cost_estimate=cost(0, 0),
        name="activation",
    )(order, by_source)
    return act.reshape(-1, units), slope.reshape(-1, units)


def stack_kernel(*refs):
    out, first = refs[-1], 0
    for ref in refs[:-1]:
        count = ref.shape[0]
        out[first : first + count, :] = ref[...]
        first += count


def join(*pieces, long=False):
    if any(x.shape[0] % 16 for x in pieces):
        return jnp.concatenate(pieces)
    rows, width = sum(x.shape[0] for x in pieces), pieces[0].shape[1]
    return pl.pallas_call(
        stack_kernel,
        out_shape=jax.ShapeDtypeStruct((rows, width), BF16),
        in_specs=[VMEM] * len(pieces),
        out_specs=VMEM,
        compiler_params=params(2 + rows * width * 4 // 1000000),
        cost_estimate=cost(LONG if long else 0, rows * width),
        name="stack_rows",
    )(*pieces)


def add(a, b):
    return (a.astype(F32) + b.astype(F32)).astype(BF16)


def halves(x):
    half = x.shape[0] // 2
    return x[:half], x[half:]


def add_halves(kept, got):
    kept, got = halves(kept), halves(got)
    return add(kept[0], got[0]), add(kept[1], got[1])


def split_slots(rows, experts):
    rows = rows.reshape(experts - 1, -1, rows.shape[1])
    cut = rows.shape[1] - rows.shape[1] // 5
    return [x.reshape(-1, rows.shape[2]) for x in (rows[:, :cut], rows[:, cut:])]


def pause_kernel(rows, out):
    out[...] = rows[...]


def pause(rows):
    return pl.pallas_call(
        pause_kernel,
        out_shape=jax.ShapeDtypeStruct(rows.shape, rows.dtype),
        in_specs=[VMEM],
        out_specs=VMEM,
        compiler_params=params(4),
        cost_estimate=cost(LONG, 0),
        name="pause",
    )(rows)


def join_slots(a, b, experts):
    a, b = [x.reshape(experts - 1, -1, x.shape[1]) for x in (a, b)]
    return jnp.concatenate([a, b], axis=1).reshape(-1, a.shape[2])


def product(a, b, dims):
    return lax.dot_general(a, b, (dims, ((), ())), preferred_element_type=F32)


def slot_grad_kernel(grads, w_out, w_in, act, slope, hidden_grad, kept, sent):
    rows, units = act.shape
    width, half = grads.shape[1], rows // 2
    gates = jnp.zeros((rows, 1), F32)
    for j in range(units // TILE):
        at = slice(j * TILE, (j + 1) * TILE)
        grad_act = product(grads[...], w_out[at, :], ((1,), (1,)))
        hidden_grad[:, at] = (grad_act * slope[:, at].astype(F32)).astype(BF16)
        gates += jnp.sum(grad_act * act[:, at].astype(F32), axis=1, keepdims=True)
    gates = jnp.broadcast_to(gates, (rows, LANES)).astype(BF16)
    kept[:, width:] = gates[:half]
    sent[:, width:] = gates[half:]
    for j in range(width // TILE):
        at = slice(j * TILE, (j + 1) * TILE)
        part = product(hidden_grad[...], w_in[at, :], ((1,), (1,))).astype(BF16)
        kept[:, at] = part[:half]
        sent[:, at] = part[half:]


def slot_grads(grads, w_out, w_in, act, slope):
    rows, units = act.shape
    wide = w_in.shape[0] + LANES
    return pl.pallas_call(
        slot_grad_kernel,
        out_shape=(
            jax.ShapeDtypeStruct((rows, units), BF16),
            jax.ShapeDtypeStruct((rows // 2, wide), BF16),
            jax.ShapeDtypeStruct((rows // 2, wide), BF16),
        ),
        in_specs=[VMEM] * 5,
        out_specs=(VMEM, VMEM, VMEM),
        compiler_params=params(16 + rows // 64),
        cost_estimate=cost(0, 0),
        name="slot_grads",
    )(grads, w_out, w_in, act, slope)


def body(tokens, out_grad, gate, expert_id, dropped, slot, saved_hidden, w_in, w_out):
    devices = lax.axis_size("expert")
    experts = devices // SPLIT
    slots = saved_hidden.shape[0] // devices
    units = saved_hidden.shape[1]
    me = lax.axis_index("expert")
    place, gate = pack_routing(expert_id, dropped, slot, gate, slots)
    order = sources_met(me, experts)
    by_source = saved_hidden.reshape(devices, slots, units)
    near_count = SPLIT * slots

    near_grad, far_grad = to_slots(slots, True, place, gate, out_grad)
    near_row, far_row = to_slots(slots, False, place, gate, tokens)

    far_grad = cross(far_grad, 1)
    got = meet(near_grad, 0)
    act, slope = activation(by_source, order)
    near_two = join(near_grad, after(got, near_row, act))
    got = meet(near_two, 1)
    far_grad = pause(after(far_grad, near_two))
    far_got = meet(far_grad, 0)
    near_four = join(near_two, after(got, far_grad))
    got = meet(near_four, 2)
    far_two = join(far_grad, after(far_got, near_four), long=True)
    far_got = meet(far_two, 1)

    far_row_a, far_row_b = split_slots(after(far_row, far_two), experts)
    far_row_a = cross(far_row_a, 1)
    near_grads = join(near_four, after(got, far_two))
    near_hg, near_kept, near_sent = slot_grads(
        near_grads, w_out, w_in, act[:near_count], slope[:near_count]
    )
    near_got = meet(near_sent, 2)
    far_row_a = after(far_row_a, near_sent)
    far_four = join(far_two, after(far_got, far_row_a), long=True)
    far_got = meet(far_four, 2)
    far_row_b = cross(after(far_row_b, far_four), 1)
    row_got = meet(after(near_row, far_four), 0)
    near_kept, near_sent = add_halves(near_kept, after(near_got, far_four))
    near_got = meet(near_sent, 1)
    far_grads = join(far_four, after(far_got, near_sent))

    far_hg, far_kept, far_sent = slot_grads(
        far_grads, w_out, w_in, act[near_count:], slope[near_count:]
    )
    far_row = join_slots(far_row_a, after(far_row_b, far_sent), experts)
    near_row2 = join(near_row, after(row_got, far_sent))
    far_kept, far_on = halves(far_kept)
    far_sent = halves(after(far_sent, far_row, near_row2))
    far_got, on_got = [meet(x, 2) for x in far_sent]
    row_got = meet(near_row2, 1)
    far_row_got = meet(far_row, 0)
    near_kept, near_sent = add_halves(near_kept, after(near_got, far_sent[1]))
    far_sent = add(far_on, after(on_got, near_sent))
    on_got = meet(far_sent, 1)
    near_got = meet(after(near_sent, far_sent), 0)
    far_kept = add(far_kept, after(far_got, far_sent))
    w_out_grad = product(
        after(act, far_kept), join(near_grads, far_grads), ((0,), (0,))
    ).astype(BF16)
    far_row2 = join(far_row, after(far_row_got, w_out_grad))
    near_row4 = join(near_row2, after(row_got, far_row2))
    row_got = meet(near_row4, 2)
    near_got = after(near_got, near_row4)
    far_kept, far_sent = add_halves(far_kept, after(on_got, near_got))
    far_got = meet(far_sent, 0)
    far_sum = pause(add(far_kept, far_got))
    back = cross(far_sum, -1)

    far_row_got = meet(after(far_row2, far_sum), 1)
    far_row4 = join(far_row2, far_row_got)
    far_row_got = meet(far_row4, 2)
    back = after(back, far_row4)
    token_grad, gate_grad = to_tokens(slots, place, gate, near_kept, near_got, back)
    rows = join(near_row4, row_got, far_row4, after(far_row_got, token_grad))
    w_in_grad = product(rows, join(near_hg, far_hg), ((0,), (0,))).astype(BF16)
    return (token_grad, gate_grad.reshape(-1), w_in_grad, w_out_grad)


def solution(mesh):
    in_specs = (
        P(("parts", "expert"), None),
        P(("parts", "expert"), None),
        P(("parts", "expert")),
        P(("parts", "expert")),
        P(("parts", "expert")),
        P(("parts", "expert")),
        P("parts", "expert"),
        P(None, "expert"),
        P("expert", None),
    )
    out_specs = (
        P(("parts", "expert"), None),
        P(("parts", "expert")),
        P("parts", "expert"),
        P(("parts", "expert"), None),
    )
    return jax.shard_map(body, mesh=mesh, in_specs=in_specs, out_specs=out_specs, check_vma=False)
```

```python
import functools

import jax
import jax.numpy as jnp
from jax import lax
from jax.experimental import pallas as pl
from jax.experimental.pallas import tpu as pltpu
from jax.sharding import PartitionSpec as P

SPLIT = 8
CORE, LOW, HIGH = 1, 2, 4
LANES, TILE = 128, 256
LONG = 20_000_000_000
VMEM = pl.BlockSpec(memory_space=pltpu.VMEM)
F32, BF16 = jnp.float32, jnp.bfloat16


def params(mib):
    return pltpu.CompilerParams(vmem_limit_bytes=mib * 1024 * 1024)


def cost(flops, moved, exps=0):
    return pl.CostEstimate(flops=flops, bytes_accessed=moved, transcendentals=exps)


def bits(core):
    return (HIGH, LOW, CORE) if core == 0 else (LOW, HIGH, CORE)


def meet(rows, step):
    devices = lax.axis_size("expert")
    return lax.ppermute(rows, "expert", [(i, i ^ bits(i % 2)[step]) for i in range(devices)])


def shift(rows, by):
    devices = lax.axis_size("expert")
    pairs = [(i, (i + by * SPLIT) % devices) for i in range(devices)]
    return lax.ppermute(rows, "expert", pairs)


def cross(rows, sign):
    experts = lax.axis_size("expert") // SPLIT
    if experts == 2:
        return shift(rows, sign)
    slots = rows.shape[0] // (experts - 1)
    return jnp.concatenate(
        [shift(rows[(s - 1) * slots : s * slots], sign * s) for s in range(1, experts)]
    )


def after(value, *earlier):
    return lax.optimization_barrier((value, *earlier))[0]


def sources_met(me, experts):
    block = jnp.arange(SPLIT * (experts - 1), dtype=jnp.int32)

    def place(i):
        first = jnp.where(((me ^ (i >> 2)) & 1) == 1, LOW, HIGH)
        second = (LOW + HIGH) - first
        mask = (i & 1) * first + ((i >> 1) & 1) * second + (i >> 2) * CORE
        return (me & (SPLIT - 1)) ^ mask

    my_expert = me >> 3
    from_expert = my_expert - 1 - block % (experts - 1)
    from_expert = jnp.where(from_expert < 0, from_expert + experts, from_expert)
    near = my_expert * SPLIT + place(block[:SPLIT])
    return jnp.concatenate([near, from_expert * SPLIT + place(block // (experts - 1))])


def pack_routing(expert_id, dropped, slot, gate, slots):
    devices = lax.axis_size("expert")
    ahead = expert_id - (lax.axis_index("expert") >> 3)
    ahead = jnp.where(ahead < 0, ahead + devices // SPLIT, ahead)
    place = jnp.where(dropped == 1, -1, ahead * slots + slot)
    return place.reshape(1, -1), gate.reshape(1, -1)


def chosen(place, first, count):
    rows = lax.broadcasted_iota(jnp.int32, (count, place.shape[1]), 0) + first
    return rows == place


def place_kernel(slots, scale, place, gate, values, near, far):
    rows = values[...]
    if scale:
        count = rows.shape[0]
        across = lax.broadcasted_iota(jnp.int32, (count, count), 1)
        down = lax.broadcasted_iota(jnp.int32, (count, count), 0)
        gates = jnp.where(across == down, gate[...], 0.0)
        column = jnp.sum(gates, axis=1, keepdims=True)
        rows = (column * rows.astype(F32)).astype(BF16)
    for first, out in ((0, near), (slots, far)):
        onehot = chosen(place[...], first, out.shape[0]).astype(F32).astype(BF16)
        out[...] = jnp.dot(onehot, rows, preferred_element_type=F32).astype(BF16)


def to_slots(slots, scale, place, gate, values):
    experts = lax.axis_size("expert") // SPLIT
    width = values.shape[1]
    return pl.pallas_call(
        functools.partial(place_kernel, slots, scale),
        out_shape=(
            jax.ShapeDtypeStruct((slots, width), BF16),
            jax.ShapeDtypeStruct(((experts - 1) * slots, width), BF16),
        ),
        in_specs=[VMEM] * 3,
        out_specs=(VMEM, VMEM),
        compiler_params=params(6),
        cost_estimate=cost(values.size, values.size),
        name="rows_to_slots",
    )(place, gate, values)


def home_kernel(slots, place, gate, kept, got, back, token_grad, gate_grad):
    width = token_grad.shape[1]
    near = kept[...].astype(F32) + got[...].astype(F32)
    total = jnp.zeros(token_grad.shape, F32)
    gates = jnp.zeros(gate_grad.shape, F32)
    for first, rows in ((0, near), (slots, back[...].astype(F32))):
        picks = chosen(place[...], first, rows.shape[0])
        total += lax.dot_general(
            picks.astype(F32).astype(BF16),
            rows[:, :width].astype(BF16),
            (((0,), (0,)), ((), ())),
            preferred_element_type=F32,
        )
        column = rows[:, width : width + 1]
        gates += jnp.sum(jnp.where(picks, column, 0.0), axis=0, keepdims=True)
    token_grad[...] = total.astype(BF16)
    gate_grad[...] = jnp.where(place[...] < 0, 0.0, gates / gate[...])


def to_tokens(slots, place, gate, kept, got, back):
    count, width = place.shape[1], kept.shape[1] - LANES
    return pl.pallas_call(
        functools.partial(home_kernel, slots),
        out_shape=(
            jax.ShapeDtypeStruct((count, width), BF16),
            jax.ShapeDtypeStruct((1, count), F32),
        ),
        in_specs=[VMEM] * 5,
        out_specs=(VMEM, VMEM),
        compiler_params=params(12),
        name="slots_to_tokens",
    )(place, gate, kept, got, back)


def activation_kernel(order, hidden, activated, slope):
    rows = hidden.shape[1]
    step = 16 if rows % 16 == 0 else rows

    def chunk(i, carry):
        at = pl.ds(i * step, step) if rows > step else slice(None)
        h = hidden[0, at, :].astype(F32)
        cdf = 0.5 * (1.0 + lax.erf(h * 0.7071067811865476))
        density = jnp.exp(-0.5 * h * h) * 0.3989422804014327
        activated[0, at, :] = (h * cdf).astype(BF16)
        slope[0, at, :] = (cdf + h * density).astype(BF16)
        return carry

    lax.fori_loop(0, rows // step, chunk, 0)


def activation(by_source, order):
    _, slots, units = by_source.shape
    block = (1, slots, units)
    shape = (order.shape[0], slots, units)
    act, slope = pl.pallas_call(
        activation_kernel,
        grid_spec=pltpu.PrefetchScalarGridSpec(
            num_scalar_prefetch=1,
            grid=(order.shape[0],),
            in_specs=[pl.BlockSpec(block, lambda i, order: (order[i], 0, 0))],
            out_specs=[pl.BlockSpec(block, lambda i, order: (i, 0, 0))] * 2,
        ),
        out_shape=(jax.ShapeDtypeStruct(shape, BF16),) * 2,
        compiler_params=params(6),
        cost_estimate=cost(0, 0),
        name="activation",
    )(order, by_source)
    return act.reshape(-1, units), slope.reshape(-1, units)


def stack_kernel(*refs):
    out, first = refs[-1], 0
    for ref in refs[:-1]:
        count = ref.shape[0]
        out[first : first + count, :] = ref[...]
        first += count


def join(*pieces, long=False):
    if any(x.shape[0] % 16 for x in pieces):
        return jnp.concatenate(pieces)
    rows, width = sum(x.shape[0] for x in pieces), pieces[0].shape[1]
    return pl.pallas_call(
        stack_kernel,
        out_shape=jax.ShapeDtypeStruct((rows, width), BF16),
        in_specs=[VMEM] * len(pieces),
        out_specs=VMEM,
        compiler_params=params(2 + rows * width * 4 // 1000000),
        cost_estimate=cost(LONG if long else 0, rows * width),
        name="stack_rows",
    )(*pieces)


def add(a, b):
    return (a.astype(F32) + b.astype(F32)).astype(BF16)


def halves(x):
    half = x.shape[0] // 2
    return x[:half], x[half:]


def add_halves(kept, got):
    kept, got = halves(kept), halves(got)
    return add(kept[0], got[0]), add(kept[1], got[1])


def split_slots(rows, experts):
    rows = rows.reshape(experts - 1, -1, rows.shape[1])
    cut = rows.shape[1] // 2
    return [x.reshape(-1, rows.shape[2]) for x in (rows[:, :cut], rows[:, cut:])]


def pause_kernel(rows, out):
    out[...] = rows[...]


def pause(rows):
    return pl.pallas_call(
        pause_kernel,
        out_shape=jax.ShapeDtypeStruct(rows.shape, rows.dtype),
        in_specs=[VMEM],
        out_specs=VMEM,
        compiler_params=params(4),
        cost_estimate=cost(LONG, 0),
        name="pause",
    )(rows)


def join_slots(a, b, experts):
    a, b = [x.reshape(experts - 1, -1, x.shape[1]) for x in (a, b)]
    return jnp.concatenate([a, b], axis=1).reshape(-1, a.shape[2])


def product(a, b, dims):
    return lax.dot_general(a, b, (dims, ((), ())), preferred_element_type=F32)


def slot_grad_kernel(grads, w_out, w_in, act, slope, hidden_grad, kept, sent):
    rows, units = act.shape
    width, half = grads.shape[1], rows // 2
    gates = jnp.zeros((rows, 1), F32)
    for j in range(units // TILE):
        at = slice(j * TILE, (j + 1) * TILE)
        grad_act = product(grads[...], w_out[at, :], ((1,), (1,)))
        hidden_grad[:, at] = (grad_act * slope[:, at].astype(F32)).astype(BF16)
        gates += jnp.sum(grad_act * act[:, at].astype(F32), axis=1, keepdims=True)
    gates = jnp.broadcast_to(gates, (rows, LANES)).astype(BF16)
    kept[:, width:] = gates[:half]
    sent[:, width:] = gates[half:]
    for j in range(width // TILE):
        at = slice(j * TILE, (j + 1) * TILE)
        part = product(hidden_grad[...], w_in[at, :], ((1,), (1,))).astype(BF16)
        kept[:, at] = part[:half]
        sent[:, at] = part[half:]


def slot_grads(grads, w_out, w_in, act, slope):
    rows, units = act.shape
    wide = w_in.shape[0] + LANES
    return pl.pallas_call(
        slot_grad_kernel,
        out_shape=(
            jax.ShapeDtypeStruct((rows, units), BF16),
            jax.ShapeDtypeStruct((rows // 2, wide), BF16),
            jax.ShapeDtypeStruct((rows // 2, wide), BF16),
        ),
        in_specs=[VMEM] * 5,
        out_specs=(VMEM, VMEM, VMEM),
        compiler_params=params(16 + rows // 64),
        cost_estimate=cost(0, 0),
        name="slot_grads",
    )(grads, w_out, w_in, act, slope)


def body(tokens, out_grad, gate, expert_id, dropped, slot, saved_hidden, w_in, w_out):
    devices = lax.axis_size("expert")
    experts = devices // SPLIT
    slots = saved_hidden.shape[0] // devices
    units = saved_hidden.shape[1]
    me = lax.axis_index("expert")
    place, gate = pack_routing(expert_id, dropped, slot, gate, slots)
    order = sources_met(me, experts)
    by_source = saved_hidden.reshape(devices, slots, units)
    near_count = SPLIT * slots

    near_grad, far_grad = to_slots(slots, True, place, gate, out_grad)
    near_row, far_row = to_slots(slots, False, place, gate, tokens)

    far_grad = cross(far_grad, 1)
    got = meet(near_grad, 0)
    near_two = join(near_grad, after(got, near_row))
    got = meet(near_two, 1)
    act, slope = activation(by_source, after(order, near_two))
    far_grad = pause(after(far_grad, act))
    far_got = meet(far_grad, 0)
    near_four = join(near_two, after(got, far_grad))
    got = meet(near_four, 2)
    far_two = join(far_grad, after(far_got, near_four), long=True)
    far_got = meet(far_two, 1)

    far_row_a, far_row_b = split_slots(after(far_row, far_two), experts)
    far_row_a = cross(far_row_a, 1)
    row_got = meet(after(near_row, far_two), 0)
    near_grads = join(near_four, after(got, far_two))
    near_hg, near_kept, near_sent = slot_grads(
        near_grads, w_out, w_in, act[:near_count], slope[:near_count]
    )
    near_got = meet(near_sent, 2)
    far_row_a = after(far_row_a, near_sent)
    near_row2 = join(near_row, after(row_got, far_row_a))
    far_four = join(far_two, after(far_got, near_row2), long=True)
    far_got = meet(far_four, 2)
    far_row_b = cross(after(far_row_b, far_four), 1)
    near_kept, near_sent = add_halves(near_kept, after(near_got, far_four))
    near_got = meet(near_sent, 1)
    far_grads = join(far_four, after(far_got, near_sent))

    far_hg, far_kept, far_sent = slot_grads(
        far_grads, w_out, w_in, act[near_count:], slope[near_count:]
    )
    far_row = join_slots(far_row_a, after(far_row_b, far_sent), experts)
    far_kept, far_on = halves(far_kept)
    far_sent = halves(after(far_sent, far_row))
    far_got, on_got = [meet(x, 2) for x in far_sent]
    row_got = meet(near_row2, 1)
    far_row_got = meet(far_row, 0)
    near_kept, near_sent = add_halves(near_kept, after(near_got, far_sent[1]))
    far_sent = add(far_on, after(on_got, near_sent))
    on_got = meet(far_sent, 1)
    far_kept = add(far_kept, after(far_got, far_sent))
    w_out_grad = product(
        after(act, far_kept), join(near_grads, far_grads), ((0,), (0,))
    ).astype(BF16)
    far_row2 = join(far_row, after(far_row_got, w_out_grad))
    far_row_got = meet(far_row2, 1)
    near_row4 = join(near_row2, after(row_got, far_row2))
    row_got = meet(near_row4, 2)
    far_kept, far_sent = add_halves(far_kept, after(on_got, near_row4))
    far_got = meet(far_sent, 0)
    far_row4 = join(far_row2, after(far_row_got, far_sent))
    far_sum = pause(add(far_kept, after(far_got, far_row4)))
    back = cross(far_sum, -1)
    near_got = meet(after(near_sent, far_sum), 0)
    rows = join(near_row4, row_got, far_row4, meet(far_row4, 2))
    w_in_grad = product(rows, join(near_hg, far_hg), ((0,), (0,))).astype(BF16)
    back = after(back, w_in_grad)
    near_got = after(near_got, back)
    token_grad, gate_grad = to_tokens(slots, place, gate, near_kept, near_got, back)
    return (token_grad, gate_grad.reshape(-1), w_in_grad, w_out_grad)


def solution(mesh):
    in_specs = (
        P(("parts", "expert"), None),
        P(("parts", "expert"), None),
        P(("parts", "expert")),
        P(("parts", "expert")),
        P(("parts", "expert")),
        P(("parts", "expert")),
        P("parts", "expert"),
        P(None, "expert"),
        P("expert", None),
    )
    out_specs = (
        P(("parts", "expert"), None),
        P(("parts", "expert")),
        P("parts", "expert"),
        P(("parts", "expert"), None),
    )
    return jax.shard_map(body, mesh=mesh, in_specs=in_specs, out_specs=out_specs, check_vma=False)
```

```python
import functools

import jax
import jax.numpy as jnp
from jax import lax
from jax.experimental import pallas as pl
from jax.experimental.pallas import tpu as pltpu
from jax.sharding import PartitionSpec as P

SPLIT = 8
CORE, LOW, HIGH = 1, 2, 4
LANES, TILE = 128, 256
LONG = 20_000_000_000
VMEM = pl.BlockSpec(memory_space=pltpu.VMEM)
F32, BF16 = jnp.float32, jnp.bfloat16


def params(mib):
    return pltpu.CompilerParams(vmem_limit_bytes=mib * 1024 * 1024)


def cost(flops, moved, exps=0):
    return pl.CostEstimate(flops=flops, bytes_accessed=moved, transcendentals=exps)


def bits(core):
    return (HIGH, LOW, CORE) if core == 0 else (LOW, HIGH, CORE)


def meet(rows, step):
    devices = lax.axis_size("expert")
    return lax.ppermute(rows, "expert", [(i, i ^ bits(i % 2)[step]) for i in range(devices)])


def shift(rows, by):
    devices = lax.axis_size("expert")
    pairs = [(i, (i + by * SPLIT) % devices) for i in range(devices)]
    return lax.ppermute(rows, "expert", pairs)


def cross(rows, sign):
    experts = lax.axis_size("expert") // SPLIT
    if experts == 2:
        return shift(rows, sign)
    slots = rows.shape[0] // (experts - 1)
    return jnp.concatenate(
        [shift(rows[(s - 1) * slots : s * slots], sign * s) for s in range(1, experts)]
    )


def after(value, *earlier):
    return lax.optimization_barrier((value, *earlier))[0]


def sources_met(me, experts):
    block = jnp.arange(SPLIT * (experts - 1), dtype=jnp.int32)

    def place(i):
        first = jnp.where(((me ^ (i >> 2)) & 1) == 1, LOW, HIGH)
        second = (LOW + HIGH) - first
        mask = (i & 1) * first + ((i >> 1) & 1) * second + (i >> 2) * CORE
        return (me & (SPLIT - 1)) ^ mask

    my_expert = me >> 3
    from_expert = my_expert - 1 - block % (experts - 1)
    from_expert = jnp.where(from_expert < 0, from_expert + experts, from_expert)
    near = my_expert * SPLIT + place(block[:SPLIT])
    return jnp.concatenate([near, from_expert * SPLIT + place(block // (experts - 1))])


def pack_routing(expert_id, dropped, slot, gate, slots):
    devices = lax.axis_size("expert")
    ahead = expert_id - (lax.axis_index("expert") >> 3)
    ahead = jnp.where(ahead < 0, ahead + devices // SPLIT, ahead)
    place = jnp.where(dropped == 1, -1, ahead * slots + slot)
    return place.reshape(1, -1), gate.reshape(1, -1)


def chosen(place, first, count):
    rows = lax.broadcasted_iota(jnp.int32, (count, place.shape[1]), 0) + first
    return rows == place


def place_kernel(slots, place, values, near, far):
    for first, out in ((0, near), (slots, far)):
        onehot = chosen(place[...], first, out.shape[0]).astype(F32).astype(BF16)
        out[...] = jnp.dot(onehot, values[...], preferred_element_type=F32).astype(BF16)


def to_slots(slots, place, values):
    experts = lax.axis_size("expert") // SPLIT
    width = values.shape[1]
    return pl.pallas_call(
        functools.partial(place_kernel, slots),
        out_shape=(
            jax.ShapeDtypeStruct((slots, width), BF16),
            jax.ShapeDtypeStruct(((experts - 1) * slots, width), BF16),
        ),
        in_specs=[VMEM] * 2,
        out_specs=(VMEM, VMEM),
        compiler_params=params(6),
        cost_estimate=cost(values.size, values.size),
        name="rows_to_slots",
    )(place, values)


def home_kernel(slots, place, gate, kept, got, back, token_grad, gate_grad):
    width = token_grad.shape[1]
    near = kept[...].astype(F32) + got[...].astype(F32)
    total = jnp.zeros(token_grad.shape, F32)
    gates = jnp.zeros(gate_grad.shape, F32)
    for first, rows in ((0, near), (slots, back[...].astype(F32))):
        picks = chosen(place[...], first, rows.shape[0])
        total += lax.dot_general(
            picks.astype(F32).astype(BF16),
            rows[:, :width].astype(BF16),
            (((0,), (0,)), ((), ())),
            preferred_element_type=F32,
        )
        column = rows[:, width : width + 1]
        gates += jnp.sum(jnp.where(picks, column, 0.0), axis=0, keepdims=True)
    token_grad[...] = total.astype(BF16)
    gate_grad[...] = jnp.where(place[...] < 0, 0.0, gates / gate[...])


def to_tokens(slots, place, gate, kept, got, back):
    count, width = place.shape[1], kept.shape[1] - LANES
    return pl.pallas_call(
        functools.partial(home_kernel, slots),
        out_shape=(
            jax.ShapeDtypeStruct((count, width), BF16),
            jax.ShapeDtypeStruct((1, count), F32),
        ),
        in_specs=[VMEM] * 5,
        out_specs=(VMEM, VMEM),
        compiler_params=params(12),
        name="slots_to_tokens",
    )(place, gate, kept, got, back)


def activation_kernel(order, hidden, activated, slope):
    rows = hidden.shape[1]
    step = 16 if rows % 16 == 0 else rows

    def chunk(i, carry):
        at = pl.ds(i * step, step) if rows > step else slice(None)
        h = hidden[0, at, :].astype(F32)
        cdf = 0.5 * (1.0 + lax.erf(h * 0.7071067811865476))
        density = jnp.exp(-0.5 * h * h) * 0.3989422804014327
        activated[0, at, :] = (h * cdf).astype(BF16)
        slope[0, at, :] = (cdf + h * density).astype(BF16)
        return carry

    lax.fori_loop(0, rows // step, chunk, 0)


def activation(by_source, order):
    _, slots, units = by_source.shape
    block = (1, slots, units)
    shape = (order.shape[0], slots, units)
    act, slope = pl.pallas_call(
        activation_kernel,
        grid_spec=pltpu.PrefetchScalarGridSpec(
            num_scalar_prefetch=1,
            grid=(order.shape[0],),
            in_specs=[pl.BlockSpec(block, lambda i, order: (order[i], 0, 0))],
            out_specs=[pl.BlockSpec(block, lambda i, order: (i, 0, 0))] * 2,
        ),
        out_shape=(jax.ShapeDtypeStruct(shape, BF16),) * 2,
        compiler_params=params(6),
        cost_estimate=cost(0, 0),
        name="activation",
    )(order, by_source)
    return act.reshape(-1, units), slope.reshape(-1, units)


def stack_kernel(*refs):
    out, first = refs[-1], 0
    for ref in refs[:-1]:
        count = ref.shape[0]
        out[first : first + count, :] = ref[...]
        first += count


def join(*pieces, long=False):
    if any(x.shape[0] % 16 for x in pieces):
        return jnp.concatenate(pieces)
    rows, width = sum(x.shape[0] for x in pieces), pieces[0].shape[1]
    return pl.pallas_call(
        stack_kernel,
        out_shape=jax.ShapeDtypeStruct((rows, width), BF16),
        in_specs=[VMEM] * len(pieces),
        out_specs=VMEM,
        compiler_params=params(2 + rows * width * 4 // 1000000),
        cost_estimate=cost(LONG if long else 0, rows * width),
        name="stack_rows",
    )(*pieces)


def add(a, b):
    return (a.astype(F32) + b.astype(F32)).astype(BF16)


def halves(x):
    half = x.shape[0] // 2
    return x[:half], x[half:]


def add_halves(kept, got):
    kept, got = halves(kept), halves(got)
    return add(kept[0], got[0]), add(kept[1], got[1])


def split_slots(rows, experts):
    rows = rows.reshape(experts - 1, -1, rows.shape[1])
    cut = rows.shape[1] // 2
    return [x.reshape(-1, rows.shape[2]) for x in (rows[:, :cut], rows[:, cut:])]


def pause_kernel(rows, out):
    out[...] = rows[...]


def pause(rows):
    return pl.pallas_call(
        pause_kernel,
        out_shape=jax.ShapeDtypeStruct(rows.shape, rows.dtype),
        in_specs=[VMEM],
        out_specs=VMEM,
        compiler_params=params(4),
        cost_estimate=cost(LONG, 0),
        name="pause",
    )(rows)


def join_slots(a, b, experts):
    a, b = [x.reshape(experts - 1, -1, x.shape[1]) for x in (a, b)]
    return jnp.concatenate([a, b], axis=1).reshape(-1, a.shape[2])


def product(a, b, dims):
    return lax.dot_general(a, b, (dims, ((), ())), preferred_element_type=F32)


def slot_grad_kernel(grads, w_out, w_in, act, slope, hidden_grad, kept, sent):
    rows, units = act.shape
    width, half = grads.shape[1], rows // 2
    gates = jnp.zeros((rows, 1), F32)
    for j in range(units // TILE):
        at = slice(j * TILE, (j + 1) * TILE)
        grad_act = product(grads[...], w_out[at, :], ((1,), (1,)))
        hidden_grad[:, at] = (grad_act * slope[:, at].astype(F32)).astype(BF16)
        gates += jnp.sum(grad_act * act[:, at].astype(F32), axis=1, keepdims=True)
    gates = jnp.broadcast_to(gates, (rows, LANES)).astype(BF16)
    kept[:, width:] = gates[:half]
    sent[:, width:] = gates[half:]
    for j in range(width // TILE):
        at = slice(j * TILE, (j + 1) * TILE)
        part = product(hidden_grad[...], w_in[at, :], ((1,), (1,))).astype(BF16)
        kept[:, at] = part[:half]
        sent[:, at] = part[half:]


def slot_grads(grads, w_out, w_in, act, slope):
    rows, units = act.shape
    wide = w_in.shape[0] + LANES
    return pl.pallas_call(
        slot_grad_kernel,
        out_shape=(
            jax.ShapeDtypeStruct((rows, units), BF16),
            jax.ShapeDtypeStruct((rows // 2, wide), BF16),
            jax.ShapeDtypeStruct((rows // 2, wide), BF16),
        ),
        in_specs=[VMEM] * 5,
        out_specs=(VMEM, VMEM, VMEM),
        compiler_params=params(16 + rows // 64),
        cost_estimate=cost(0, 0),
        name="slot_grads",
    )(grads, w_out, w_in, act, slope)


def body(tokens, out_grad, gate, expert_id, dropped, slot, saved_hidden, w_in, w_out):
    devices = lax.axis_size("expert")
    experts = devices // SPLIT
    slots = saved_hidden.shape[0] // devices
    units = saved_hidden.shape[1]
    me = lax.axis_index("expert")
    scaled = (gate[:, None] * out_grad.astype(F32)).astype(BF16)
    place, gate = pack_routing(expert_id, dropped, slot, gate, slots)
    order = sources_met(me, experts)
    by_source = saved_hidden.reshape(devices, slots, units)
    near_count = SPLIT * slots

    near_grad, far_grad = to_slots(slots, place, scaled)
    near_row, far_row = to_slots(slots, place, tokens)

    far_grad = cross(far_grad, 1)
    got = meet(near_grad, 0)
    near_two = join(near_grad, after(got, near_row))
    got = meet(near_two, 1)
    far_grad = pause(after(far_grad, near_two))
    act, slope = activation(by_source, after(order, far_grad))
    far_got = meet(far_grad, 0)
    near_four = join(near_two, after(got, act))
    got = meet(near_four, 2)
    far_two = join(far_grad, after(far_got, near_four), long=True)
    far_got = meet(far_two, 1)

    far_row_a, far_row_b = split_slots(after(far_row, far_two), experts)
    far_row_a = cross(far_row_a, 1)
    row_got = meet(after(near_row, far_two), 0)
    near_grads = join(near_four, after(got, far_two))
    near_hg, near_kept, near_sent = slot_grads(
        near_grads, w_out, w_in, act[:near_count], slope[:near_count]
    )
    near_got = meet(near_sent, 2)
    far_row_a = after(far_row_a, near_sent)
    near_row2 = join(near_row, after(row_got, far_row_a))
    far_four = join(far_two, after(far_got, near_row2), long=True)
    far_got = meet(far_four, 2)
    far_row_b = cross(after(far_row_b, far_four), 1)
    near_kept, near_sent = add_halves(near_kept, after(near_got, far_four))
    near_got = meet(near_sent, 1)
    far_grads = join(far_four, after(far_got, near_sent))

    far_hg, far_kept, far_sent = slot_grads(
        far_grads, w_out, w_in, act[near_count:], slope[near_count:]
    )
    far_row = join_slots(far_row_a, after(far_row_b, far_sent), experts)
    far_kept, far_on = halves(far_kept)
    far_sent = halves(after(far_sent, far_row))
    far_got, on_got = [meet(x, 2) for x in far_sent]
    row_got = meet(near_row2, 1)
    far_row_got = meet(far_row, 0)
    near_kept, near_sent = add_halves(near_kept, after(near_got, far_sent[1]))
    far_sent = add(far_on, after(on_got, near_sent))
    on_got = meet(far_sent, 1)
    far_kept = add(far_kept, after(far_got, far_sent))
    w_out_grad = product(
        after(act, far_kept), join(near_grads, far_grads), ((0,), (0,))
    ).astype(BF16)
    far_row2 = join(far_row, after(far_row_got, w_out_grad))
    far_row_got = meet(far_row2, 1)
    near_row4 = join(near_row2, after(row_got, far_row2))
    row_got = meet(near_row4, 2)
    far_kept, far_sent = add_halves(far_kept, after(on_got, near_row4))
    far_got = meet(far_sent, 0)
    far_row4 = join(far_row2, after(far_row_got, far_sent))
    far_sum = pause(add(far_kept, after(far_got, far_row4)))
    back = cross(far_sum, -1)
    near_got = meet(after(near_sent, far_sum), 0)
    rows = join(near_row4, row_got, far_row4, meet(far_row4, 2))
    w_in_grad = product(rows, join(near_hg, far_hg), ((0,), (0,))).astype(BF16)
    back = after(back, w_in_grad)
    near_got = after(near_got, back)
    token_grad, gate_grad = to_tokens(slots, place, gate, near_kept, near_got, back)
    return (token_grad, gate_grad.reshape(-1), w_in_grad, w_out_grad)


def solution(mesh):
    in_specs = (
        P(("parts", "expert"), None),
        P(("parts", "expert"), None),
        P(("parts", "expert")),
        P(("parts", "expert")),
        P(("parts", "expert")),
        P(("parts", "expert")),
        P("parts", "expert"),
        P(None, "expert"),
        P("expert", None),
    )
    out_specs = (
        P(("parts", "expert"), None),
        P(("parts", "expert")),
        P("parts", "expert"),
        P(("parts", "expert"), None),
    )
    return jax.shard_map(body, mesh=mesh, in_specs=in_specs, out_specs=out_specs, check_vma=False)
```

```python
import functools

import jax
import jax.numpy as jnp
from jax import lax
from jax.experimental import pallas as pl
from jax.experimental.pallas import tpu as pltpu
from jax.sharding import PartitionSpec as P

SPLIT = 8
CORE, LOW, HIGH = 1, 2, 4
LANES, TILE = 128, 256
LONG = 20_000_000_000
VMEM = pl.BlockSpec(memory_space=pltpu.VMEM)
F32, BF16 = jnp.float32, jnp.bfloat16


def params(mib):
    return pltpu.CompilerParams(vmem_limit_bytes=mib * 1024 * 1024)


def cost(flops, moved, exps=0):
    return pl.CostEstimate(flops=flops, bytes_accessed=moved, transcendentals=exps)


def bits(core):
    return (HIGH, LOW, CORE) if core == 0 else (LOW, HIGH, CORE)


def meet(rows, step):
    devices = lax.axis_size("expert")
    return lax.ppermute(rows, "expert", [(i, i ^ bits(i % 2)[step]) for i in range(devices)])


def shift(rows, by):
    devices = lax.axis_size("expert")
    pairs = [(i, (i + by * SPLIT) % devices) for i in range(devices)]
    return lax.ppermute(rows, "expert", pairs)


def cross(rows, sign):
    experts = lax.axis_size("expert") // SPLIT
    if experts == 2:
        return shift(rows, sign)
    slots = rows.shape[0] // (experts - 1)
    return jnp.concatenate(
        [shift(rows[(s - 1) * slots : s * slots], sign * s) for s in range(1, experts)]
    )


def after(value, *earlier):
    return lax.optimization_barrier((value, *earlier))[0]


def sources_met(me, experts):
    block = jnp.arange(SPLIT * (experts - 1), dtype=jnp.int32)

    def place(i):
        first = jnp.where(((me ^ (i >> 2)) & 1) == 1, LOW, HIGH)
        second = (LOW + HIGH) - first
        mask = (i & 1) * first + ((i >> 1) & 1) * second + (i >> 2) * CORE
        return (me & (SPLIT - 1)) ^ mask

    my_expert = me >> 3
    from_expert = my_expert - 1 - block % (experts - 1)
    from_expert = jnp.where(from_expert < 0, from_expert + experts, from_expert)
    near = my_expert * SPLIT + place(block[:SPLIT])
    return jnp.concatenate([near, from_expert * SPLIT + place(block // (experts - 1))])


def pack_routing(expert_id, dropped, slot, gate, slots):
    devices = lax.axis_size("expert")
    ahead = expert_id - (lax.axis_index("expert") >> 3)
    ahead = jnp.where(ahead < 0, ahead + devices // SPLIT, ahead)
    place = jnp.where(dropped == 1, -1, ahead * slots + slot)
    return place.reshape(1, -1), gate.reshape(1, -1)


def chosen(place, first, count):
    rows = lax.broadcasted_iota(jnp.int32, (count, place.shape[1]), 0) + first
    return rows == place


def place_kernel(slots, scale, place, gate, values, near, far):
    rows = values[...]
    if scale:
        count = rows.shape[0]
        across = lax.broadcasted_iota(jnp.int32, (count, count), 1)
        down = lax.broadcasted_iota(jnp.int32, (count, count), 0)
        gates = jnp.where(across == down, gate[...], 0.0)
        column = jnp.sum(gates, axis=1, keepdims=True)
        rows = (column * rows.astype(F32)).astype(BF16)
    for first, out in ((0, near), (slots, far)):
        onehot = chosen(place[...], first, out.shape[0]).astype(F32).astype(BF16)
        out[...] = jnp.dot(onehot, rows, preferred_element_type=F32).astype(BF16)


def to_slots(slots, scale, place, gate, values):
    experts = lax.axis_size("expert") // SPLIT
    width = values.shape[1]
    return pl.pallas_call(
        functools.partial(place_kernel, slots, scale),
        out_shape=(
            jax.ShapeDtypeStruct((slots, width), BF16),
            jax.ShapeDtypeStruct(((experts - 1) * slots, width), BF16),
        ),
        in_specs=[VMEM] * 3,
        out_specs=(VMEM, VMEM),
        compiler_params=params(6),
        cost_estimate=cost(values.size, values.size),
        name="rows_to_slots",
    )(place, gate, values)


def home_kernel(slots, place, gate, kept, got, back, token_grad, gate_grad):
    width = token_grad.shape[1]
    near = kept[...].astype(F32) + got[...].astype(F32)
    total = jnp.zeros(token_grad.shape, F32)
    gates = jnp.zeros(gate_grad.shape, F32)
    for first, rows in ((0, near), (slots, back[...].astype(F32))):
        picks = chosen(place[...], first, rows.shape[0])
        total += lax.dot_general(
            picks.astype(F32).astype(BF16),
            rows[:, :width].astype(BF16),
            (((0,), (0,)), ((), ())),
            preferred_element_type=F32,
        )
        column = rows[:, width : width + 1]
        gates += jnp.sum(jnp.where(picks, column, 0.0), axis=0, keepdims=True)
    token_grad[...] = total.astype(BF16)
    gate_grad[...] = jnp.where(place[...] < 0, 0.0, gates / gate[...])


def to_tokens(slots, place, gate, kept, got, back):
    count, width = place.shape[1], kept.shape[1] - LANES
    return pl.pallas_call(
        functools.partial(home_kernel, slots),
        out_shape=(
            jax.ShapeDtypeStruct((count, width), BF16),
            jax.ShapeDtypeStruct((1, count), F32),
        ),
        in_specs=[VMEM] * 5,
        out_specs=(VMEM, VMEM),
        compiler_params=params(12),
        name="slots_to_tokens",
    )(place, gate, kept, got, back)


def activation_kernel(order, hidden, activated, slope):
    rows = hidden.shape[1]
    step = 16 if rows % 16 == 0 else rows

    def chunk(i, carry):
        at = pl.ds(i * step, step) if rows > step else slice(None)
        h = hidden[0, at, :].astype(F32)
        cdf = 0.5 * (1.0 + lax.erf(h * 0.7071067811865476))
        density = jnp.exp(-0.5 * h * h) * 0.3989422804014327
        activated[0, at, :] = (h * cdf).astype(BF16)
        slope[0, at, :] = (cdf + h * density).astype(BF16)
        return carry

    lax.fori_loop(0, rows // step, chunk, 0)


def activation(by_source, order):
    _, slots, units = by_source.shape
    block = (1, slots, units)
    shape = (order.shape[0], slots, units)
    act, slope = pl.pallas_call(
        activation_kernel,
        grid_spec=pltpu.PrefetchScalarGridSpec(
            num_scalar_prefetch=1,
            grid=(order.shape[0],),
            in_specs=[pl.BlockSpec(block, lambda i, order: (order[i], 0, 0))],
            out_specs=[pl.BlockSpec(block, lambda i, order: (i, 0, 0))] * 2,
        ),
        out_shape=(jax.ShapeDtypeStruct(shape, BF16),) * 2,
        compiler_params=params(6),
        cost_estimate=cost(0, 0),
        name="activation",
    )(order, by_source)
    return act.reshape(-1, units), slope.reshape(-1, units)


def stack_kernel(*refs):
    out, first = refs[-1], 0
    for ref in refs[:-1]:
        count = ref.shape[0]
        out[first : first + count, :] = ref[...]
        first += count


def join(*pieces, long=False):
    if any(x.shape[0] % 16 for x in pieces):
        return jnp.concatenate(pieces)
    rows, width = sum(x.shape[0] for x in pieces), pieces[0].shape[1]
    return pl.pallas_call(
        stack_kernel,
        out_shape=jax.ShapeDtypeStruct((rows, width), BF16),
        in_specs=[VMEM] * len(pieces),
        out_specs=VMEM,
        compiler_params=params(2 + rows * width * 4 // 1000000),
        cost_estimate=cost(LONG if long else 0, rows * width),
        name="stack_rows",
    )(*pieces)


def add(a, b):
    return (a.astype(F32) + b.astype(F32)).astype(BF16)


def halves(x):
    half = x.shape[0] // 2
    return x[:half], x[half:]


def add_halves(kept, got):
    kept, got = halves(kept), halves(got)
    return add(kept[0], got[0]), add(kept[1], got[1])


def split_slots(rows, experts):
    rows = rows.reshape(experts - 1, -1, rows.shape[1])
    cut = rows.shape[1] // 2
    return [x.reshape(-1, rows.shape[2]) for x in (rows[:, :cut], rows[:, cut:])]


def pause_kernel(rows, out):
    out[...] = rows[...]


def pause(rows):
    return pl.pallas_call(
        pause_kernel,
        out_shape=jax.ShapeDtypeStruct(rows.shape, rows.dtype),
        in_specs=[VMEM],
        out_specs=VMEM,
        compiler_params=params(4),
        cost_estimate=cost(LONG, 0),
        name="pause",
    )(rows)


def join_slots(a, b, experts):
    a, b = [x.reshape(experts - 1, -1, x.shape[1]) for x in (a, b)]
    return jnp.concatenate([a, b], axis=1).reshape(-1, a.shape[2])


def product(a, b, dims):
    return lax.dot_general(a, b, (dims, ((), ())), preferred_element_type=F32)


def slot_grad_kernel(grads, w_out, w_in, act, slope, hidden_grad, kept, sent):
    rows, units = act.shape
    width, half = grads.shape[1], rows // 2
    gates = jnp.zeros((rows, 1), F32)
    for j in range(units // TILE):
        at = slice(j * TILE, (j + 1) * TILE)
        grad_act = product(grads[...], w_out[at, :], ((1,), (1,)))
        hidden_grad[:, at] = (grad_act * slope[:, at].astype(F32)).astype(BF16)
        gates += jnp.sum(grad_act * act[:, at].astype(F32), axis=1, keepdims=True)
    gates = jnp.broadcast_to(gates, (rows, LANES)).astype(BF16)
    kept[:, width:] = gates[:half]
    sent[:, width:] = gates[half:]
    for j in range(width // TILE):
        at = slice(j * TILE, (j + 1) * TILE)
        part = product(hidden_grad[...], w_in[at, :], ((1,), (1,))).astype(BF16)
        kept[:, at] = part[:half]
        sent[:, at] = part[half:]


def slot_grads(grads, w_out, w_in, act, slope):
    rows, units = act.shape
    wide = w_in.shape[0] + LANES
    return pl.pallas_call(
        slot_grad_kernel,
        out_shape=(
            jax.ShapeDtypeStruct((rows, units), BF16),
            jax.ShapeDtypeStruct((rows // 2, wide), BF16),
            jax.ShapeDtypeStruct((rows // 2, wide), BF16),
        ),
        in_specs=[VMEM] * 5,
        out_specs=(VMEM, VMEM, VMEM),
        compiler_params=params(16 + rows // 64),
        cost_estimate=cost(0, 0),
        name="slot_grads",
    )(grads, w_out, w_in, act, slope)


def body(tokens, out_grad, gate, expert_id, dropped, slot, saved_hidden, w_in, w_out):
    devices = lax.axis_size("expert")
    experts = devices // SPLIT
    slots = saved_hidden.shape[0] // devices
    units = saved_hidden.shape[1]
    me = lax.axis_index("expert")
    place, gate = pack_routing(expert_id, dropped, slot, gate, slots)
    order = sources_met(me, experts)
    by_source = saved_hidden.reshape(devices, slots, units)
    near_count = SPLIT * slots

    near_grad, far_grad = to_slots(slots, True, place, gate, out_grad)
    near_row, far_row = to_slots(slots, False, place, gate, tokens)

    far_grad = cross(far_grad, 1)
    got = meet(near_grad, 0)
    near_two = join(near_grad, after(got, near_row))
    got = meet(near_two, 1)
    act, slope = activation(by_source, after(order, near_two))
    far_grad = pause(after(far_grad, act))
    far_got = meet(far_grad, 0)
    near_four = join(near_two, after(got, far_grad))
    got = meet(near_four, 2)
    far_row_a, far_row_b = split_slots(after(far_row, far_grad), experts)
    far_row_a = cross(far_row_a, 1)
    far_two = join(far_grad, after(far_got, near_four, far_row_a), long=True)
    far_got = meet(far_two, 1)

    row_got = meet(after(near_row, far_two), 0)
    near_grads = join(near_four, after(got, far_two))
    near_hg, near_kept, near_sent = slot_grads(
        near_grads, w_out, w_in, act[:near_count], slope[:near_count]
    )
    near_got = meet(near_sent, 2)
    near_row2 = join(near_row, after(row_got, near_sent))
    far_four = join(far_two, after(far_got, near_row2), long=True)
    far_got = meet(far_four, 2)
    far_row_b = cross(after(far_row_b, far_four), 1)
    near_kept, near_sent = add_halves(near_kept, after(near_got, far_four))
    near_got = meet(near_sent, 1)
    far_grads = join(far_four, after(far_got, near_sent))

    far_hg, far_kept, far_sent = slot_grads(
        far_grads, w_out, w_in, act[near_count:], slope[near_count:]
    )
    far_row = join_slots(far_row_a, after(far_row_b, far_sent), experts)
    far_kept, far_on = halves(far_kept)
    far_sent = halves(after(far_sent, far_row))
    far_got, on_got = [meet(x, 2) for x in far_sent]
    row_got = meet(near_row2, 1)
    far_row_got = meet(far_row, 0)
    near_kept, near_sent = add_halves(near_kept, after(near_got, far_sent[1]))
    far_sent = add(far_on, after(on_got, near_sent))
    on_got = meet(far_sent, 1)
    far_kept = add(far_kept, after(far_got, far_sent))
    w_out_grad = product(
        after(act, far_kept), join(near_grads, far_grads), ((0,), (0,))
    ).astype(BF16)
    far_row2 = join(far_row, after(far_row_got, w_out_grad))
    far_row_got = meet(far_row2, 1)
    near_row4 = join(near_row2, after(row_got, far_row2))
    row_got = meet(near_row4, 2)
    far_kept, far_sent = add_halves(far_kept, after(on_got, near_row4))
    far_got = meet(far_sent, 0)
    far_row4 = join(far_row2, after(far_row_got, far_sent))
    far_sum = pause(add(far_kept, after(far_got, far_row4)))
    back = cross(far_sum, -1)
    near_got = meet(after(near_sent, far_sum), 0)
    rows = join(near_row4, row_got, far_row4, meet(far_row4, 2))
    w_in_grad = product(rows, join(near_hg, far_hg), ((0,), (0,))).astype(BF16)
    back = after(back, w_in_grad)
    near_got = after(near_got, back)
    token_grad, gate_grad = to_tokens(slots, place, gate, near_kept, near_got, back)
    return (token_grad, gate_grad.reshape(-1), w_in_grad, w_out_grad)


def solution(mesh):
    in_specs = (
        P(("parts", "expert"), None),
        P(("parts", "expert"), None),
        P(("parts", "expert")),
        P(("parts", "expert")),
        P(("parts", "expert")),
        P(("parts", "expert")),
        P("parts", "expert"),
        P(None, "expert"),
        P("expert", None),
    )
    out_specs = (
        P(("parts", "expert"), None),
        P(("parts", "expert")),
        P("parts", "expert"),
        P(("parts", "expert"), None),
    )
    return jax.shard_map(body, mesh=mesh, in_specs=in_specs, out_specs=out_specs, check_vma=False)
```

```python
import functools

import jax
import jax.numpy as jnp
from jax import lax
from jax.experimental import pallas as pl
from jax.experimental.pallas import tpu as pltpu
from jax.sharding import PartitionSpec as P

SPLIT = 8
CORE, LOW, HIGH = 1, 2, 4
LANES, TILE = 128, 256
LONG = 20_000_000_000
VMEM = pl.BlockSpec(memory_space=pltpu.VMEM)
F32, BF16 = jnp.float32, jnp.bfloat16


def params(mib):
    return pltpu.CompilerParams(vmem_limit_bytes=mib * 1024 * 1024)


def cost(flops, moved, exps=0):
    return pl.CostEstimate(flops=flops, bytes_accessed=moved, transcendentals=exps)


def bits(core):
    return (HIGH, LOW, CORE) if core == 0 else (LOW, HIGH, CORE)


def meet(rows, step):
    devices = lax.axis_size("expert")
    return lax.ppermute(rows, "expert", [(i, i ^ bits(i % 2)[step]) for i in range(devices)])


def shift(rows, by):
    devices = lax.axis_size("expert")
    pairs = [(i, (i + by * SPLIT) % devices) for i in range(devices)]
    return lax.ppermute(rows, "expert", pairs)


def cross(rows, sign):
    experts = lax.axis_size("expert") // SPLIT
    if experts == 2:
        return shift(rows, sign)
    slots = rows.shape[0] // (experts - 1)
    return jnp.concatenate(
        [shift(rows[(s - 1) * slots : s * slots], sign * s) for s in range(1, experts)]
    )


def after(value, *earlier):
    return lax.optimization_barrier((value, *earlier))[0]


def sources_met(me, experts):
    block = jnp.arange(SPLIT * (experts - 1), dtype=jnp.int32)

    def place(i):
        first = jnp.where(((me ^ (i >> 2)) & 1) == 1, LOW, HIGH)
        second = (LOW + HIGH) - first
        mask = (i & 1) * first + ((i >> 1) & 1) * second + (i >> 2) * CORE
        return (me & (SPLIT - 1)) ^ mask

    my_expert = me >> 3
    from_expert = my_expert - 1 - block % (experts - 1)
    from_expert = jnp.where(from_expert < 0, from_expert + experts, from_expert)
    near = my_expert * SPLIT + place(block[:SPLIT])
    return jnp.concatenate([near, from_expert * SPLIT + place(block // (experts - 1))])


def pack_routing(expert_id, dropped, slot, gate, slots):
    devices = lax.axis_size("expert")
    ahead = expert_id - (lax.axis_index("expert") >> 3)
    ahead = jnp.where(ahead < 0, ahead + devices // SPLIT, ahead)
    place = jnp.where(dropped == 1, -1, ahead * slots + slot)
    return place.reshape(1, -1), gate.reshape(1, -1)


def chosen(place, first, count):
    rows = lax.broadcasted_iota(jnp.int32, (count, place.shape[1]), 0) + first
    return rows == place


def place_kernel(slots, scale, place, gate, values, near, far):
    rows = values[...]
    if scale:
        count = rows.shape[0]
        across = lax.broadcasted_iota(jnp.int32, (count, count), 1)
        down = lax.broadcasted_iota(jnp.int32, (count, count), 0)
        gates = jnp.where(across == down, gate[...], 0.0)
        column = jnp.sum(gates, axis=1, keepdims=True)
        rows = (column * rows.astype(F32)).astype(BF16)
    for first, out in ((0, near), (slots, far)):
        onehot = chosen(place[...], first, out.shape[0]).astype(F32).astype(BF16)
        out[...] = jnp.dot(onehot, rows, preferred_element_type=F32).astype(BF16)


def to_slots(slots, scale, place, gate, values):
    experts = lax.axis_size("expert") // SPLIT
    width = values.shape[1]
    return pl.pallas_call(
        functools.partial(place_kernel, slots, scale),
        out_shape=(
            jax.ShapeDtypeStruct((slots, width), BF16),
            jax.ShapeDtypeStruct(((experts - 1) * slots, width), BF16),
        ),
        in_specs=[VMEM] * 3,
        out_specs=(VMEM, VMEM),
        compiler_params=params(6),
        cost_estimate=cost(values.size, values.size),
        name="rows_to_slots",
    )(place, gate, values)


def home_kernel(slots, place, gate, kept, got, back, token_grad, gate_grad):
    width = token_grad.shape[1]
    near = kept[...].astype(F32) + got[...].astype(F32)
    total = jnp.zeros(token_grad.shape, F32)
    gates = jnp.zeros(gate_grad.shape, F32)
    for first, rows in ((0, near), (slots, back[...].astype(F32))):
        picks = chosen(place[...], first, rows.shape[0])
        total += lax.dot_general(
            picks.astype(F32).astype(BF16),
            rows[:, :width].astype(BF16),
            (((0,), (0,)), ((), ())),
            preferred_element_type=F32,
        )
        column = rows[:, width : width + 1]
        gates += jnp.sum(jnp.where(picks, column, 0.0), axis=0, keepdims=True)
    token_grad[...] = total.astype(BF16)
    gate_grad[...] = jnp.where(place[...] < 0, 0.0, gates / gate[...])


def to_tokens(slots, place, gate, kept, got, back):
    count, width = place.shape[1], kept.shape[1] - LANES
    return pl.pallas_call(
        functools.partial(home_kernel, slots),
        out_shape=(
            jax.ShapeDtypeStruct((count, width), BF16),
            jax.ShapeDtypeStruct((1, count), F32),
        ),
        in_specs=[VMEM] * 5,
        out_specs=(VMEM, VMEM),
        compiler_params=params(12),
        name="slots_to_tokens",
    )(place, gate, kept, got, back)


def activation_kernel(order, hidden, activated, slope):
    rows = hidden.shape[1]
    step = 16 if rows % 16 == 0 else rows

    def chunk(i, carry):
        at = pl.ds(i * step, step) if rows > step else slice(None)
        h = hidden[0, at, :].astype(F32)
        cdf = 0.5 * (1.0 + lax.erf(h * 0.7071067811865476))
        density = jnp.exp(-0.5 * h * h) * 0.3989422804014327
        activated[0, at, :] = (h * cdf).astype(BF16)
        slope[0, at, :] = (cdf + h * density).astype(BF16)
        return carry

    lax.fori_loop(0, rows // step, chunk, 0)


def activation(by_source, order):
    _, slots, units = by_source.shape
    block = (1, slots, units)
    shape = (order.shape[0], slots, units)
    act, slope = pl.pallas_call(
        activation_kernel,
        grid_spec=pltpu.PrefetchScalarGridSpec(
            num_scalar_prefetch=1,
            grid=(order.shape[0],),
            in_specs=[pl.BlockSpec(block, lambda i, order: (order[i], 0, 0))],
            out_specs=[pl.BlockSpec(block, lambda i, order: (i, 0, 0))] * 2,
        ),
        out_shape=(jax.ShapeDtypeStruct(shape, BF16),) * 2,
        compiler_params=params(6),
        cost_estimate=cost(0, 0),
        name="activation",
    )(order, by_source)
    return act.reshape(-1, units), slope.reshape(-1, units)


def stack_kernel(*refs):
    out, first = refs[-1], 0
    for ref in refs[:-1]:
        count = ref.shape[0]
        out[first : first + count, :] = ref[...]
        first += count


def join(*pieces, long=False):
    if any(x.shape[0] % 16 for x in pieces):
        return jnp.concatenate(pieces)
    rows, width = sum(x.shape[0] for x in pieces), pieces[0].shape[1]
    return pl.pallas_call(
        stack_kernel,
        out_shape=jax.ShapeDtypeStruct((rows, width), BF16),
        in_specs=[VMEM] * len(pieces),
        out_specs=VMEM,
        compiler_params=params(2 + rows * width * 4 // 1000000),
        cost_estimate=cost(LONG if long else 0, rows * width),
        name="stack_rows",
    )(*pieces)


def add(a, b):
    return (a.astype(F32) + b.astype(F32)).astype(BF16)


def halves(x):
    half = x.shape[0] // 2
    return x[:half], x[half:]


def add_halves(kept, got):
    kept, got = halves(kept), halves(got)
    return add(kept[0], got[0]), add(kept[1], got[1])


def split_slots(rows, experts):
    rows = rows.reshape(experts - 1, -1, rows.shape[1])
    cut = rows.shape[1] // 2
    return [x.reshape(-1, rows.shape[2]) for x in (rows[:, :cut], rows[:, cut:])]


def pause_kernel(rows, out):
    out[...] = rows[...]


def pause(rows):
    return pl.pallas_call(
        pause_kernel,
        out_shape=jax.ShapeDtypeStruct(rows.shape, rows.dtype),
        in_specs=[VMEM],
        out_specs=VMEM,
        compiler_params=params(4),
        cost_estimate=cost(LONG, 0),
        name="pause",
    )(rows)


def join_slots(a, b, experts):
    a, b = [x.reshape(experts - 1, -1, x.shape[1]) for x in (a, b)]
    return jnp.concatenate([a, b], axis=1).reshape(-1, a.shape[2])


def product(a, b, dims):
    return lax.dot_general(a, b, (dims, ((), ())), preferred_element_type=F32)


def slot_grad_kernel(grads, w_out, w_in, act, slope, hidden_grad, kept, sent):
    rows, units = act.shape
    width, half = grads.shape[1], rows // 2
    gates = jnp.zeros((rows, 1), F32)
    for j in range(units // TILE):
        at = slice(j * TILE, (j + 1) * TILE)
        grad_act = product(grads[...], w_out[at, :], ((1,), (1,)))
        hidden_grad[:, at] = (grad_act * slope[:, at].astype(F32)).astype(BF16)
        gates += jnp.sum(grad_act * act[:, at].astype(F32), axis=1, keepdims=True)
    gates = jnp.broadcast_to(gates, (rows, LANES)).astype(BF16)
    kept[:, width:] = gates[:half]
    sent[:, width:] = gates[half:]
    for j in range(width // TILE):
        at = slice(j * TILE, (j + 1) * TILE)
        part = product(hidden_grad[...], w_in[at, :], ((1,), (1,))).astype(BF16)
        kept[:, at] = part[:half]
        sent[:, at] = part[half:]


def slot_grads(grads, w_out, w_in, act, slope):
    rows, units = act.shape
    wide = w_in.shape[0] + LANES
    return pl.pallas_call(
        slot_grad_kernel,
        out_shape=(
            jax.ShapeDtypeStruct((rows, units), BF16),
            jax.ShapeDtypeStruct((rows // 2, wide), BF16),
            jax.ShapeDtypeStruct((rows // 2, wide), BF16),
        ),
        in_specs=[VMEM] * 5,
        out_specs=(VMEM, VMEM, VMEM),
        compiler_params=params(16 + rows // 64),
        cost_estimate=cost(0, 0),
        name="slot_grads",
    )(grads, w_out, w_in, act, slope)


def body(tokens, out_grad, gate, expert_id, dropped, slot, saved_hidden, w_in, w_out):
    devices = lax.axis_size("expert")
    experts = devices // SPLIT
    slots = saved_hidden.shape[0] // devices
    units = saved_hidden.shape[1]
    me = lax.axis_index("expert")
    place, gate = pack_routing(expert_id, dropped, slot, gate, slots)
    order = sources_met(me, experts)
    by_source = saved_hidden.reshape(devices, slots, units)
    near_count = SPLIT * slots

    near_grad, far_grad = to_slots(slots, True, place, gate, out_grad)
    near_row, far_row = to_slots(slots, False, place, gate, tokens)

    far_grad = cross(far_grad, 1)
    got = meet(near_grad, 0)
    near_two = join(near_grad, after(got, near_row))
    got = meet(near_two, 1)
    act, slope = activation(by_source, after(order, near_two))
    far_grad = pause(after(far_grad, act))
    far_got = meet(far_grad, 0)
    near_four = join(near_two, after(got, far_grad))
    got = meet(near_four, 2)
    far_row_a, far_row_b = split_slots(after(far_row, far_grad), experts)
    far_row_a = cross(far_row_a, 1)
    far_two = join(far_grad, after(far_got, near_four, far_row_a), long=True)
    far_got = meet(far_two, 1)

    far_row_b = cross(after(far_row_b, far_two), 1)
    row_got = meet(after(near_row, far_two), 0)
    near_grads = join(near_four, after(got, far_two))
    near_hg, near_kept, near_sent = slot_grads(
        near_grads, w_out, w_in, act[:near_count], slope[:near_count]
    )
    near_got = meet(near_sent, 2)
    near_row2 = join(near_row, after(row_got, near_sent))
    far_row_b = after(far_row_b, near_row2)
    far_four = join(far_two, after(far_got, far_row_b), long=True)
    far_got = meet(far_four, 2)
    near_kept, near_sent = add_halves(near_kept, after(near_got, far_four))
    near_got = meet(near_sent, 1)
    far_grads = join(far_four, after(far_got, near_sent))

    far_hg, far_kept, far_sent = slot_grads(
        far_grads, w_out, w_in, act[near_count:], slope[near_count:]
    )
    far_row = join_slots(far_row_a, after(far_row_b, far_sent), experts)
    far_kept, far_on = halves(far_kept)
    far_sent = halves(after(far_sent, far_row))
    far_got, on_got = [meet(x, 2) for x in far_sent]
    row_got = meet(near_row2, 1)
    far_row_got = meet(far_row, 0)
    near_kept, near_sent = add_halves(near_kept, after(near_got, far_sent[1]))
    far_sent = add(far_on, after(on_got, near_sent))
    on_got = meet(far_sent, 1)
    far_kept = add(far_kept, after(far_got, far_sent))
    w_out_grad = product(
        after(act, far_kept), join(near_grads, far_grads), ((0,), (0,))
    ).astype(BF16)
    far_row2 = join(far_row, after(far_row_got, w_out_grad))
    far_row_got = meet(far_row2, 1)
    near_row4 = join(near_row2, after(row_got, far_row2))
    row_got = meet(near_row4, 2)
    far_kept, far_sent = add_halves(far_kept, after(on_got, near_row4))
    far_got = meet(far_sent, 0)
    far_row4 = join(far_row2, after(far_row_got, far_sent))
    far_sum = pause(add(far_kept, after(far_got, far_row4)))
    back = cross(far_sum, -1)
    near_got = meet(after(near_sent, far_sum), 0)
    rows = join(near_row4, row_got, far_row4, meet(far_row4, 2))
    w_in_grad = product(rows, join(near_hg, far_hg), ((0,), (0,))).astype(BF16)
    back = after(back, w_in_grad)
    near_got = after(near_got, back)
    token_grad, gate_grad = to_tokens(slots, place, gate, near_kept, near_got, back)
    return (token_grad, gate_grad.reshape(-1), w_in_grad, w_out_grad)


def solution(mesh):
    in_specs = (
        P(("parts", "expert"), None),
        P(("parts", "expert"), None),
        P(("parts", "expert")),
        P(("parts", "expert")),
        P(("parts", "expert")),
        P(("parts", "expert")),
        P("parts", "expert"),
        P(None, "expert"),
        P("expert", None),
    )
    out_specs = (
        P(("parts", "expert"), None),
        P(("parts", "expert")),
        P("parts", "expert"),
        P(("parts", "expert"), None),
    )
    return jax.shard_map(body, mesh=mesh, in_specs=in_specs, out_specs=out_specs, check_vma=False)
```

```python
import functools

import jax
import jax.numpy as jnp
from jax import lax
from jax.experimental import pallas as pl
from jax.experimental.pallas import tpu as pltpu
from jax.sharding import PartitionSpec as P

SPLIT = 8
CORE, LOW, HIGH = 1, 2, 4
LANES, TILE = 128, 256
LONG = 20_000_000_000
VMEM = pl.BlockSpec(memory_space=pltpu.VMEM)
F32, BF16 = jnp.float32, jnp.bfloat16


def params(mib):
    return pltpu.CompilerParams(vmem_limit_bytes=mib * 1024 * 1024)


def cost(flops, moved, exps=0):
    return pl.CostEstimate(flops=flops, bytes_accessed=moved, transcendentals=exps)


def bits(core):
    return (HIGH, LOW, CORE) if core == 0 else (LOW, HIGH, CORE)


def meet(rows, step):
    devices = lax.axis_size("expert")
    return lax.ppermute(rows, "expert", [(i, i ^ bits(i % 2)[step]) for i in range(devices)])


def shift(rows, by):
    devices = lax.axis_size("expert")
    pairs = [(i, (i + by * SPLIT) % devices) for i in range(devices)]
    return lax.ppermute(rows, "expert", pairs)


def cross(rows, sign):
    experts = lax.axis_size("expert") // SPLIT
    if experts == 2:
        return shift(rows, sign)
    slots = rows.shape[0] // (experts - 1)
    return jnp.concatenate(
        [shift(rows[(s - 1) * slots : s * slots], sign * s) for s in range(1, experts)]
    )


def after(value, *earlier):
    return lax.optimization_barrier((value, *earlier))[0]


def sources_met(me, experts):
    block = jnp.arange(SPLIT * (experts - 1), dtype=jnp.int32)

    def place(i):
        first = jnp.where(((me ^ (i >> 2)) & 1) == 1, LOW, HIGH)
        second = (LOW + HIGH) - first
        mask = (i & 1) * first + ((i >> 1) & 1) * second + (i >> 2) * CORE
        return (me & (SPLIT - 1)) ^ mask

    my_expert = me >> 3
    from_expert = my_expert - 1 - block % (experts - 1)
    from_expert = jnp.where(from_expert < 0, from_expert + experts, from_expert)
    near = my_expert * SPLIT + place(block[:SPLIT])
    return jnp.concatenate([near, from_expert * SPLIT + place(block // (experts - 1))])


def pack_routing(expert_id, dropped, slot, gate, slots):
    devices = lax.axis_size("expert")
    ahead = expert_id - (lax.axis_index("expert") >> 3)
    ahead = jnp.where(ahead < 0, ahead + devices // SPLIT, ahead)
    place = jnp.where(dropped == 1, -1, ahead * slots + slot)
    return place.reshape(1, -1), gate.reshape(1, -1)


def chosen(place, first, count):
    rows = lax.broadcasted_iota(jnp.int32, (count, place.shape[1]), 0) + first
    return rows == place


def place_kernel(slots, scale, place, gate, values, near, far):
    rows = values[...]
    if scale:
        count = rows.shape[0]
        across = lax.broadcasted_iota(jnp.int32, (count, count), 1)
        down = lax.broadcasted_iota(jnp.int32, (count, count), 0)
        gates = jnp.where(across == down, gate[...], 0.0)
        column = jnp.sum(gates, axis=1, keepdims=True)
        rows = (column * rows.astype(F32)).astype(BF16)
    for first, out in ((0, near), (slots, far)):
        onehot = chosen(place[...], first, out.shape[0]).astype(F32).astype(BF16)
        out[...] = jnp.dot(onehot, rows, preferred_element_type=F32).astype(BF16)


def to_slots(slots, scale, place, gate, values):
    experts = lax.axis_size("expert") // SPLIT
    width = values.shape[1]
    return pl.pallas_call(
        functools.partial(place_kernel, slots, scale),
        out_shape=(
            jax.ShapeDtypeStruct((slots, width), BF16),
            jax.ShapeDtypeStruct(((experts - 1) * slots, width), BF16),
        ),
        in_specs=[VMEM] * 3,
        out_specs=(VMEM, VMEM),
        compiler_params=params(6),
        cost_estimate=cost(values.size, values.size),
        name="rows_to_slots",
    )(place, gate, values)


def home_kernel(slots, place, gate, kept, got, back, token_grad, gate_grad):
    width = token_grad.shape[1]
    near = kept[...].astype(F32) + got[...].astype(F32)
    total = jnp.zeros(token_grad.shape, F32)
    gates = jnp.zeros(gate_grad.shape, F32)
    for first, rows in ((0, near), (slots, back[...].astype(F32))):
        picks = chosen(place[...], first, rows.shape[0])
        total += lax.dot_general(
            picks.astype(F32).astype(BF16),
            rows[:, :width].astype(BF16),
            (((0,), (0,)), ((), ())),
            preferred_element_type=F32,
        )
        column = rows[:, width : width + 1]
        gates += jnp.sum(jnp.where(picks, column, 0.0), axis=0, keepdims=True)
    token_grad[...] = total.astype(BF16)
    gate_grad[...] = jnp.where(place[...] < 0, 0.0, gates / gate[...])


def to_tokens(slots, place, gate, kept, got, back):
    count, width = place.shape[1], kept.shape[1] - LANES
    return pl.pallas_call(
        functools.partial(home_kernel, slots),
        out_shape=(
            jax.ShapeDtypeStruct((count, width), BF16),
            jax.ShapeDtypeStruct((1, count), F32),
        ),
        in_specs=[VMEM] * 5,
        out_specs=(VMEM, VMEM),
        compiler_params=params(12),
        name="slots_to_tokens",
    )(place, gate, kept, got, back)


def activation_kernel(order, hidden, activated, slope):
    rows = hidden.shape[1]
    step = 16 if rows % 16 == 0 else rows

    def chunk(i, carry):
        at = pl.ds(i * step, step) if rows > step else slice(None)
        h = hidden[0, at, :].astype(F32)
        cdf = 0.5 * (1.0 + lax.erf(h * 0.7071067811865476))
        density = jnp.exp(-0.5 * h * h) * 0.3989422804014327
        activated[0, at, :] = (h * cdf).astype(BF16)
        slope[0, at, :] = (cdf + h * density).astype(BF16)
        return carry

    lax.fori_loop(0, rows // step, chunk, 0)


def activation(by_source, order):
    _, slots, units = by_source.shape
    block = (1, slots, units)
    shape = (order.shape[0], slots, units)
    act, slope = pl.pallas_call(
        activation_kernel,
        grid_spec=pltpu.PrefetchScalarGridSpec(
            num_scalar_prefetch=1,
            grid=(order.shape[0],),
            in_specs=[pl.BlockSpec(block, lambda i, order: (order[i], 0, 0))],
            out_specs=[pl.BlockSpec(block, lambda i, order: (i, 0, 0))] * 2,
        ),
        out_shape=(jax.ShapeDtypeStruct(shape, BF16),) * 2,
        compiler_params=params(6),
        cost_estimate=cost(0, 0),
        name="activation",
    )(order, by_source)
    return act.reshape(-1, units), slope.reshape(-1, units)


def stack_kernel(*refs):
    out, first = refs[-1], 0
    for ref in refs[:-1]:
        count = ref.shape[0]
        out[first : first + count, :] = ref[...]
        first += count


def join(*pieces, long=False):
    if any(x.shape[0] % 16 for x in pieces):
        return jnp.concatenate(pieces)
    rows, width = sum(x.shape[0] for x in pieces), pieces[0].shape[1]
    return pl.pallas_call(
        stack_kernel,
        out_shape=jax.ShapeDtypeStruct((rows, width), BF16),
        in_specs=[VMEM] * len(pieces),
        out_specs=VMEM,
        compiler_params=params(2 + rows * width * 4 // 1000000),
        cost_estimate=cost(LONG if long else 0, rows * width),
        name="stack_rows",
    )(*pieces)


def add(a, b):
    return (a.astype(F32) + b.astype(F32)).astype(BF16)


def halves(x):
    half = x.shape[0] // 2
    return x[:half], x[half:]


def add_halves(kept, got):
    kept, got = halves(kept), halves(got)
    return add(kept[0], got[0]), add(kept[1], got[1])


def split_slots(rows, experts):
    rows = rows.reshape(experts - 1, -1, rows.shape[1])
    cut = rows.shape[1] // 2
    return [x.reshape(-1, rows.shape[2]) for x in (rows[:, :cut], rows[:, cut:])]


def pause_kernel(rows, out):
    out[...] = rows[...]


def pause(rows):
    return pl.pallas_call(
        pause_kernel,
        out_shape=jax.ShapeDtypeStruct(rows.shape, rows.dtype),
        in_specs=[VMEM],
        out_specs=VMEM,
        compiler_params=params(4),
        cost_estimate=cost(LONG, 0),
        name="pause",
    )(rows)


def join_slots(a, b, experts):
    a, b = [x.reshape(experts - 1, -1, x.shape[1]) for x in (a, b)]
    return jnp.concatenate([a, b], axis=1).reshape(-1, a.shape[2])


def product(a, b, dims):
    return lax.dot_general(a, b, (dims, ((), ())), preferred_element_type=F32)


def slot_grad_kernel(grads, w_out, w_in, act, slope, hidden_grad, kept, sent):
    rows, units = act.shape
    width, half = grads.shape[1], rows // 2
    gates = jnp.zeros((rows, 1), F32)
    for j in range(units // TILE):
        at = slice(j * TILE, (j + 1) * TILE)
        grad_act = product(grads[...], w_out[at, :], ((1,), (1,)))
        hidden_grad[:, at] = (grad_act * slope[:, at].astype(F32)).astype(BF16)
        gates += jnp.sum(grad_act * act[:, at].astype(F32), axis=1, keepdims=True)
    gates = jnp.broadcast_to(gates, (rows, LANES)).astype(BF16)
    kept[:, width:] = gates[:half]
    sent[:, width:] = gates[half:]
    for j in range(width // TILE):
        at = slice(j * TILE, (j + 1) * TILE)
        part = product(hidden_grad[...], w_in[at, :], ((1,), (1,))).astype(BF16)
        kept[:, at] = part[:half]
        sent[:, at] = part[half:]


def slot_grads(grads, w_out, w_in, act, slope):
    rows, units = act.shape
    wide = w_in.shape[0] + LANES
    return pl.pallas_call(
        slot_grad_kernel,
        out_shape=(
            jax.ShapeDtypeStruct((rows, units), BF16),
            jax.ShapeDtypeStruct((rows // 2, wide), BF16),
            jax.ShapeDtypeStruct((rows // 2, wide), BF16),
        ),
        in_specs=[VMEM] * 5,
        out_specs=(VMEM, VMEM, VMEM),
        compiler_params=params(16 + rows // 64),
        cost_estimate=cost(0, 0),
        name="slot_grads",
    )(grads, w_out, w_in, act, slope)


def body(tokens, out_grad, gate, expert_id, dropped, slot, saved_hidden, w_in, w_out):
    devices = lax.axis_size("expert")
    experts = devices // SPLIT
    slots = saved_hidden.shape[0] // devices
    units = saved_hidden.shape[1]
    me = lax.axis_index("expert")
    place, gate = pack_routing(expert_id, dropped, slot, gate, slots)
    order = sources_met(me, experts)
    by_source = saved_hidden.reshape(devices, slots, units)
    near_count = SPLIT * slots

    near_grad, far_grad = to_slots(slots, True, place, gate, out_grad)
    near_row, far_row = to_slots(slots, False, place, gate, tokens)

    far_grad = cross(far_grad, 1)
    got = meet(near_grad, 0)
    near_two = join(near_grad, after(got, near_row))
    got = meet(near_two, 1)
    act, slope = activation(by_source, after(order, near_two))
    far_grad = pause(after(far_grad, act))
    far_got = meet(far_grad, 0)
    near_four = join(near_two, after(got, far_grad))
    got = meet(near_four, 2)
    far_row_a, far_row_b = split_slots(after(far_row, far_grad), experts)
    far_row_a = cross(far_row_a, 1)
    far_two = join(far_grad, after(far_got, near_four, far_row_a), long=True)
    far_got = meet(far_two, 1)

    far_row_b = cross(after(far_row_b, far_two), 1)
    row_got = meet(after(near_row, far_two), 0)
    near_grads = join(near_four, after(got, far_two))
    near_hg, near_kept, near_sent = slot_grads(
        near_grads, w_out, w_in, act[:near_count], slope[:near_count]
    )
    near_got = meet(near_sent, 2)
    near_row2 = join(near_row, after(row_got, near_sent))
    far_row_b = after(far_row_b, near_row2)
    far_four = join(far_two, after(far_got, far_row_b), long=True)
    far_got = meet(far_four, 2)
    near_kept, near_sent = add_halves(near_kept, after(near_got, far_four))
    near_got = meet(near_sent, 1)
    far_row = join_slots(far_row_a, far_row_b, experts)
    far_row_got = meet(after(far_row, far_four), 0)
    far_grads = join(far_four, after(far_got, near_sent))

    far_hg, far_kept, far_sent = slot_grads(
        far_grads, w_out, w_in, act[near_count:], slope[near_count:]
    )
    far_kept, far_on = halves(far_kept)
    far_sent = halves(far_sent)
    far_got, on_got = [meet(x, 2) for x in far_sent]
    row_got = meet(near_row2, 1)
    near_kept, near_sent = add_halves(near_kept, after(near_got, far_sent[1]))
    far_row2 = join(far_row, after(far_row_got, near_sent), long=True)
    far_sent = add(far_on, after(on_got, far_row2))
    on_got = meet(far_sent, 1)
    far_kept = add(far_kept, after(far_got, far_sent))
    w_out_grad = product(
        after(act, far_kept), join(near_grads, far_grads), ((0,), (0,))
    ).astype(BF16)
    far_row_got = meet(after(far_row2, w_out_grad), 1)
    near_row4 = join(near_row2, after(row_got, w_out_grad))
    row_got = meet(near_row4, 2)
    far_kept, far_sent = add_halves(far_kept, after(on_got, near_row4))
    far_got = meet(far_sent, 0)
    far_row4 = join(far_row2, after(far_row_got, far_sent))
    far_sum = pause(add(far_kept, after(far_got, far_row4)))
    back = cross(far_sum, -1)
    near_got = meet(after(near_sent, far_sum), 0)
    rows = join(near_row4, row_got, far_row4, meet(far_row4, 2))
    w_in_grad = product(rows, join(near_hg, far_hg), ((0,), (0,))).astype(BF16)
    back = after(back, w_in_grad)
    near_got = after(near_got, back)
    token_grad, gate_grad = to_tokens(slots, place, gate, near_kept, near_got, back)
    return (token_grad, gate_grad.reshape(-1), w_in_grad, w_out_grad)


def solution(mesh):
    in_specs = (
        P(("parts", "expert"), None),
        P(("parts", "expert"), None),
        P(("parts", "expert")),
        P(("parts", "expert")),
        P(("parts", "expert")),
        P(("parts", "expert")),
        P("parts", "expert"),
        P(None, "expert"),
        P("expert", None),
    )
    out_specs = (
        P(("parts", "expert"), None),
        P(("parts", "expert")),
        P("parts", "expert"),
        P(("parts", "expert"), None),
    )
    return jax.shard_map(body, mesh=mesh, in_specs=in_specs, out_specs=out_specs, check_vma=False)
```
